256 devices in a mesh: member: 8 (over z), band: 32 (over x, y, core).
Axes of the slice: x: 4, y: 4, z: 8, core: 2. Of those that a mesh axis runs over, the one named last changes fastest.
Arguments:
- perturbations: bfloat16 [80, 4, 2, 768, 1536], P('member', None, None, 'band'), may hold values from -0.625 to 0.625
- innovations: float32 [4, 2, 768, 1536], P(None, None, 'band'), may hold values from -6 to 6
- error_weight: float32 [4, 2, 768, 1536], P(None, None, 'band'), may hold values from 1 to 30, as said below
- localization: float32 [256, 128], P('band'), may hold values from 0.5 to 4
Outputs:
- control: float32 [80, 2, 256, 128], P('member', None, 'band')
- residual: float32 [80, 2, 256, 128], P('member', None, 'band')
- increment: float32 [4, 2, 768, 1536], P(None, None, 'band', 'member')
The draws below stay inside these ranges and needn't reach their ends.
Inputs may be any that keep to these rules, and one draw needn't show every extreme that they name: `error_weight`: positive weights.
All inputs are finite; a program needn't handle non-finite values.
Results may differ from the reference program's by a relative error of at most 0.0003.
Values sent between devices are 32-bit elements; how exact they have to be, the bound alone decides.
No kernel may reach another device: no remote copies, remote signals or barrier semaphores. Data moves between devices by JAX's collectives and lax.ppermute only.
A program may use at most 128 MiB of HBM per device.

```python
import math
import jax
import jax.numpy as jnp
from jax import lax

NLON = 1536
ZW = 256
MW = 128
VARS = 4
LEV = 2
ITERS = 2
MEMBERS = 80
NLAT = 768


def draw_error_weight(key, part):
    key = jax.random.fold_in(key, 11)
    uniform_part = jax.random.uniform(key, (VARS, LEV, NLAT, NLON), jnp.float32)
    latitude = jnp.arange(NLAT, dtype=jnp.float32) / NLAT
    rising = 1.0 + 2.0 * latitude[None, None, :, None]
    base = jnp.exp(2.302585 * uniform_part)
    return base * rising


def block_levels(key, dims, split, low, largest):
    loudness, own = 1.0, jax.random.fold_in(key, 6)
    for position, shards_of in split:
        draws = jnp.exp(jax.random.uniform(jax.random.fold_in(own, position), (shards_of,), jnp.float32, low / len(split), largest / len(split)))
        loudness = loudness * jnp.repeat(draws, dims[position] // shards_of).reshape([-1 if axis == position else 1 for axis in range(len(dims))])
    return loudness


def noise(own_key, dims, spread, most, cuts=(), held_as=jnp.bfloat16):
    entries = jax.random.normal(own_key, dims, jnp.float32) * spread
    if len(cuts) > 0:
        entries = block_levels(own_key, dims, cuts, -0.22, 0.18) * entries
    return jnp.clip(entries, min=-most, max=most).astype(held_as)


def setup_inputs(seed: int = 0) -> dict:
    streams_of = jax.random.split(jax.random.key(seed), 5)
    perturbations = noise(streams_of[0], (MEMBERS, VARS, LEV, NLAT, NLON), MEMBERS ** -0.5, 0.625, ((0, 8), (3, 32)))
    innovations = noise(streams_of[1], (VARS, LEV, NLAT, NLON), 1.0, 6.0, ((2, 32),), jnp.float32)
    error_weight = draw_error_weight(jax.random.fold_in(streams_of[4], 71), 0)
    localization = jnp.clip(jnp.exp(math.log(4.0) - 2.0794415 * jax.random.uniform(streams_of[3], (ZW, MW), jnp.float32) ** block_levels(streams_of[3], (ZW, MW), ((0, 32),), -0.2, 0.2)), 0.5, 4.0)
    return {"perturbations": perturbations, "innovations": innovations, "error_weight": error_weight, "localization": localization}


def zonal_basis(waves, columns):
    wave_index = jnp.arange(waves, dtype=jnp.int32)
    wave_number = (wave_index + 1) // 2
    column_index = jnp.arange(columns, dtype=jnp.int32)
    product = wave_number[:, None] * column_index[None, :] % columns
    angle = 2.0 * math.pi / columns * product.astype(jnp.float32)
    picked = jnp.where((wave_index % 2 == 0)[:, None], jnp.cos(angle), jnp.sin(angle))
    factor = jnp.where(wave_index == 0, math.sqrt(0.5), 1.0).astype(jnp.float32) * math.sqrt(2.0 / columns)
    return picked * factor[:, None]

def meridional_basis(rows_total, modes):
    row_index = jnp.arange(rows_total, dtype=jnp.int32)
    mode_index = jnp.arange(modes, dtype=jnp.int32)
    product = mode_index[None, :] * (2 * row_index[:, None] + 1) % (4 * rows_total)
    angle = math.pi / (2.0 * rows_total) * product.astype(jnp.float32)
    factor = jnp.where(mode_index == 0, math.sqrt(0.5), 1.0).astype(jnp.float32) * math.sqrt(2.0 / rows_total)
    return jnp.cos(angle) * factor[None, :]

def reference(perturbations, innovations, error_weight, localization):
    highest = lax.Precision.HIGHEST
    zonal = zonal_basis(ZW, NLON)
    merid = meridional_basis(NLAT, MW)

    def synthesize(coeffs):
        rows_out = jnp.einsum('lzm,ym->lzy', coeffs * localization, merid, precision=highest)
        return jnp.einsum('lzy,zx->lyx', rows_out, zonal, precision=highest)

    def analyse_member(member):
        projected = lax.optimization_barrier(jnp.sum(member * weighted_now[0], axis=0))
        coeffs = jnp.einsum('lyx,zx->lzy', projected, zonal, precision=highest)
        return jnp.einsum('lzy,ym->lzm', coeffs, merid, precision=highest) * localization
    weighted_now = [None]

    def adjoint(weighted):
        weighted_now[0] = weighted
        return lax.map(analyse_member, perturbations)

    def ensemble(control_field):

        def accumulate(total, pair):
            member, coeffs = pair
            return (total + member * synthesize(coeffs)[None], None)
        start = jnp.zeros((VARS, LEV, NLAT, NLON), jnp.float32)
        total, unused = lax.scan(accumulate, start, (perturbations, control_field))
        return total

    def hessian(direction):
        grid_field = ensemble(direction)
        return (direction + adjoint(error_weight * grid_field), grid_field)
    gradient = adjoint(error_weight * innovations)
    control = jnp.zeros_like(gradient)
    increment = jnp.zeros((VARS, LEV, NLAT, NLON), jnp.float32)
    residual = gradient
    direction = gradient
    norm_now = jnp.sum(residual * residual)
    for iteration in range(ITERS):
        image, grid_field = hessian(direction)
        step = norm_now / jnp.sum(direction * image)
        control = control + step * direction
        increment = increment + step * grid_field
        residual = residual - step * image
        norm_next = jnp.sum(residual * residual)
        direction = residual + norm_next / norm_now * direction
        norm_now = norm_next
    return (control, residual, increment)
```

```python
import functools
import math

import jax
import jax.numpy as jnp
import ml_dtypes
import numpy as np
from jax import lax
from jax.experimental import pallas as pl
from jax.experimental.pallas import tpu as pltpu
from jax.sharding import PartitionSpec as P

NLON = 1536
NLAT = 768
ZW = 256
MW = 128
VARS = 4
LEV = 2
KLOC = 10
BANDS = 32
RING = 8
ROWS = 24
TILES = 3
LTILES = NLON // 128
SHARE = NLON // RING
CHUNK = TILES * LTILES * 8
SLOTS = TILES * KLOC
VMEM_LIMIT = 40 * 1024 * 1024


def halves(array):
    high = array.astype(np.float32).astype(ml_dtypes.bfloat16)
    low = (array - high.astype(np.float64)).astype(np.float32).astype(ml_dtypes.bfloat16)
    return high, low


@functools.lru_cache(None)
def bases():
    wave = np.arange(ZW)
    number = (wave + 1) // 2
    angle = 2.0 * math.pi / NLON * ((number[:, None] * np.arange(NLON)[None, :]) % NLON)
    zonal = np.where((wave % 2 == 0)[:, None], np.cos(angle), np.sin(angle))
    zonal = zonal * (np.where(wave == 0, math.sqrt(0.5), 1.0) * math.sqrt(2.0 / NLON))[:, None]
    mode, row = np.arange(MW), np.arange(NLAT)
    angle = math.pi / (2.0 * NLAT) * ((mode[None, :] * (2 * row[:, None] + 1)) % (4 * NLAT))
    merid = np.cos(angle) * (np.where(mode == 0, math.sqrt(0.5), 1.0) * math.sqrt(2.0 / NLAT))
    parts = merid.reshape(BANDS, TILES, 8, MW).transpose(1, 0, 2, 3).reshape(TILES, BANDS * 8, MW)
    first = np.concatenate([parts[0], parts[1]], axis=1)
    second = np.concatenate([parts[1], parts[2]], axis=1)
    return {
        "zonal": np.stack(halves(zonal)),
        "zonal_t": np.stack(halves(zonal.T.copy())),
        "merid": np.stack([np.stack(halves(first)), np.stack(halves(second))]),
        "merid_t": np.stack([np.stack(halves(first.T.copy())), np.stack(halves(second.T.copy()))]),
    }


def split(value):
    high = value.astype(jnp.bfloat16)
    low = (value - high.astype(jnp.float32)).astype(jnp.bfloat16)
    return high, low


def dot(left, right):
    return jnp.dot(left, right, preferred_element_type=jnp.float32)


def swap_groups(vectors):
    group = lax.broadcasted_iota(jnp.int32, (8, 128), 1) // 8
    vectors = list(vectors)
    for bit in (1, 2, 4, 8):
        low = (group & bit) == 0
        for i in range(16):
            if i & bit:
                continue
            a, b = vectors[i], vectors[i | bit]
            vectors[i] = jnp.where(low, a, pltpu.roll(b, 8 * bit, 1))
            vectors[i | bit] = jnp.where(low, pltpu.roll(a, 128 - 8 * bit, 1), b)
    return vectors


def total_of(value):
    return jnp.sum(jnp.sum(value, axis=1, keepdims=True), axis=0, keepdims=True)


def project_and_send(weights, pert, zonal_t, proj, coef, spare, send):
    for level in range(LEV):
        for lt in range(LTILES):
            lanes = pl.ds(lt * 128, 128)
            fields = [
                jnp.concatenate([weights(v * LEV + level, rt, lt) for rt in range(TILES)], axis=0)
                for v in range(VARS)
            ]

            def member(k, carry, level=level, lanes=lanes, fields=fields):
                acc = pert[k, 0, level, :, lanes].astype(jnp.float32) * fields[0]
                for v in range(1, VARS):
                    acc = acc + pert[k, v, level, :, lanes].astype(jnp.float32) * fields[v]
                for rt in range(TILES):
                    at = pl.multiple_of(level * 240 + (rt * KLOC + k) * 8, 8)
                    proj[pl.ds(at, 8), lanes] = acc[rt * 8 : rt * 8 + 8]
                return carry

            lax.fori_loop(0, KLOC, member, 0, unroll=2)
    high, low = split(proj[...])
    result = dot(high, zonal_t[0]) + dot(low, zonal_t[0]) + dot(high, zonal_t[1])
    for level in range(LEV):
        coef[pl.ds(level * 256, 240), :] = result[level * 240 : level * 240 + 240]
        coef[pl.ds(level * 256 + 240, 16), :] = jnp.zeros((16, ZW), jnp.float32)
    if spare is not None:
        coef[pl.ds(240, 8), :] = jnp.broadcast_to(spare, (8, ZW))
    for level in range(LEV):
        for tile in range(2):
            for half in range(2):
                got = swap_groups(
                    coef[pl.ds(level * 256 + (tile * 16 + i) * 8, 8), pl.ds(half * 128, 128)]
                    for i in range(16)
                )
                for g in range(16):
                    send[half * 16 + g, pl.ds(level * 16 + tile * 8, 8), :] = got[g]


def first_kernel(pert, innovations, weight, zonal_t, send, proj, coef):
    def weights(c, rt, lt):
        at = (c // LEV, c % LEV, pl.ds(rt * 8, 8), pl.ds(lt * 128, 128))
        return weight[at] * innovations[at]

    project_and_send(weights, pert, zonal_t, proj, coef, None, send)


def assemble(me, parts, field):
    for j in range(RING):
        field[lax.rem(me - j + RING, RING)] = parts[j][pl.ds(0, CHUNK), :]


def own_columns(me, field, out):
    start = (3 * me) // 2
    odd = lax.rem(me, 2) == 1
    for c in range(RING):
        for rt in range(TILES):
            at = pl.multiple_of((rt * LTILES + start) * 8, 8)
            window = jnp.concatenate(
                [field[c, pl.ds(at, 8), :], field[c, pl.ds(at + 8, 8), :]], axis=1
            )
            window = jnp.where(odd, pltpu.roll(window, 192, 1), window)
            out[c // LEV, c % LEV, pl.ds(rt * 8, 8), :] = window[:, :SHARE]


def energy(weight, field):
    acc = jnp.zeros((8, 128), jnp.float32)
    for c in range(RING):
        for rt in range(TILES):
            for lt in range(LTILES):
                value = field[c, pl.ds((rt * LTILES + lt) * 8, 8), :]
                acc = acc + weight[
                    c // LEV, c % LEV, pl.ds(rt * 8, 8), pl.ds(lt * 128, 128)
                ] * (value * value)
    return total_of(acc)


def second_kernel(me_ref, pert, weight, zonal_t, *refs):
    parts, (send, field, own, scal, proj, coef) = refs[:RING], refs[RING:]
    me = me_ref[0]
    assemble(me, parts, field)
    own_columns(me, field, own)
    scal[...] = parts[0][pl.ds(CHUNK, 8), :]
    curve = energy(weight, field)

    def weights(c, rt, lt):
        at = (c // LEV, c % LEV, pl.ds(rt * 8, 8), pl.ds(lt * 128, 128))
        return weight[at] * field[c, pl.ds((rt * LTILES + lt) * 8, 8), :]

    project_and_send(weights, pert, zonal_t, proj, coef, curve, send)


def third_kernel(me_ref, pert, weight, zonal_t, old_scal, old_field, *refs):
    parts, (send, own, scal, proj, coef, field) = refs[:RING], refs[RING:]
    me = me_ref[0]
    norm = old_scal[0:1, 0:1]
    norm_next = parts[0][CHUNK : CHUNK + 1, 0:1]
    cross = parts[0][CHUNK + 1 : CHUNK + 2, 0:1]
    beta = norm_next / norm
    for j in range(RING):
        c = lax.rem(me - j + RING, RING)
        field[c] = parts[j][pl.ds(0, CHUNK), :] + beta * old_field[c]
    own_columns(me, field, own)
    square = norm_next + 2.0 * beta * cross + beta * beta * norm
    row = lax.broadcasted_iota(jnp.int32, (8, 128), 0)
    scal[...] = jnp.where(row == 0, norm_next, jnp.where(row == 1, square, beta))
    curve = energy(weight, field)

    def weights(c, rt, lt):
        at = (c // LEV, c % LEV, pl.ds(rt * 8, 8), pl.ds(lt * 128, 128))
        return weight[at] * field[c, pl.ds((rt * LTILES + lt) * 8, 8), :]

    project_and_send(weights, pert, zonal_t, proj, coef, curve, send)


def to_modes(received, level, merid_t):
    lane = lax.broadcasted_iota(jnp.int32, (MW, 128), 1)
    sums = []
    for tile in range(2):
        data = received[:, pl.ds(level * 16 + tile * 8, 8), :].reshape(BANDS * 8, 128)
        high, low = split(data)
        sums.append(
            dot(merid_t[tile, 0], high) + dot(merid_t[tile, 0], low) + dot(merid_t[tile, 1], high)
        )
    result = sums[0][:MW] + jnp.where(lane < 48, pltpu.roll(sums[0][MW:], 48, 1), 0.0)
    result = result + jnp.where(lane >= 48, pltpu.roll(sums[1][:MW], 48, 1), 0.0)
    result = result + pltpu.roll(sums[1][MW:], 96, 1)
    return jnp.where(lane < 80, result, 0.0)


def to_rows(value, merid, level, send, spares):
    lane = lax.broadcasted_iota(jnp.int32, (MW, 128), 1)
    moved = pltpu.roll(value, 80, 1)
    second = jnp.where(lane >= 80, moved, 0.0)
    third = jnp.where(lane < 32, moved, 0.0)
    fourth = pltpu.roll(value, 32, 1)
    for tile, pair in enumerate(((value, second), (third, fourth))):
        high, low = split(jnp.concatenate(pair, axis=0))
        rows = dot(merid[tile, 0], high) + dot(merid[tile, 0], low) + dot(merid[tile, 1], high)
        if tile == 1 and spares:
            row = lax.broadcasted_iota(jnp.int32, (BANDS * 8, 128), 0)
            column = lax.broadcasted_iota(jnp.int32, (BANDS * 8, 128), 1)
            top = (row % 8) == 0
            for position, spare in enumerate(spares):
                rows = rows + jnp.where(top & (column == 112 + 8 * position), spare, 0.0)
        send[:, pl.ds(level * 16 + tile * 8, 8), :] = rows.reshape(BANDS, 8, 128)


def spare_sum(received):
    data = received[:, pl.ds(8, 8), :].reshape(BANDS * 8, 128)
    row = lax.broadcasted_iota(jnp.int32, (BANDS * 8, 128), 0)
    column = lax.broadcasted_iota(jnp.int32, (BANDS * 8, 128), 1)
    return total_of(jnp.where(((row % 8) == 0) & (column == 112), data, 0.0))


def scale_of(localization):
    return jnp.concatenate([localization[...]] * 16, axis=0).T


def gradient_kernel(received, localization, merid_t, merid, send, gradient):
    scale = scale_of(localization)
    acc = jnp.zeros((MW, 128), jnp.float32)
    for level in range(LEV):
        value = to_modes(received, level, merid_t) * scale
        gradient[level] = value
        acc = acc + value * value
    norm = total_of(acc)
    for level in range(LEV):
        to_rows(gradient[level] * scale, merid, level, send, (norm,) if level == 0 else ())


def residual_kernel(received, localization, merid_t, merid, gradient, scal, send, residual, step_out):
    scale = scale_of(localization)
    norm = scal[0:1, 0:1]
    step = norm / (norm + spare_sum(received))
    step_out[...] = jnp.broadcast_to(step, (8, 128))
    squares = jnp.zeros((MW, 128), jnp.float32)
    cross = jnp.zeros((MW, 128), jnp.float32)
    for level in range(LEV):
        old = gradient[level]
        image = old + to_modes(received, level, merid_t) * scale
        value = old - step * image
        residual[level] = value
        squares = squares + value * value
        cross = cross + value * old
    spares = (total_of(squares), total_of(cross))
    for level in range(LEV):
        to_rows(residual[level] * scale, merid, level, send, spares if level == 0 else ())


def last_kernel(
    received, localization, merid_t, gradient, residual, scal, step_in, first_own, second_own,
    control_out, residual_out, increment_out,
):
    scale = scale_of(localization)
    norm_next, square, beta = scal[0:1, 0:1], scal[1:2, 0:1], scal[2:3, 0:1]
    first_step = step_in[0:1, 0:1]
    step = norm_next / (square + spare_sum(received))
    for level in range(LEV):
        old, res = gradient[level], residual[level]
        direction = res + beta * old
        image = direction + to_modes(received, level, merid_t) * scale
        for out, value in (
            (control_out, first_step * old + step * direction),
            (residual_out, res - step * image),
        ):
            turned = value.T
            for k in range(KLOC):
                out[k, level] = turned[k * 8 : k * 8 + 8]
    increment_out[...] = first_step[None, None] * first_own[...] + step[None, None] * second_own[...]


def synth_kernel(me_ref, received, pert, zonal, *refs):
    outs, (coef, amp, total) = refs[:RING], refs[RING:]
    me = me_ref[0]
    for level in range(LEV):
        for tile in range(2):
            for half in range(2):
                got = swap_groups(
                    received[half * 16 + g, pl.ds(level * 16 + tile * 8, 8), :] for g in range(16)
                )
                for i in range(16):
                    at = level * 256 + (tile * 16 + i) * 8
                    coef[pl.ds(at, 8), pl.ds(half * 128, 128)] = got[i]
    scalars = [total_of(coef[pl.ds(240 + 8 * i, 8), :]) for i in range(2)]
    high, low = split(jnp.concatenate([coef[pl.ds(0, 240), :], coef[pl.ds(256, 240), :]], axis=0))
    for part in range(LTILES // 2):
        wide = pl.ds(part * 256, 256)
        amp[...] = (
            dot(high, zonal[0, :, wide]) + dot(low, zonal[0, :, wide]) + dot(high, zonal[1, :, wide])
        )
        for level in range(LEV):
            for side in range(2):
                lt = part * 2 + side
                lanes = pl.ds(lt * 128, 128)

                def member(k, sums, level=level, side=side, lanes=lanes):
                    pieces = []
                    for rt in range(TILES):
                        at = pl.multiple_of(level * 240 + (rt * KLOC + k) * 8, 8)
                        pieces.append(amp[pl.ds(at, 8), pl.ds(side * 128, 128)])
                    field = jnp.concatenate(pieces, axis=0)
                    return tuple(
                        sums[v] + pert[k, v, level, :, lanes].astype(jnp.float32) * field
                        for v in range(VARS)
                    )

                zero = jnp.zeros((ROWS, 128), jnp.float32)
                sums = lax.fori_loop(0, KLOC, member, (zero,) * VARS, unroll=2)
                for v in range(VARS):
                    for rt in range(TILES):
                        total[v * LEV + level, pl.ds((rt * LTILES + lt) * 8, 8), :] = sums[v][
                            rt * 8 : rt * 8 + 8
                        ]
    row = lax.broadcasted_iota(jnp.int32, (8, 128), 0)
    extra = jnp.where(row == 0, scalars[0], jnp.where(row == 1, scalars[1], 0.0))
    for j in range(RING):
        outs[j][pl.ds(0, CHUNK), :] = total[lax.rem(me + j, RING)]
        outs[j][pl.ds(CHUNK, 8), :] = extra


def f32(*shape):
    return jax.ShapeDtypeStruct(shape, jnp.float32)


def call(kernel, outs, scratch, *args, scalars=0, flops=0):
    in_specs = [pl.BlockSpec(memory_space=pltpu.SMEM)] * scalars
    in_specs += [pl.BlockSpec(memory_space=pltpu.VMEM)] * (len(args) - scalars)
    moved = sum(math.prod(a.shape) * a.dtype.itemsize for a in args)
    return pl.pallas_call(
        kernel,
        out_shape=outs,
        in_specs=in_specs,
        out_specs=jax.tree.map(lambda _: pl.BlockSpec(memory_space=pltpu.VMEM), outs),
        scratch_shapes=scratch,
        compiler_params=pltpu.CompilerParams(vmem_limit_bytes=VMEM_LIMIT),
        cost_estimate=pl.CostEstimate(flops=flops, bytes_accessed=moved, transcendentals=0),
    )(*args)


def ring_permute(value, distance):
    return lax.ppermute(value, "member", [(i, (i + distance) % RING) for i in range(RING)])


def sum_members(outs):
    parts = [outs[0]] + [ring_permute(outs[j], j) for j in range(1, RING)]
    own = functools.reduce(lambda a, b: a + b, parts)
    return [own] + [ring_permute(own, j) for j in range(1, RING)]


def local(perturbations, innovations, error_weight, localization):
    const = {name: jnp.asarray(value) for name, value in bases().items()}
    me = lax.axis_index("member").astype(jnp.int32)[None]
    payload = f32(BANDS, 32, 128)
    vmem = lambda *shape: pltpu.VMEM(shape, jnp.float32)
    project_scratch = [vmem(480, NLON), vmem(512, ZW)]
    synth_scratch = [vmem(512, ZW), vmem(480, 256), vmem(RING, CHUNK, 128)]
    own = f32(VARS, LEV, ROWS, SHARE)
    modes = f32(LEV, MW, 128)
    field = f32(RING, CHUNK, 128)

    def exchange(value):
        return lax.all_to_all(value, "band", 0, 0)

    def synthesize(rows):
        outs = call(
            synth_kernel, [f32(CHUNK + 8, 128)] * RING, synth_scratch,
            me, rows, perturbations, const["zonal"], scalars=1, flops=1200000000,
        )
        return sum_members(outs)

    sent = call(
        first_kernel, payload, project_scratch,
        perturbations, innovations, error_weight, const["zonal_t"], flops=1200000000,
    )
    sent, gradient = call(
        gradient_kernel, [payload, modes], [],
        exchange(sent), localization, const["merid_t"], const["merid"], flops=200000000,
    )
    parts = synthesize(exchange(sent))
    sent, first_field, first_own, scal = call(
        second_kernel, [payload, field, own, f32(8, 128)], project_scratch,
        me, perturbations, error_weight, const["zonal_t"], *parts, scalars=1, flops=1200000000,
    )
    sent, residual, step = call(
        residual_kernel, [payload, modes, f32(8, 128)], [],
        exchange(sent), localization, const["merid_t"], const["merid"], gradient, scal,
        flops=200000000,
    )
    parts = synthesize(exchange(sent))
    sent, second_own, scal = call(
        third_kernel, [payload, own, f32(8, 128)], project_scratch + [vmem(RING, CHUNK, 128)],
        me, perturbations, error_weight, const["zonal_t"], scal, first_field, *parts,
        scalars=1, flops=1200000000,
    )
    return tuple(call(
        last_kernel,
        [f32(KLOC, LEV, ZW // BANDS, MW), f32(KLOC, LEV, ZW // BANDS, MW), own], [],
        exchange(sent), localization, const["merid_t"], gradient, residual, scal, step,
        first_own, second_own, flops=100000000,
    ))


def solution(mesh):
    return jax.shard_map(
        local,
        mesh=mesh,
        in_specs=(
            P("member", None, None, "band", None),
            P(None, None, "band", None),
            P(None, None, "band", None),
            P("band", None),
        ),
        out_specs=(
            P("member", None, "band", None),
            P("member", None, "band", None),
            P(None, None, "band", "member"),
        ),
        check_vma=False,
    )
```

```python
import functools
import math

import jax
import jax.numpy as jnp
import ml_dtypes
import numpy as np
from jax import lax
from jax.experimental import pallas as pl
from jax.experimental.pallas import tpu as pltpu
from jax.sharding import PartitionSpec as P

NLON = 1536
NLAT = 768
ZW = 256
MW = 128
VARS = 4
LEV = 2
KLOC = 10
BANDS = 32
RING = 8
ROWS = 24
TILES = 3
LTILES = NLON // 128
SHARE = NLON // RING
CHUNK = TILES * LTILES * 8
SLOTS = TILES * KLOC


def halves(array):
    high = array.astype(np.float32).astype(ml_dtypes.bfloat16)
    low = (array - high.astype(np.float64)).astype(np.float32).astype(ml_dtypes.bfloat16)
    return high, low


@functools.lru_cache(None)
def bases():
    wave = np.arange(ZW)
    number = (wave + 1) // 2
    angle = 2.0 * math.pi / NLON * ((number[:, None] * np.arange(NLON)[None, :]) % NLON)
    zonal = np.where((wave % 2 == 0)[:, None], np.cos(angle), np.sin(angle))
    zonal = zonal * (np.where(wave == 0, math.sqrt(0.5), 1.0) * math.sqrt(2.0 / NLON))[:, None]
    mode, row = np.arange(MW), np.arange(NLAT)
    angle = math.pi / (2.0 * NLAT) * ((mode[None, :] * (2 * row[:, None] + 1)) % (4 * NLAT))
    merid = np.cos(angle) * (np.where(mode == 0, math.sqrt(0.5), 1.0) * math.sqrt(2.0 / NLAT))
    parts = merid.reshape(BANDS, TILES, 8, MW).transpose(1, 0, 2, 3).reshape(TILES, BANDS * 8, MW)
    first = np.concatenate([parts[0], parts[1]], axis=1)
    second = np.concatenate([parts[1], parts[2]], axis=1)
    return {
        "zonal": np.stack(halves(zonal)),
        "zonal_t": np.stack(halves(zonal.T.copy())),
        "merid": np.stack([np.stack(halves(first)), np.stack(halves(second))]),
        "merid_t": np.stack([np.stack(halves(first.T.copy())), np.stack(halves(second.T.copy()))]),
    }


def split(value):
    high = value.astype(jnp.bfloat16)
    low = (value - high.astype(jnp.float32)).astype(jnp.bfloat16)
    return high, low


def dot(left, right):
    return jnp.dot(left, right, preferred_element_type=jnp.float32)


def swap_groups(vectors):
    group = lax.broadcasted_iota(jnp.int32, (8, 128), 1) // 8
    vectors = list(vectors)
    for bit in (1, 2, 4, 8):
        low = (group & bit) == 0
        for i in range(16):
            if i & bit:
                continue
            a, b = vectors[i], vectors[i | bit]
            vectors[i] = jnp.where(low, a, pltpu.roll(b, 8 * bit, 1))
            vectors[i | bit] = jnp.where(low, pltpu.roll(a, 128 - 8 * bit, 1), b)
    return vectors


def total_of(value):
    return jnp.sum(jnp.sum(value, axis=1, keepdims=True), axis=0, keepdims=True)


def project_and_send(weights, pert, zonal_t, proj, coef, spare, send, ready=lambda stage: None):
    for level in range(LEV):
        ready(level)
        for lt in range(LTILES):
            lanes = pl.ds(lt * 128, 128)
            fields = [
                jnp.concatenate([weights(v * LEV + level, rt, lt) for rt in range(TILES)], axis=0)
                for v in range(VARS)
            ]

            def member(k, carry, level=level, lanes=lanes, fields=fields):
                acc = pert[k, 0, level, :, lanes].astype(jnp.float32) * fields[0]
                for v in range(1, VARS):
                    acc = acc + pert[k, v, level, :, lanes].astype(jnp.float32) * fields[v]
                for rt in range(TILES):
                    at = pl.multiple_of(level * 240 + (rt * KLOC + k) * 8, 8)
                    proj[pl.ds(at, 8), lanes] = acc[rt * 8 : rt * 8 + 8]
                return carry

            lax.fori_loop(0, KLOC, member, 0, unroll=2)
    ready(2)
    high, low = split(proj[...])
    result = dot(high, zonal_t[0]) + dot(low, zonal_t[0]) + dot(high, zonal_t[1])
    for level in range(LEV):
        coef[pl.ds(level * 256, 240), :] = result[level * 240 : level * 240 + 240]
        coef[pl.ds(level * 256 + 240, 16), :] = jnp.zeros((16, ZW), jnp.float32)
    if spare is not None:
        coef[pl.ds(240, 8), :] = jnp.broadcast_to(spare, (8, ZW))
    for level in range(LEV):
        for tile in range(2):
            for half in range(2):
                got = swap_groups(
                    coef[pl.ds(level * 256 + (tile * 16 + i) * 8, 8), pl.ds(half * 128, 128)]
                    for i in range(16)
                )
                for g in range(16):
                    send[half * 16 + g, pl.ds(level * 16 + tile * 8, 8), :] = got[g]


def first_kernel(
    pert_in, innovations_in, weight_in, zonal_in, send,
    proj, coef, pert, innovations, weight, zonal_t, sems,
):
    copies = [
        pltpu.make_async_copy(innovations_in, innovations, sems.at[0]),
        pltpu.make_async_copy(weight_in, weight, sems.at[1]),
        pltpu.make_async_copy(pert_in.at[:, :, 0], pert.at[:, :, 0], sems.at[2]),
        pltpu.make_async_copy(pert_in.at[:, :, 1], pert.at[:, :, 1], sems.at[3]),
        pltpu.make_async_copy(zonal_in, zonal_t, sems.at[4]),
    ]
    for copy in copies:
        copy.start()

    def weights(c, rt, lt):
        at = (c // LEV, c % LEV, pl.ds(rt * 8, 8), pl.ds(lt * 128, 128))
        return weight[at] * innovations[at]

    def ready(stage):
        for copy in (copies[:3], copies[3:4], copies[4:])[stage]:
            copy.wait()

    project_and_send(weights, pert, zonal_t, proj, coef, None, send, ready)


def chunk_pieces(me, parts):
    half = CHUNK // 2
    for j, part in zip((0, 1, 7, 2, 6, 3, 5), parts):
        yield lax.rem(me + (RING - j), RING), pl.ds(0, CHUNK), part[pl.ds(0, CHUNK), :]
    for side in range(2):
        yield lax.rem(me + RING // 2, RING), pl.ds(side * half, half), parts[7 + side][...]


def assemble(me, parts, field):
    for c, rows, value in chunk_pieces(me, parts):
        field[c, rows, :] = value


def own_columns(me, field, out):
    start = (3 * me) // 2
    odd = lax.rem(me, 2) == 1
    for c in range(RING):
        for rt in range(TILES):
            at = pl.multiple_of((rt * LTILES + start) * 8, 8)
            window = jnp.concatenate(
                [field[c, pl.ds(at, 8), :], field[c, pl.ds(at + 8, 8), :]], axis=1
            )
            window = jnp.where(odd, pltpu.roll(window, 192, 1), window)
            out[c // LEV, c % LEV, pl.ds(rt * 8, 8), :] = window[:, :SHARE]


def energy(weight, field):
    acc = jnp.zeros((8, 128), jnp.float32)
    for c in range(RING):
        for rt in range(TILES):
            for lt in range(LTILES):
                value = field[c, pl.ds((rt * LTILES + lt) * 8, 8), :]
                acc = acc + weight[
                    c // LEV, c % LEV, pl.ds(rt * 8, 8), pl.ds(lt * 128, 128)
                ] * (value * value)
    return total_of(acc)


def second_kernel(me_ref, pert, weight, zonal_t, *refs):
    parts, (send, field, own, scal, proj, coef) = refs[: RING + 1], refs[RING + 1 :]
    me = me_ref[0]
    assemble(me, parts, field)
    own_columns(me, field, own)
    scal[...] = parts[0][pl.ds(CHUNK, 8), :]
    curve = energy(weight, field)

    def weights(c, rt, lt):
        at = (c // LEV, c % LEV, pl.ds(rt * 8, 8), pl.ds(lt * 128, 128))
        return weight[at] * field[c, pl.ds((rt * LTILES + lt) * 8, 8), :]

    project_and_send(weights, pert, zonal_t, proj, coef, curve, send)


def third_kernel(me_ref, pert, weight, zonal_t, old_scal, old_field, *refs):
    parts, (send, own, scal, proj, coef, field) = refs[: RING + 1], refs[RING + 1 :]
    me = me_ref[0]
    norm = old_scal[0:1, 0:1]
    norm_next = parts[0][CHUNK : CHUNK + 1, 0:1]
    cross = parts[0][CHUNK + 1 : CHUNK + 2, 0:1]
    beta = norm_next / norm
    for c, rows, value in chunk_pieces(me, parts):
        field[c, rows, :] = value + beta * old_field[c, rows, :]
    own_columns(me, field, own)
    square = norm_next + 2.0 * beta * cross + beta * beta * norm
    row = lax.broadcasted_iota(jnp.int32, (8, 128), 0)
    scal[...] = jnp.where(row == 0, norm_next, jnp.where(row == 1, square, beta))
    curve = energy(weight, field)

    def weights(c, rt, lt):
        at = (c // LEV, c % LEV, pl.ds(rt * 8, 8), pl.ds(lt * 128, 128))
        return weight[at] * field[c, pl.ds((rt * LTILES + lt) * 8, 8), :]

    project_and_send(weights, pert, zonal_t, proj, coef, curve, send)


def to_modes(received, level, merid_t):
    lane = lax.broadcasted_iota(jnp.int32, (MW, 128), 1)
    sums = []
    for tile in range(2):
        data = received[:, pl.ds(level * 16 + tile * 8, 8), :].reshape(BANDS * 8, 128)
        high, low = split(data)
        sums.append(
            dot(merid_t[tile, 0], high) + dot(merid_t[tile, 0], low) + dot(merid_t[tile, 1], high)
        )
    result = sums[0][:MW] + jnp.where(lane < 48, pltpu.roll(sums[0][MW:], 48, 1), 0.0)
    result = result + jnp.where(lane >= 48, pltpu.roll(sums[1][:MW], 48, 1), 0.0)
    result = result + pltpu.roll(sums[1][MW:], 96, 1)
    return jnp.where(lane < 80, result, 0.0)


def to_rows(value, merid, level, send, spares):
    lane = lax.broadcasted_iota(jnp.int32, (MW, 128), 1)
    moved = pltpu.roll(value, 80, 1)
    second = jnp.where(lane >= 80, moved, 0.0)
    third = jnp.where(lane < 32, moved, 0.0)
    fourth = pltpu.roll(value, 32, 1)
    for tile, pair in enumerate(((value, second), (third, fourth))):
        high, low = split(jnp.concatenate(pair, axis=0))
        rows = dot(merid[tile, 0], high) + dot(merid[tile, 0], low) + dot(merid[tile, 1], high)
        if tile == 1 and spares:
            row = lax.broadcasted_iota(jnp.int32, (BANDS * 8, 128), 0)
            column = lax.broadcasted_iota(jnp.int32, (BANDS * 8, 128), 1)
            top = (row % 8) == 0
            for position, spare in enumerate(spares):
                rows = rows + jnp.where(top & (column == 112 + 8 * position), spare, 0.0)
        send[:, pl.ds(level * 16 + tile * 8, 8), :] = rows.reshape(BANDS, 8, 128)


def spare_sum(received):
    data = received[:, pl.ds(8, 8), :].reshape(BANDS * 8, 128)
    row = lax.broadcasted_iota(jnp.int32, (BANDS * 8, 128), 0)
    column = lax.broadcasted_iota(jnp.int32, (BANDS * 8, 128), 1)
    return total_of(jnp.where(((row % 8) == 0) & (column == 112), data, 0.0))


def scale_of(localization):
    return jnp.concatenate([localization[...]] * 16, axis=0).T


def gradient_kernel(received, localization, merid_t, merid, send, gradient):
    scale = scale_of(localization)
    acc = jnp.zeros((MW, 128), jnp.float32)
    for level in range(LEV):
        value = to_modes(received, level, merid_t) * scale
        gradient[level] = value
        acc = acc + value * value
    norm = total_of(acc)
    for level in range(LEV):
        to_rows(gradient[level] * scale, merid, level, send, (norm,) if level == 0 else ())


def residual_kernel(received, localization, merid_t, merid, gradient, scal, send, residual, step_out):
    scale = scale_of(localization)
    norm = scal[0:1, 0:1]
    step = norm / (norm + spare_sum(received))
    step_out[...] = jnp.broadcast_to(step, (8, 128))
    squares = jnp.zeros((MW, 128), jnp.float32)
    cross = jnp.zeros((MW, 128), jnp.float32)
    for level in range(LEV):
        old = gradient[level]
        image = old + to_modes(received, level, merid_t) * scale
        value = old - step * image
        residual[level] = value
        squares = squares + value * value
        cross = cross + value * old
    spares = (total_of(squares), total_of(cross))
    for level in range(LEV):
        to_rows(residual[level] * scale, merid, level, send, spares if level == 0 else ())


def last_kernel(
    received, localization, merid_t, gradient, residual, scal, step_in, first_own, second_own,
    control_out, residual_out, increment_out,
):
    scale = scale_of(localization)
    norm_next, square, beta = scal[0:1, 0:1], scal[1:2, 0:1], scal[2:3, 0:1]
    first_step = step_in[0:1, 0:1]
    step = norm_next / (square + spare_sum(received))
    for level in range(LEV):
        old, res = gradient[level], residual[level]
        direction = res + beta * old
        image = direction + to_modes(received, level, merid_t) * scale
        for out, value in (
            (control_out, first_step * old + step * direction),
            (residual_out, res - step * image),
        ):
            turned = value.T
            for k in range(KLOC):
                out[k, level] = turned[k * 8 : k * 8 + 8]
    increment_out[...] = first_step[None, None] * first_own[...] + step[None, None] * second_own[...]


def synth_kernel(me_ref, received, pert, zonal, *refs):
    outs, (coef, amp, total) = refs[:RING], refs[RING:]
    me = me_ref[0]
    for level in range(LEV):
        for tile in range(2):
            for half in range(2):
                got = swap_groups(
                    received[half * 16 + g, pl.ds(level * 16 + tile * 8, 8), :] for g in range(16)
                )
                for i in range(16):
                    at = level * 256 + (tile * 16 + i) * 8
                    coef[pl.ds(at, 8), pl.ds(half * 128, 128)] = got[i]
    scalars = [total_of(coef[pl.ds(240 + 8 * i, 8), :]) for i in range(2)]
    high, low = split(jnp.concatenate([coef[pl.ds(0, 240), :], coef[pl.ds(256, 240), :]], axis=0))
    for part in range(LTILES // 2):
        wide = pl.ds(part * 256, 256)
        amp[...] = (
            dot(high, zonal[0, :, wide]) + dot(low, zonal[0, :, wide]) + dot(high, zonal[1, :, wide])
        )
        for level in range(LEV):
            for side in range(2):
                lt = part * 2 + side
                lanes = pl.ds(lt * 128, 128)

                def member(k, sums, level=level, side=side, lanes=lanes):
                    pieces = []
                    for rt in range(TILES):
                        at = pl.multiple_of(level * 240 + (rt * KLOC + k) * 8, 8)
                        pieces.append(amp[pl.ds(at, 8), pl.ds(side * 128, 128)])
                    field = jnp.concatenate(pieces, axis=0)
                    return tuple(
                        sums[v] + pert[k, v, level, :, lanes].astype(jnp.float32) * field
                        for v in range(VARS)
                    )

                zero = jnp.zeros((ROWS, 128), jnp.float32)
                sums = lax.fori_loop(0, KLOC, member, (zero,) * VARS, unroll=2)
                for v in range(VARS):
                    for rt in range(TILES):
                        total[v * LEV + level, pl.ds((rt * LTILES + lt) * 8, 8), :] = sums[v][
                            rt * 8 : rt * 8 + 8
                        ]
    row = lax.broadcasted_iota(jnp.int32, (8, 128), 0)
    extra = jnp.where(row == 0, scalars[0], jnp.where(row == 1, scalars[1], 0.0))
    for j in range(RING):
        outs[j][pl.ds(0, CHUNK), :] = total[lax.rem(me + j, RING)]
        outs[j][pl.ds(CHUNK, 8), :] = extra


def f32(*shape):
    return jax.ShapeDtypeStruct(shape, jnp.float32)


def call(kernel, outs, scratch, *args, scalars=0, flops=0, space=pltpu.VMEM, limit=16):
    in_specs = [pl.BlockSpec(memory_space=pltpu.SMEM)] * scalars
    in_specs += [pl.BlockSpec(memory_space=space)] * (len(args) - scalars)
    moved = sum(math.prod(a.shape) * a.dtype.itemsize for a in args)
    return pl.pallas_call(
        kernel,
        out_shape=outs,
        in_specs=in_specs,
        out_specs=jax.tree.map(lambda _: pl.BlockSpec(memory_space=pltpu.VMEM), outs),
        scratch_shapes=scratch,
        compiler_params=pltpu.CompilerParams(vmem_limit_bytes=limit * 1024 * 1024),
        cost_estimate=pl.CostEstimate(flops=flops, bytes_accessed=moved, transcendentals=0),
    )(*args)


def ring_permute(value, distance):
    return lax.ppermute(value, "member", [(i, (i + distance) % RING) for i in range(RING)])


def sum_members(outs):
    half = CHUNK // 2
    rest = CHUNK + 8 - half
    right = outs[3] + jnp.pad(ring_permute(outs[4][:half], 1), ((0, rest), (0, 0)))
    left = outs[5] + jnp.pad(ring_permute(outs[4][half:], -1), ((half, 0), (0, 0)))
    for s in (2, 1, 0):
        right, left = ring_permute(right, 1), ring_permute(left, -1)
        if s:
            right, left = outs[s] + right, outs[RING - s] + left
    own = outs[0] + right + left
    parts = [own]
    right = left = own[:CHUNK]
    for s in range(3):
        right, left = ring_permute(right, 1), ring_permute(left, -1)
        parts += [right, left]
    return parts + [ring_permute(right[:half], 1), ring_permute(left[half:], -1)]


def local(perturbations, innovations, error_weight, localization):
    const = {name: jnp.asarray(value) for name, value in bases().items()}
    me = lax.axis_index("member").astype(jnp.int32)[None]
    payload = f32(BANDS, 32, 128)
    vmem = lambda *shape: pltpu.VMEM(shape, jnp.float32)
    project_scratch = [vmem(480, NLON), vmem(512, ZW)]
    synth_scratch = [vmem(512, ZW), vmem(480, 256), vmem(RING, CHUNK, 128)]
    own = f32(VARS, LEV, ROWS, SHARE)
    modes = f32(LEV, MW, 128)
    field = f32(RING, CHUNK, 128)

    def exchange(value):
        return lax.all_to_all(value, "band", 0, 0)

    def synthesize(rows):
        outs = call(
            synth_kernel, [f32(CHUNK + 8, 128)] * RING, synth_scratch,
            me, rows, perturbations, const["zonal"], scalars=1, flops=1200000000,
        )
        return sum_members(outs)

    sent = call(
        first_kernel, payload,
        project_scratch + [
            pltpu.VMEM(perturbations.shape, jnp.bfloat16), vmem(*innovations.shape),
            vmem(*error_weight.shape), pltpu.VMEM(const["zonal_t"].shape, jnp.bfloat16),
            pltpu.SemaphoreType.DMA((5,)),
        ],
        perturbations, innovations, error_weight, const["zonal_t"],
        flops=1200000000, space=pl.ANY, limit=32,
    )
    sent, gradient = call(
        gradient_kernel, [payload, modes], [],
        exchange(sent), localization, const["merid_t"], const["merid"], flops=200000000,
    )
    parts = synthesize(exchange(sent))
    sent, first_field, first_own, scal = call(
        second_kernel, [payload, field, own, f32(8, 128)], project_scratch,
        me, perturbations, error_weight, const["zonal_t"], *parts, scalars=1, flops=1200000000,
    )
    sent, residual, step = call(
        residual_kernel, [payload, modes, f32(8, 128)], [],
        exchange(sent), localization, const["merid_t"], const["merid"], gradient, scal,
        flops=200000000,
    )
    parts = synthesize(exchange(sent))
    sent, second_own, scal = call(
        third_kernel, [payload, own, f32(8, 128)], project_scratch + [vmem(RING, CHUNK, 128)],
        me, perturbations, error_weight, const["zonal_t"], scal, first_field, *parts,
        scalars=1, flops=1200000000,
    )
    return tuple(call(
        last_kernel,
        [f32(KLOC, LEV, ZW // BANDS, MW), f32(KLOC, LEV, ZW // BANDS, MW), own], [],
        exchange(sent), localization, const["merid_t"], gradient, residual, scal, step,
        first_own, second_own, flops=100000000,
    ))


def solution(mesh):
    return jax.shard_map(
        local,
        mesh=mesh,
        in_specs=(
            P("member", None, None, "band", None),
            P(None, None, "band", None),
            P(None, None, "band", None),
            P("band", None),
        ),
        out_specs=(
            P("member", None, "band", None),
            P("member", None, "band", None),
            P(None, None, "band", "member"),
        ),
        check_vma=False,
    )
```

```python
import functools
import math

import jax
import jax.numpy as jnp
import ml_dtypes
import numpy as np
from jax import lax
from jax.experimental import pallas as pl
from jax.experimental.pallas import tpu as pltpu
from jax.sharding import PartitionSpec as P

NLON = 1536
NLAT = 768
ZW = 256
MW = 128
VARS = 4
LEV = 2
KLOC = 10
BANDS = 32
RING = 8
ROWS = 24
TILES = 3
LTILES = NLON // 128
SHARE = NLON // RING
CHUNK = TILES * LTILES * 8
SLOTS = TILES * KLOC


def halves(array):
    high = array.astype(np.float32).astype(ml_dtypes.bfloat16)
    low = (array - high.astype(np.float64)).astype(np.float32).astype(ml_dtypes.bfloat16)
    return high, low


@functools.lru_cache(None)
def bases():
    wave = np.arange(ZW)
    number = (wave + 1) // 2
    angle = 2.0 * math.pi / NLON * ((number[:, None] * np.arange(NLON)[None, :]) % NLON)
    zonal = np.where((wave % 2 == 0)[:, None], np.cos(angle), np.sin(angle))
    zonal = zonal * (np.where(wave == 0, math.sqrt(0.5), 1.0) * math.sqrt(2.0 / NLON))[:, None]
    mode, row = np.arange(MW), np.arange(NLAT)
    angle = math.pi / (2.0 * NLAT) * ((mode[None, :] * (2 * row[:, None] + 1)) % (4 * NLAT))
    merid = np.cos(angle) * (np.where(mode == 0, math.sqrt(0.5), 1.0) * math.sqrt(2.0 / NLAT))
    parts = merid.reshape(BANDS, TILES, 8, MW).transpose(1, 0, 2, 3).reshape(TILES, BANDS * 8, MW)
    first = np.concatenate([parts[0], parts[1]], axis=1)
    second = np.concatenate([parts[1], parts[2]], axis=1)
    return {
        "zonal": np.stack(halves(zonal)),
        "zonal_t": np.stack(halves(zonal.T.copy())),
        "merid": np.stack([np.stack(halves(first)), np.stack(halves(second))]),
        "merid_t": np.stack([np.stack(halves(first.T.copy())), np.stack(halves(second.T.copy()))]),
    }


def split(value):
    high = value.astype(jnp.bfloat16)
    low = (value - high.astype(jnp.float32)).astype(jnp.bfloat16)
    return high, low


def dot(left, right):
    return jnp.dot(left, right, preferred_element_type=jnp.float32)


def swap_groups(vectors):
    group = lax.broadcasted_iota(jnp.int32, (8, 128), 1) // 8
    vectors = [pltpu.roll(v, 8 * i, 1) if i else v for i, v in enumerate(vectors)]
    for bit in (1, 2, 4, 8):
        move = (group & bit) != 0
        vectors = [jnp.where(move, vectors[(j + bit) % 16], vectors[j]) for j in range(16)]
    return [pltpu.roll(vectors[16 - g], 128 - 8 * g, 1) if g else vectors[0] for g in range(16)]


def total_of(value):
    return jnp.sum(jnp.sum(value, axis=1, keepdims=True), axis=0, keepdims=True)


def project_and_send(weights, pert, zonal_t, proj, coef, send, spare=None, ready=None):
    def zonal(first, rows):
        high, low = split(proj[pl.ds(first, rows), :])
        return dot(high, zonal_t[0]) + dot(low, zonal_t[0]) + dot(high, zonal_t[1])

    def keep(level, result):
        coef[pl.ds(level * 256, 240), :] = result
        coef[pl.ds(level * 256 + 240, 16), :] = jnp.zeros((16, ZW), jnp.float32)

    for level in range(LEV):
        if ready:
            ready(2 * level)
        for lt in range(LTILES):
            lanes = pl.ds(lt * 128, 128)
            fields = [
                jnp.concatenate([weights(v, level, rt, lt) for rt in range(TILES)], axis=0)
                for v in range(VARS)
            ]
            for k in range(KLOC):
                acc = pert[k, 0, level, :, lanes].astype(jnp.float32) * fields[0]
                for v in range(1, VARS):
                    acc = acc + pert[k, v, level, :, lanes].astype(jnp.float32) * fields[v]
                for rt in range(TILES):
                    proj[pl.ds(level * 240 + (rt * KLOC + k) * 8, 8), lanes] = acc[
                        rt * 8 : rt * 8 + 8
                    ]
        if ready:
            if level == 0:
                ready(1)
            keep(level, zonal(level * 240, 240))
    if not ready:
        result = zonal(0, 480)
        for level in range(LEV):
            keep(level, result[level * 240 : level * 240 + 240])
    if spare:
        coef[pl.ds(240, 8), :] = jnp.broadcast_to(spare(), (8, ZW))
    for level in range(LEV):
        for tile in range(2):
            for half in range(2):
                got = swap_groups(
                    coef[pl.ds(level * 256 + (tile * 16 + i) * 8, 8), pl.ds(half * 128, 128)]
                    for i in range(16)
                )
                for g in range(16):
                    send[half * 16 + g, pl.ds(level * 16 + tile * 8, 8), :] = got[g]


def first_kernel(
    pert_in, innovations_in, weight_in, zonal_in, send,
    proj, coef, pert, innovations, weight, zonal_t, sems,
):
    copies = [
        pltpu.make_async_copy(innovations_in, innovations, sems.at[0]),
        pltpu.make_async_copy(weight_in, weight, sems.at[1]),
        pltpu.make_async_copy(pert_in.at[:, :, 0], pert.at[:, :, 0], sems.at[2]),
        pltpu.make_async_copy(zonal_in, zonal_t, sems.at[3]),
        pltpu.make_async_copy(pert_in.at[:, :, 1], pert.at[:, :, 1], sems.at[4]),
    ]
    for copy in copies:
        copy.start()

    def weights(v, level, rt, lt):
        at = (v, level, pl.ds(rt * 8, 8), pl.ds(lt * 128, 128))
        return weight[at] * innovations[at]

    def ready(stage):
        for copy in (copies[:3], copies[3:4], copies[4:])[stage]:
            copy.wait()

    project_and_send(weights, pert, zonal_t, proj, coef, send, ready=ready)


def chunk_pieces(me, parts):
    half = CHUNK // 2
    for j, part in zip((0, 2, 6, 1, 7, 3, 5), parts):
        yield lax.rem(me + (RING - j), RING), pl.ds(0, CHUNK), part[pl.ds(0, CHUNK), :]
    for side in range(2):
        yield lax.rem(me + RING // 2, RING), pl.ds(side * half, half), parts[7 + side][...]


def assemble(me, parts, field):
    for c, rows, value in chunk_pieces(me, parts):
        field[c, rows, :] = value


def own_columns(me, field, out):
    start = (3 * me) // 2
    odd = lax.rem(me, 2) == 1
    for c in range(RING):
        for rt in range(TILES):
            at = pl.multiple_of((rt * LTILES + start) * 8, 8)
            window = jnp.concatenate(
                [field[c, pl.ds(at, 8), :], field[c, pl.ds(at + 8, 8), :]], axis=1
            )
            window = jnp.where(odd, pltpu.roll(window, 192, 1), window)
            out[c // LEV, c % LEV, pl.ds(rt * 8, 8), :] = window[:, :SHARE]


def weigh(weight, field):
    energy = [jnp.zeros((8, 128), jnp.float32)]

    def weights(v, level, rt, lt):
        value = field[v * LEV + level, pl.ds((rt * LTILES + lt) * 8, 8), :]
        weighted = weight[v, level, pl.ds(rt * 8, 8), pl.ds(lt * 128, 128)] * value
        energy[0] = energy[0] + weighted * value
        return weighted

    return weights, lambda: total_of(energy[0])


def second_kernel(me_ref, pert, weight, zonal_t, *refs):
    parts, (send, field, own, scal, proj, coef) = refs[: RING + 1], refs[RING + 1 :]
    me = me_ref[0]
    assemble(me, parts, field)
    own_columns(me, field, own)
    scal[...] = parts[0][pl.ds(CHUNK, 8), :]
    weights, energy = weigh(weight, field)
    project_and_send(weights, pert, zonal_t, proj, coef, send, spare=energy)


def third_kernel(me_ref, pert, weight, zonal_t, old_scal, old_field, *refs):
    parts, (send, own, scal, proj, coef, field) = refs[: RING + 1], refs[RING + 1 :]
    me = me_ref[0]
    norm = old_scal[0:1, 0:1]
    norm_next = parts[0][CHUNK : CHUNK + 1, 0:1]
    cross = parts[0][CHUNK + 1 : CHUNK + 2, 0:1]
    beta = norm_next / norm
    for c, rows, value in chunk_pieces(me, parts):
        field[c, rows, :] = value + beta * old_field[c, rows, :]
    own_columns(me, field, own)
    square = norm_next + 2.0 * beta * cross + beta * beta * norm
    row = lax.broadcasted_iota(jnp.int32, (8, 128), 0)
    scal[...] = jnp.where(row == 0, norm_next, jnp.where(row == 1, square, beta))
    weights, energy = weigh(weight, field)
    project_and_send(weights, pert, zonal_t, proj, coef, send, spare=energy)


def to_modes(received, level, merid_t):
    lane = lax.broadcasted_iota(jnp.int32, (MW, 128), 1)
    sums = []
    for tile in range(2):
        data = received[:, pl.ds(level * 16 + tile * 8, 8), :].reshape(BANDS * 8, 128)
        high, low = split(data)
        sums.append(
            dot(merid_t[tile, 0], high) + dot(merid_t[tile, 0], low) + dot(merid_t[tile, 1], high)
        )
    result = sums[0][:MW] + jnp.where(lane < 48, pltpu.roll(sums[0][MW:], 48, 1), 0.0)
    result = result + jnp.where(lane >= 48, pltpu.roll(sums[1][:MW], 48, 1), 0.0)
    result = result + pltpu.roll(sums[1][MW:], 96, 1)
    return jnp.where(lane < 80, result, 0.0)


def to_rows(value, merid, level, send, spares):
    lane = lax.broadcasted_iota(jnp.int32, (MW, 128), 1)
    moved = pltpu.roll(value, 80, 1)
    second = jnp.where(lane >= 80, moved, 0.0)
    third = jnp.where(lane < 32, moved, 0.0)
    fourth = pltpu.roll(value, 32, 1)
    for tile, pair in enumerate(((value, second), (third, fourth))):
        high, low = split(jnp.concatenate(pair, axis=0))
        rows = dot(merid[tile, 0], high) + dot(merid[tile, 0], low) + dot(merid[tile, 1], high)
        if tile == 1 and spares:
            row = lax.broadcasted_iota(jnp.int32, (BANDS * 8, 128), 0)
            column = lax.broadcasted_iota(jnp.int32, (BANDS * 8, 128), 1)
            top = (row % 8) == 0
            for position, spare in enumerate(spares):
                rows = rows + jnp.where(top & (column == 112 + 8 * position), spare, 0.0)
        send[:, pl.ds(level * 16 + tile * 8, 8), :] = rows.reshape(BANDS, 8, 128)


def spare_sum(received):
    data = received[:, pl.ds(8, 8), :].reshape(BANDS * 8, 128)
    row = lax.broadcasted_iota(jnp.int32, (BANDS * 8, 128), 0)
    column = lax.broadcasted_iota(jnp.int32, (BANDS * 8, 128), 1)
    return total_of(jnp.where(((row % 8) == 0) & (column == 112), data, 0.0))


def scale_of(localization):
    return jnp.concatenate([localization[...]] * 16, axis=0).T


def gradient_kernel(received, localization, merid_t, merid, send, gradient):
    scale = scale_of(localization)
    acc = jnp.zeros((MW, 128), jnp.float32)
    for level in range(LEV):
        value = to_modes(received, level, merid_t) * scale
        gradient[level] = value
        acc = acc + value * value
    norm = total_of(acc)
    for level in range(LEV):
        to_rows(gradient[level] * scale, merid, level, send, (norm,) if level == 0 else ())


def residual_kernel(received, localization, merid_t, merid, gradient, scal, send, residual, step_out):
    scale = scale_of(localization)
    norm = scal[0:1, 0:1]
    step = norm / (norm + spare_sum(received))
    step_out[...] = jnp.broadcast_to(step, (8, 128))
    squares = jnp.zeros((MW, 128), jnp.float32)
    cross = jnp.zeros((MW, 128), jnp.float32)
    for level in range(LEV):
        old = gradient[level]
        image = old + to_modes(received, level, merid_t) * scale
        value = old - step * image
        residual[level] = value
        squares = squares + value * value
        cross = cross + value * old
    spares = (total_of(squares), total_of(cross))
    for level in range(LEV):
        to_rows(residual[level] * scale, merid, level, send, spares if level == 0 else ())


def last_kernel(
    received, localization, merid_t, gradient, residual, scal, step_in, first_own, second_own,
    control_out, residual_out, increment_out,
):
    scale = scale_of(localization)
    norm_next, square, beta = scal[0:1, 0:1], scal[1:2, 0:1], scal[2:3, 0:1]
    first_step = step_in[0:1, 0:1]
    step = norm_next / (square + spare_sum(received))
    for level in range(LEV):
        old, res = gradient[level], residual[level]
        direction = res + beta * old
        image = direction + to_modes(received, level, merid_t) * scale
        for out, value in (
            (control_out, first_step * old + step * direction),
            (residual_out, res - step * image),
        ):
            turned = value.T
            for k in range(KLOC):
                out[k, level] = turned[k * 8 : k * 8 + 8]
    increment_out[...] = first_step[None, None] * first_own[...] + step[None, None] * second_own[...]


def synth_kernel(me_ref, received, zonal, pert_in, *refs):
    outs, (coef, amp, total, pert, sems) = refs[:RING], refs[RING:]
    me = me_ref[0]
    copies = [
        pltpu.make_async_copy(pert_in.at[:, :, level], pert.at[:, :, level], sems.at[level])
        for level in range(LEV)
    ]
    for copy in copies:
        copy.start()
    for level in range(LEV):
        for tile in range(2):
            for half in range(2):
                got = swap_groups(
                    received[half * 16 + g, pl.ds(level * 16 + tile * 8, 8), :] for g in range(16)
                )
                for i in range(16):
                    at = level * 256 + (tile * 16 + i) * 8
                    coef[pl.ds(at, 8), pl.ds(half * 128, 128)] = got[i]
    scalars = [total_of(coef[pl.ds(240 + 8 * i, 8), :]) for i in range(2)]
    for level in range(LEV):
        high, low = split(coef[pl.ds(level * 256, 240), :])
        for part in range(LTILES // 2):
            wide = pl.ds(part * 256, 256)
            amp[:, wide] = (
                dot(high, zonal[0, :, wide])
                + dot(low, zonal[0, :, wide])
                + dot(high, zonal[1, :, wide])
            )
        copies[level].wait()
        for lt in range(LTILES):
            lanes = pl.ds(lt * 128, 128)
            sums = [jnp.zeros((ROWS, 128), jnp.float32)] * VARS
            for k in range(KLOC):
                field = jnp.concatenate(
                    [amp[pl.ds((rt * KLOC + k) * 8, 8), lanes] for rt in range(TILES)], axis=0
                )
                for v in range(VARS):
                    sums[v] = sums[v] + pert[k, v, level, :, lanes].astype(jnp.float32) * field
            for v in range(VARS):
                for rt in range(TILES):
                    total[v * LEV + level, pl.ds((rt * LTILES + lt) * 8, 8), :] = sums[v][
                        rt * 8 : rt * 8 + 8
                    ]
    row = lax.broadcasted_iota(jnp.int32, (8, 128), 0)
    extra = jnp.where(row == 0, scalars[0], jnp.where(row == 1, scalars[1], 0.0))
    for j in range(RING):
        outs[j][pl.ds(0, CHUNK), :] = total[lax.rem(me + j, RING)]
        outs[j][pl.ds(CHUNK, 8), :] = extra


def f32(*shape):
    return jax.ShapeDtypeStruct(shape, jnp.float32)


def call(kernel, outs, scratch, *args, scalars=0, flops=0, far=0, limit=16):
    in_specs = [pl.BlockSpec(memory_space=pltpu.SMEM)] * scalars
    in_specs += [pl.BlockSpec(memory_space=pltpu.VMEM)] * (len(args) - scalars - far)
    in_specs += [pl.BlockSpec(memory_space=pl.ANY)] * far
    moved = sum(math.prod(a.shape) * a.dtype.itemsize for a in args)
    return pl.pallas_call(
        kernel,
        out_shape=outs,
        in_specs=in_specs,
        out_specs=jax.tree.map(lambda _: pl.BlockSpec(memory_space=pltpu.VMEM), outs),
        scratch_shapes=scratch,
        compiler_params=pltpu.CompilerParams(vmem_limit_bytes=limit * 1024 * 1024),
        cost_estimate=pl.CostEstimate(flops=flops, bytes_accessed=moved, transcendentals=0),
    )(*args)


def ring_permute(value, distance):
    return lax.ppermute(value, "member", [(i, (i + distance) % RING) for i in range(RING)])


def sum_members(outs):
    half = CHUNK // 2
    rest = CHUNK + 8 - half
    right4, left4 = ring_permute(outs[4][:half], 2), ring_permute(outs[4][half:], -2)
    right3, left3 = ring_permute(outs[3], 1), ring_permute(outs[5], -1)
    right1, left1 = ring_permute(outs[1], 1), ring_permute(outs[7], -1)
    right = outs[2] + right3 + jnp.pad(right4, ((0, rest), (0, 0)))
    left = outs[6] + left3 + jnp.pad(left4, ((half, 0), (0, 0)))
    right, left = lax.optimization_barrier((right, left))
    own = outs[0] + right1 + left1 + ring_permute(right, 2) + ring_permute(left, -2)
    mine = own[:CHUNK]
    right2, left2 = ring_permute(mine, 2), ring_permute(mine, -2)
    right1, left1 = ring_permute(mine, 1), ring_permute(mine, -1)
    right2, left2 = lax.optimization_barrier((right2, left2))
    right3, left3 = ring_permute(right2, 1), ring_permute(left2, -1)
    right4, left4 = ring_permute(right2[:half], 2), ring_permute(left2[half:], -2)
    return [own, right2, left2, right1, left1, right3, left3, right4, left4]


def local(perturbations, innovations, error_weight, localization):
    const = {name: jnp.asarray(value) for name, value in bases().items()}
    me = lax.axis_index("member").astype(jnp.int32)[None]
    payload = f32(BANDS, 32, 128)
    vmem = lambda *shape: pltpu.VMEM(shape, jnp.float32)
    project_scratch = [vmem(480, NLON), vmem(512, ZW)]
    synth_scratch = [
        vmem(512, ZW), vmem(240, NLON), vmem(RING, CHUNK, 128),
        pltpu.VMEM(perturbations.shape, jnp.bfloat16), pltpu.SemaphoreType.DMA((LEV,)),
    ]
    own = f32(VARS, LEV, ROWS, SHARE)
    modes = f32(LEV, MW, 128)
    field = f32(RING, CHUNK, 128)

    def exchange(value):
        return lax.all_to_all(value, "band", 0, 0)

    def synthesize(rows):
        outs = call(
            synth_kernel, [f32(CHUNK + 8, 128)] * RING, synth_scratch,
            me, rows, const["zonal"], perturbations, scalars=1, flops=1200000000, far=1, limit=57,
        )
        return sum_members(outs)

    sent = call(
        first_kernel, payload,
        project_scratch + [
            pltpu.VMEM(perturbations.shape, jnp.bfloat16), vmem(*innovations.shape),
            vmem(*error_weight.shape), pltpu.VMEM(const["zonal_t"].shape, jnp.bfloat16),
            pltpu.SemaphoreType.DMA((5,)),
        ],
        perturbations, innovations, error_weight, const["zonal_t"],
        flops=1200000000, far=4, limit=59,
    )
    sent, gradient = call(
        gradient_kernel, [payload, modes], [],
        exchange(sent), localization, const["merid_t"], const["merid"], flops=200000000,
    )
    parts = synthesize(exchange(sent))
    sent, first_field, first_own, scal = call(
        second_kernel, [payload, field, own, f32(8, 128)], project_scratch,
        me, perturbations, error_weight, const["zonal_t"], *parts, scalars=1, flops=1200000000,
    )
    sent, residual, step = call(
        residual_kernel, [payload, modes, f32(8, 128)], [],
        exchange(sent), localization, const["merid_t"], const["merid"], gradient, scal,
        flops=200000000,
    )
    parts = synthesize(exchange(sent))
    sent, second_own, scal = call(
        third_kernel, [payload, own, f32(8, 128)], project_scratch + [vmem(RING, CHUNK, 128)],
        me, perturbations, error_weight, const["zonal_t"], scal, first_field, *parts,
        scalars=1, flops=1200000000,
    )
    return tuple(call(
        last_kernel,
        [f32(KLOC, LEV, ZW // BANDS, MW), f32(KLOC, LEV, ZW // BANDS, MW), own], [],
        exchange(sent), localization, const["merid_t"], gradient, residual, scal, step,
        first_own, second_own, flops=100000000,
    ))


def solution(mesh):
    return jax.shard_map(
        local,
        mesh=mesh,
        in_specs=(
            P("member", None, None, "band", None),
            P(None, None, "band", None),
            P(None, None, "band", None),
            P("band", None),
        ),
        out_specs=(
            P("member", None, "band", None),
            P("member", None, "band", None),
            P(None, None, "band", "member"),
        ),
        check_vma=False,
    )
```

```python
import functools
import math

import jax
import jax.numpy as jnp
import ml_dtypes
import numpy as np
from jax import lax
from jax.experimental import pallas as pl
from jax.experimental.pallas import tpu as pltpu
from jax.sharding import PartitionSpec as P

NLON = 1536
NLAT = 768
ZW = 256
MW = 128
VARS = 4
LEV = 2
KLOC = 10
BANDS = 32
RING = 8
ROWS = 24
TILES = 3
LTILES = NLON // 128
SHARE = NLON // RING
CHUNK = TILES * LTILES * 8
SLOTS = TILES * KLOC


def halves(array):
    high = array.astype(np.float32).astype(ml_dtypes.bfloat16)
    low = (array - high.astype(np.float64)).astype(np.float32).astype(ml_dtypes.bfloat16)
    return high, low


@functools.lru_cache(None)
def bases():
    wave = np.arange(ZW)
    number = (wave + 1) // 2
    angle = 2.0 * math.pi / NLON * ((number[:, None] * np.arange(NLON)[None, :]) % NLON)
    zonal = np.where((wave % 2 == 0)[:, None], np.cos(angle), np.sin(angle))
    zonal = zonal * (np.where(wave == 0, math.sqrt(0.5), 1.0) * math.sqrt(2.0 / NLON))[:, None]
    mode, row = np.arange(MW), np.arange(NLAT)
    angle = math.pi / (2.0 * NLAT) * ((mode[None, :] * (2 * row[:, None] + 1)) % (4 * NLAT))
    merid = np.cos(angle) * (np.where(mode == 0, math.sqrt(0.5), 1.0) * math.sqrt(2.0 / NLAT))
    parts = merid.reshape(BANDS, TILES, 8, MW).transpose(1, 0, 2, 3).reshape(TILES, BANDS * 8, MW)
    first = np.concatenate([parts[0], parts[1]], axis=1)
    second = np.concatenate([parts[1], parts[2]], axis=1)
    return {
        "zonal": np.stack(halves(zonal)),
        "zonal_t": np.stack(halves(zonal.T.copy())),
        "merid": np.stack([np.stack(halves(first)), np.stack(halves(second))]),
        "merid_t": np.stack([np.stack(halves(first.T.copy())), np.stack(halves(second.T.copy()))]),
    }


def split(value):
    high = value.astype(jnp.bfloat16)
    low = (value - high.astype(jnp.float32)).astype(jnp.bfloat16)
    return high, low


def dot(left, right):
    return jnp.dot(left, right, preferred_element_type=jnp.float32)


def swap_groups(vectors):
    group = lax.broadcasted_iota(jnp.int32, (8, 128), 1) // 8
    vectors = [pltpu.roll(v, 8 * i, 1) if i else v for i, v in enumerate(vectors)]
    for bit in (1, 2, 4, 8):
        move = (group & bit) != 0
        vectors = [jnp.where(move, vectors[(j + bit) % 16], vectors[j]) for j in range(16)]
    return [pltpu.roll(vectors[16 - g], 128 - 8 * g, 1) if g else vectors[0] for g in range(16)]


def total_of(value):
    return jnp.sum(jnp.sum(value, axis=1, keepdims=True), axis=0, keepdims=True)


def project_and_send(weights, pert, zonal_t, proj, coef, send, spare=None, ready=None):
    def zonal(first, rows):
        high, low = split(proj[pl.ds(first, rows), :])
        return dot(high, zonal_t[0]) + dot(low, zonal_t[0]) + dot(high, zonal_t[1])

    def keep(level, result):
        coef[pl.ds(level * 256, 240), :] = result
        coef[pl.ds(level * 256 + 240, 16), :] = jnp.zeros((16, ZW), jnp.float32)

    for level in range(LEV):
        if ready:
            ready(2 * level)
        for lt in range(LTILES):
            lanes = pl.ds(lt * 128, 128)
            fields = [
                jnp.concatenate([weights(v, level, rt, lt) for rt in range(TILES)], axis=0)
                for v in range(VARS)
            ]
            for k in range(KLOC):
                acc = pert[k, 0, level, :, lanes].astype(jnp.float32) * fields[0]
                for v in range(1, VARS):
                    acc = acc + pert[k, v, level, :, lanes].astype(jnp.float32) * fields[v]
                for rt in range(TILES):
                    proj[pl.ds(level * 240 + (rt * KLOC + k) * 8, 8), lanes] = acc[
                        rt * 8 : rt * 8 + 8
                    ]
        if ready:
            if level == 0:
                ready(1)
            keep(level, zonal(level * 240, 240))
    if not ready:
        result = zonal(0, 480)
        for level in range(LEV):
            keep(level, result[level * 240 : level * 240 + 240])
    if spare:
        coef[pl.ds(240, 8), :] = jnp.broadcast_to(spare(), (8, ZW))
    for level in range(LEV):
        for tile in range(2):
            for half in range(2):
                got = swap_groups(
                    coef[pl.ds(level * 256 + (tile * 16 + i) * 8, 8), pl.ds(half * 128, 128)]
                    for i in range(16)
                )
                for g in range(16):
                    send[half * 16 + g, pl.ds(level * 16 + tile * 8, 8), :] = got[g]


def first_kernel(
    pert_in, innovations_in, weight_in, zonal_in, send, pert,
    proj, coef, innovations, weight, zonal_t, sems,
):
    copies = [
        pltpu.make_async_copy(innovations_in, innovations, sems.at[0]),
        pltpu.make_async_copy(weight_in, weight, sems.at[1]),
        pltpu.make_async_copy(pert_in.at[:, :, 0], pert.at[:, :, 0], sems.at[2]),
        pltpu.make_async_copy(zonal_in, zonal_t, sems.at[3]),
        pltpu.make_async_copy(pert_in.at[:, :, 1], pert.at[:, :, 1], sems.at[4]),
    ]
    for copy in copies:
        copy.start()

    def weights(v, level, rt, lt):
        at = (v, level, pl.ds(rt * 8, 8), pl.ds(lt * 128, 128))
        return weight[at] * innovations[at]

    def ready(stage):
        for copy in (copies[:3], copies[3:4], copies[4:])[stage]:
            copy.wait()

    project_and_send(weights, pert, zonal_t, proj, coef, send, ready=ready)


def chunk_pieces(me, parts):
    half = CHUNK // 2
    for j, part in zip((0, 2, 6, 1, 7, 3, 5), parts):
        yield lax.rem(me + (RING - j), RING), pl.ds(0, CHUNK), part[pl.ds(0, CHUNK), :]
    for side in range(2):
        yield lax.rem(me + RING // 2, RING), pl.ds(side * half, half), parts[7 + side][...]


def assemble(me, parts, field):
    for c, rows, value in chunk_pieces(me, parts):
        field[c, rows, :] = value


def own_columns(me, field, out):
    start = (3 * me) // 2
    odd = lax.rem(me, 2) == 1
    for c in range(RING):
        for rt in range(TILES):
            at = pl.multiple_of((rt * LTILES + start) * 8, 8)
            window = jnp.concatenate(
                [field[c, pl.ds(at, 8), :], field[c, pl.ds(at + 8, 8), :]], axis=1
            )
            window = jnp.where(odd, pltpu.roll(window, 192, 1), window)
            out[c // LEV, c % LEV, pl.ds(rt * 8, 8), :] = window[:, :SHARE]


def weigh(weight, field):
    energy = [jnp.zeros((8, 128), jnp.float32)]

    def weights(v, level, rt, lt):
        value = field[v * LEV + level, pl.ds((rt * LTILES + lt) * 8, 8), :]
        weighted = weight[v, level, pl.ds(rt * 8, 8), pl.ds(lt * 128, 128)] * value
        energy[0] = energy[0] + weighted * value
        return weighted

    return weights, lambda: total_of(energy[0])


def second_kernel(me_ref, pert, weight, zonal_t, *refs):
    parts, (send, field, own, scal, proj, coef) = refs[: RING + 1], refs[RING + 1 :]
    me = me_ref[0]
    assemble(me, parts, field)
    own_columns(me, field, own)
    scal[...] = parts[0][pl.ds(CHUNK, 8), :]
    weights, energy = weigh(weight, field)
    project_and_send(weights, pert, zonal_t, proj, coef, send, spare=energy)


def third_kernel(me_ref, pert, weight, zonal_t, old_scal, old_field, *refs):
    parts, (send, own, scal, proj, coef, field) = refs[: RING + 1], refs[RING + 1 :]
    me = me_ref[0]
    norm = old_scal[0:1, 0:1]
    norm_next = parts[0][CHUNK : CHUNK + 1, 0:1]
    cross = parts[0][CHUNK + 1 : CHUNK + 2, 0:1]
    beta = norm_next / norm
    for c, rows, value in chunk_pieces(me, parts):
        field[c, rows, :] = value + beta * old_field[c, rows, :]
    own_columns(me, field, own)
    square = norm_next + 2.0 * beta * cross + beta * beta * norm
    row = lax.broadcasted_iota(jnp.int32, (8, 128), 0)
    scal[...] = jnp.where(row == 0, norm_next, jnp.where(row == 1, square, beta))
    weights, energy = weigh(weight, field)
    project_and_send(weights, pert, zonal_t, proj, coef, send, spare=energy)


def to_modes(received, level, merid_t):
    lane = lax.broadcasted_iota(jnp.int32, (MW, 128), 1)
    sums = []
    for tile in range(2):
        data = received[:, pl.ds(level * 16 + tile * 8, 8), :].reshape(BANDS * 8, 128)
        high, low = split(data)
        sums.append(
            dot(merid_t[tile, 0], high) + dot(merid_t[tile, 0], low) + dot(merid_t[tile, 1], high)
        )
    result = sums[0][:MW] + jnp.where(lane < 48, pltpu.roll(sums[0][MW:], 48, 1), 0.0)
    result = result + jnp.where(lane >= 48, pltpu.roll(sums[1][:MW], 48, 1), 0.0)
    result = result + pltpu.roll(sums[1][MW:], 96, 1)
    return jnp.where(lane < 80, result, 0.0)


def to_rows(value, merid, level, send, spares):
    lane = lax.broadcasted_iota(jnp.int32, (MW, 128), 1)
    moved = pltpu.roll(value, 80, 1)
    second = jnp.where(lane >= 80, moved, 0.0)
    third = jnp.where(lane < 32, moved, 0.0)
    fourth = pltpu.roll(value, 32, 1)
    for tile, pair in enumerate(((value, second), (third, fourth))):
        high, low = split(jnp.concatenate(pair, axis=0))
        rows = dot(merid[tile, 0], high) + dot(merid[tile, 0], low) + dot(merid[tile, 1], high)
        if tile == 1 and spares:
            row = lax.broadcasted_iota(jnp.int32, (BANDS * 8, 128), 0)
            column = lax.broadcasted_iota(jnp.int32, (BANDS * 8, 128), 1)
            top = (row % 8) == 0
            for position, spare in enumerate(spares):
                rows = rows + jnp.where(top & (column == 112 + 8 * position), spare, 0.0)
        send[:, pl.ds(level * 16 + tile * 8, 8), :] = rows.reshape(BANDS, 8, 128)


def spare_sum(received):
    data = received[:, pl.ds(8, 8), :].reshape(BANDS * 8, 128)
    row = lax.broadcasted_iota(jnp.int32, (BANDS * 8, 128), 0)
    column = lax.broadcasted_iota(jnp.int32, (BANDS * 8, 128), 1)
    return total_of(jnp.where(((row % 8) == 0) & (column == 112), data, 0.0))


def scale_of(localization):
    return jnp.concatenate([localization[...]] * 16, axis=0).T


def gradient_kernel(received, localization, merid_t, merid, send, gradient):
    scale = scale_of(localization)
    acc = jnp.zeros((MW, 128), jnp.float32)
    for level in range(LEV):
        value = to_modes(received, level, merid_t) * scale
        gradient[level] = value
        acc = acc + value * value
    norm = total_of(acc)
    for level in range(LEV):
        to_rows(gradient[level] * scale, merid, level, send, (norm,) if level == 0 else ())


def residual_kernel(received, localization, merid_t, merid, gradient, scal, send, residual, step_out):
    scale = scale_of(localization)
    norm = scal[0:1, 0:1]
    step = norm / (norm + spare_sum(received))
    step_out[...] = jnp.broadcast_to(step, (8, 128))
    squares = jnp.zeros((MW, 128), jnp.float32)
    cross = jnp.zeros((MW, 128), jnp.float32)
    for level in range(LEV):
        old = gradient[level]
        image = old + to_modes(received, level, merid_t) * scale
        value = old - step * image
        residual[level] = value
        squares = squares + value * value
        cross = cross + value * old
    spares = (total_of(squares), total_of(cross))
    for level in range(LEV):
        to_rows(residual[level] * scale, merid, level, send, spares if level == 0 else ())


def last_kernel(
    received, localization, merid_t, gradient, residual, scal, step_in, first_own, second_own,
    control_out, residual_out, increment_out,
):
    scale = scale_of(localization)
    norm_next, square, beta = scal[0:1, 0:1], scal[1:2, 0:1], scal[2:3, 0:1]
    first_step = step_in[0:1, 0:1]
    step = norm_next / (square + spare_sum(received))
    for level in range(LEV):
        old, res = gradient[level], residual[level]
        direction = res + beta * old
        image = direction + to_modes(received, level, merid_t) * scale
        for out, value in (
            (control_out, first_step * old + step * direction),
            (residual_out, res - step * image),
        ):
            turned = value.T
            for k in range(KLOC):
                out[k, level] = turned[k * 8 : k * 8 + 8]
    increment_out[...] = first_step[None, None] * first_own[...] + step[None, None] * second_own[...]


def chunk_of(me, ahead, amp, pert, extra, out):
    c = lax.rem(me + ahead, RING)
    variable, level = c // LEV, lax.rem(c, LEV)
    for lt in range(LTILES):
        lanes = pl.ds(lt * 128, 128)
        acc = jnp.zeros((ROWS, 128), jnp.float32)
        for k in range(KLOC):
            field = jnp.concatenate(
                [
                    amp[pl.ds(pl.multiple_of(level * 240 + (rt * KLOC + k) * 8, 8), 8), lanes]
                    for rt in range(TILES)
                ],
                axis=0,
            )
            acc = acc + pert[k, variable, level, :, lanes].astype(jnp.float32) * field
        for rt in range(TILES):
            out[pl.ds((rt * LTILES + lt) * 8, 8), :] = acc[rt * 8 : rt * 8 + 8]
    out[pl.ds(CHUNK, 8), :] = extra


def synth_kernel(me_ref, received, zonal, pert, out3, out4, out5, amp, extra, coef):
    me = me_ref[0]
    for level in range(LEV):
        for tile in range(2):
            for half in range(2):
                got = swap_groups(
                    received[half * 16 + g, pl.ds(level * 16 + tile * 8, 8), :] for g in range(16)
                )
                for i in range(16):
                    at = level * 256 + (tile * 16 + i) * 8
                    coef[pl.ds(at, 8), pl.ds(half * 128, 128)] = got[i]
    scalars = [total_of(coef[pl.ds(240 + 8 * i, 8), :]) for i in range(2)]
    high, low = split(jnp.concatenate([coef[pl.ds(0, 240), :], coef[pl.ds(256, 240), :]], axis=0))
    for part in range(LTILES // 2):
        wide = pl.ds(part * 256, 256)
        amp[:, wide] = (
            dot(high, zonal[0, :, wide]) + dot(low, zonal[0, :, wide]) + dot(high, zonal[1, :, wide])
        )
    row = lax.broadcasted_iota(jnp.int32, (8, 128), 0)
    extra[...] = jnp.where(row == 0, scalars[0], jnp.where(row == 1, scalars[1], 0.0))
    for ahead, out in ((4, out4), (3, out3), (5, out5)):
        chunk_of(me, ahead, amp, pert, extra[...], out)


def rest_kernel(me_ref, amp, pert, extra, out1, out7, out2, out6, out0):
    for ahead, out in ((1, out1), (7, out7), (2, out2), (6, out6), (0, out0)):
        chunk_of(me_ref[0], ahead, amp, pert, extra[...], out)


def f32(*shape):
    return jax.ShapeDtypeStruct(shape, jnp.float32)


def call(kernel, outs, scratch, *args, scalars=0, flops=0, far=0, limit=16):
    in_specs = [pl.BlockSpec(memory_space=pltpu.SMEM)] * scalars
    in_specs += [pl.BlockSpec(memory_space=pltpu.VMEM)] * (len(args) - scalars - far)
    in_specs += [pl.BlockSpec(memory_space=pl.ANY)] * far
    moved = sum(math.prod(a.shape) * a.dtype.itemsize for a in args)
    return pl.pallas_call(
        kernel,
        out_shape=outs,
        in_specs=in_specs,
        out_specs=jax.tree.map(lambda _: pl.BlockSpec(memory_space=pltpu.VMEM), outs),
        scratch_shapes=scratch,
        compiler_params=pltpu.CompilerParams(vmem_limit_bytes=limit * 1024 * 1024),
        cost_estimate=pl.CostEstimate(flops=flops, bytes_accessed=moved, transcendentals=0),
    )(*args)


def ring_permute(value, distance):
    return lax.ppermute(value, "member", [(i, (i + distance) % RING) for i in range(RING)])


def sum_members(outs):
    half = CHUNK // 2
    rest = CHUNK + 8 - half
    right4, left4 = ring_permute(outs[4][:half], 2), ring_permute(outs[4][half:], -2)
    right3, left3 = ring_permute(outs[3], 1), ring_permute(outs[5], -1)
    right1, left1 = ring_permute(outs[1], 1), ring_permute(outs[7], -1)
    right = outs[2] + right3 + jnp.pad(right4, ((0, rest), (0, 0)))
    left = outs[6] + left3 + jnp.pad(left4, ((half, 0), (0, 0)))
    right, left = lax.optimization_barrier((right, left))
    own = outs[0] + right1 + left1 + ring_permute(right, 2) + ring_permute(left, -2)
    mine = own[:CHUNK]
    right2, left2 = ring_permute(mine, 2), ring_permute(mine, -2)
    right1, left1 = ring_permute(mine, 1), ring_permute(mine, -1)
    right2, left2 = lax.optimization_barrier((right2, left2))
    right3, left3 = ring_permute(right2, 1), ring_permute(left2, -1)
    right4, left4 = ring_permute(right2[:half], 2), ring_permute(left2[half:], -2)
    return [own, right2, left2, right1, left1, right3, left3, right4, left4]


def local(perturbations, innovations, error_weight, localization):
    const = {name: jnp.asarray(value) for name, value in bases().items()}
    me = lax.axis_index("member").astype(jnp.int32)[None]
    payload = f32(BANDS, 32, 128)
    vmem = lambda *shape: pltpu.VMEM(shape, jnp.float32)
    project_scratch = [vmem(480, NLON), vmem(512, ZW)]
    own = f32(VARS, LEV, ROWS, SHARE)
    modes = f32(LEV, MW, 128)
    field = f32(RING, CHUNK, 128)

    def exchange(value):
        return lax.all_to_all(value, "band", 0, 0)

    def synthesize(rows):
        piece = f32(CHUNK + 8, 128)
        out3, out4, out5, amp, extra = call(
            synth_kernel, [piece] * 3 + [f32(480, NLON), f32(8, 128)], [vmem(512, ZW)],
            me, rows, const["zonal"], pert, scalars=1, flops=1200000000,
        )
        out1, out7, out2, out6, out0 = call(
            rest_kernel, [piece] * 5, [], me, amp, pert, extra, scalars=1, flops=400000000,
        )
        outs = [out0, out1, out2, out3, out4, out5, out6, out7]
        return sum_members(outs)

    sent, pert = call(
        first_kernel, [payload, jax.ShapeDtypeStruct(perturbations.shape, jnp.bfloat16)],
        project_scratch + [
            vmem(*innovations.shape),
            vmem(*error_weight.shape), pltpu.VMEM(const["zonal_t"].shape, jnp.bfloat16),
            pltpu.SemaphoreType.DMA((5,)),
        ],
        perturbations, innovations, error_weight, const["zonal_t"],
        flops=1200000000, far=4, limit=44,
    )
    sent, gradient = call(
        gradient_kernel, [payload, modes], [],
        exchange(sent), localization, const["merid_t"], const["merid"], flops=200000000,
    )
    parts = synthesize(exchange(sent))
    sent, first_field, first_own, scal = call(
        second_kernel, [payload, field, own, f32(8, 128)], project_scratch,
        me, pert, error_weight, const["zonal_t"], *parts, scalars=1, flops=1200000000,
    )
    sent, residual, step = call(
        residual_kernel, [payload, modes, f32(8, 128)], [],
        exchange(sent), localization, const["merid_t"], const["merid"], gradient, scal,
        flops=200000000,
    )
    parts = synthesize(exchange(sent))
    sent, second_own, scal = call(
        third_kernel, [payload, own, f32(8, 128)], project_scratch + [vmem(RING, CHUNK, 128)],
        me, pert, error_weight, const["zonal_t"], scal, first_field, *parts,
        scalars=1, flops=1200000000,
    )
    return tuple(call(
        last_kernel,
        [f32(KLOC, LEV, ZW // BANDS, MW), f32(KLOC, LEV, ZW // BANDS, MW), own], [],
        exchange(sent), localization, const["merid_t"], gradient, residual, scal, step,
        first_own, second_own, flops=100000000,
    ))


def solution(mesh):
    return jax.shard_map(
        local,
        mesh=mesh,
        in_specs=(
            P("member", None, None, "band", None),
            P(None, None, "band", None),
            P(None, None, "band", None),
            P("band", None),
        ),
        out_specs=(
            P("member", None, "band", None),
            P("member", None, "band", None),
            P(None, None, "band", "member"),
        ),
        check_vma=False,
    )
```

```python
import functools
import math

import jax
import jax.numpy as jnp
import ml_dtypes
import numpy as np
from jax import lax
from jax.experimental import pallas as pl
from jax.experimental.pallas import tpu as pltpu
from jax.sharding import PartitionSpec as P

NLON = 1536
NLAT = 768
ZW = 256
MW = 128
VARS = 4
LEV = 2
KLOC = 10
BANDS = 32
RING = 8
ROWS = 24
TILES = 3
LTILES = NLON // 128
SHARE = NLON // RING
CHUNK = TILES * LTILES * 8
SLOTS = TILES * KLOC


def halves(array):
    high = array.astype(np.float32).astype(ml_dtypes.bfloat16)
    low = (array - high.astype(np.float64)).astype(np.float32).astype(ml_dtypes.bfloat16)
    return high, low


@functools.lru_cache(None)
def bases():
    wave = np.arange(ZW)
    number = (wave + 1) // 2
    angle = 2.0 * math.pi / NLON * ((number[:, None] * np.arange(NLON)[None, :]) % NLON)
    zonal = np.where((wave % 2 == 0)[:, None], np.cos(angle), np.sin(angle))
    zonal = zonal * (np.where(wave == 0, math.sqrt(0.5), 1.0) * math.sqrt(2.0 / NLON))[:, None]
    mode, row = np.arange(MW), np.arange(NLAT)
    angle = math.pi / (2.0 * NLAT) * ((mode[None, :] * (2 * row[:, None] + 1)) % (4 * NLAT))
    merid = np.cos(angle) * (np.where(mode == 0, math.sqrt(0.5), 1.0) * math.sqrt(2.0 / NLAT))
    parts = merid.reshape(BANDS, TILES, 8, MW).transpose(1, 0, 2, 3).reshape(TILES, BANDS * 8, MW)
    first = np.concatenate([parts[0], parts[1]], axis=1)
    second = np.concatenate([parts[1], parts[2]], axis=1)
    return {
        "zonal": np.stack(halves(zonal)),
        "zonal_t": np.stack(halves(zonal.T.copy())),
        "merid": np.stack([np.stack(halves(first)), np.stack(halves(second))]),
        "merid_t": np.stack([np.stack(halves(first.T.copy())), np.stack(halves(second.T.copy()))]),
    }


def split(value):
    high = value.astype(jnp.bfloat16)
    low = (value - high.astype(jnp.float32)).astype(jnp.bfloat16)
    return high, low


def dot(left, right):
    return jnp.dot(left, right, preferred_element_type=jnp.float32)


def swap_groups(vectors):
    group = lax.broadcasted_iota(jnp.int32, (8, 128), 1) // 8
    vectors = [pltpu.roll(v, 8 * i, 1) if i else v for i, v in enumerate(vectors)]
    for bit in (1, 2, 4, 8):
        move = (group & bit) != 0
        vectors = [jnp.where(move, vectors[(j + bit) % 16], vectors[j]) for j in range(16)]
    return [pltpu.roll(vectors[16 - g], 128 - 8 * g, 1) if g else vectors[0] for g in range(16)]


def total_of(value):
    return jnp.sum(jnp.sum(value, axis=1, keepdims=True), axis=0, keepdims=True)


def project_and_send(weights, pert, zonal_t, proj, coef, send, spare=None, ready=None):
    def zonal(first, rows):
        high, low = split(proj[pl.ds(first, rows), :])
        return dot(high, zonal_t[0]) + dot(low, zonal_t[0]) + dot(high, zonal_t[1])

    def keep(level, result):
        coef[pl.ds(level * 256, 240), :] = result
        coef[pl.ds(level * 256 + 240, 16), :] = jnp.zeros((16, ZW), jnp.float32)

    for level in range(LEV):
        if ready:
            ready(2 * level)
        for lt in range(LTILES):
            lanes = pl.ds(lt * 128, 128)
            fields = [
                jnp.concatenate([weights(v, level, rt, lt) for rt in range(TILES)], axis=0)
                for v in range(VARS)
            ]
            for k in range(KLOC):
                acc = pert[k, 0, level, :, lanes].astype(jnp.float32) * fields[0]
                for v in range(1, VARS):
                    acc = acc + pert[k, v, level, :, lanes].astype(jnp.float32) * fields[v]
                for rt in range(TILES):
                    proj[pl.ds(level * 240 + (rt * KLOC + k) * 8, 8), lanes] = acc[
                        rt * 8 : rt * 8 + 8
                    ]
        if ready:
            if level == 0:
                ready(1)
            keep(level, zonal(level * 240, 240))
    if not ready:
        result = zonal(0, 480)
        for level in range(LEV):
            keep(level, result[level * 240 : level * 240 + 240])
    if spare:
        coef[pl.ds(240, 8), :] = jnp.broadcast_to(spare(), (8, ZW))
    for level in range(LEV):
        for tile in range(2):
            for half in range(2):
                got = swap_groups(
                    coef[pl.ds(level * 256 + (tile * 16 + i) * 8, 8), pl.ds(half * 128, 128)]
                    for i in range(16)
                )
                for g in range(16):
                    send[half * 16 + g, pl.ds(level * 16 + tile * 8, 8), :] = got[g]


def first_kernel(
    unused_me, pert_in, innovations_in, weight_in, zonal_in, send, pert,
    proj, coef, innovations, weight, zonal_t, sems,
):
    copies = [
        pltpu.make_async_copy(innovations_in, innovations, sems.at[0]),
        pltpu.make_async_copy(weight_in, weight, sems.at[1]),
        pltpu.make_async_copy(pert_in.at[:, :, 0], pert.at[:, :, 0], sems.at[2]),
        pltpu.make_async_copy(zonal_in, zonal_t, sems.at[3]),
        pltpu.make_async_copy(pert_in.at[:, :, 1], pert.at[:, :, 1], sems.at[4]),
    ]
    for copy in copies:
        copy.start()

    def weights(v, level, rt, lt):
        at = (v, level, pl.ds(rt * 8, 8), pl.ds(lt * 128, 128))
        return weight[at] * innovations[at]

    def ready(stage):
        for copy in (copies[:3], copies[3:4], copies[4:])[stage]:
            copy.wait()

    project_and_send(weights, pert, zonal_t, proj, coef, send, ready=ready)


def arrived(me, parts):
    for j, part in zip((0, 4, 2, 6, 1, 7, 3, 5), parts):
        yield lax.rem(me + (RING - j), RING), part[pl.ds(0, CHUNK), :]


def assemble(me, parts, field):
    for c, value in arrived(me, parts):
        field[c] = value


def own_columns(me, field, out):
    start = (3 * me) // 2
    odd = lax.rem(me, 2) == 1
    for c in range(RING):
        for rt in range(TILES):
            at = pl.multiple_of((rt * LTILES + start) * 8, 8)
            window = jnp.concatenate(
                [field[c, pl.ds(at, 8), :], field[c, pl.ds(at + 8, 8), :]], axis=1
            )
            window = jnp.where(odd, pltpu.roll(window, 192, 1), window)
            out[c // LEV, c % LEV, pl.ds(rt * 8, 8), :] = window[:, :SHARE]


def weigh(weight, field):
    energy = [jnp.zeros((8, 128), jnp.float32)]

    def weights(v, level, rt, lt):
        value = field[v * LEV + level, pl.ds((rt * LTILES + lt) * 8, 8), :]
        weighted = weight[v, level, pl.ds(rt * 8, 8), pl.ds(lt * 128, 128)] * value
        energy[0] = energy[0] + weighted * value
        return weighted

    return weights, lambda: total_of(energy[0])


def second_kernel(me_ref, pert, weight, zonal_t, *refs):
    parts, (send, field, own, scal, proj, coef) = refs[:RING], refs[RING:]
    me = me_ref[0]
    assemble(me, parts, field)
    own_columns(me, field, own)
    scal[...] = parts[0][pl.ds(CHUNK, 8), :]
    weights, energy = weigh(weight, field)
    project_and_send(weights, pert, zonal_t, proj, coef, send, spare=energy)


def third_kernel(me_ref, pert, weight, zonal_t, old_scal, old_field, *refs):
    parts, (send, own, scal, proj, coef, field) = refs[:RING], refs[RING:]
    me = me_ref[0]
    norm = old_scal[0:1, 0:1]
    norm_next = parts[0][CHUNK : CHUNK + 1, 0:1]
    cross = parts[0][CHUNK + 1 : CHUNK + 2, 0:1]
    beta = norm_next / norm
    for c, value in arrived(me, parts):
        field[c] = value + beta * old_field[c]
    own_columns(me, field, own)
    square = norm_next + 2.0 * beta * cross + beta * beta * norm
    row = lax.broadcasted_iota(jnp.int32, (8, 128), 0)
    scal[...] = jnp.where(row == 0, norm_next, jnp.where(row == 1, square, beta))
    weights, energy = weigh(weight, field)
    project_and_send(weights, pert, zonal_t, proj, coef, send, spare=energy)


def to_modes(received, level, merid_t):
    lane = lax.broadcasted_iota(jnp.int32, (MW, 128), 1)
    sums = []
    for tile in range(2):
        data = received[:, pl.ds(level * 16 + tile * 8, 8), :].reshape(BANDS * 8, 128)
        high, low = split(data)
        sums.append(
            dot(merid_t[tile, 0], high) + dot(merid_t[tile, 0], low) + dot(merid_t[tile, 1], high)
        )
    result = sums[0][:MW] + jnp.where(lane < 48, pltpu.roll(sums[0][MW:], 48, 1), 0.0)
    result = result + jnp.where(lane >= 48, pltpu.roll(sums[1][:MW], 48, 1), 0.0)
    result = result + pltpu.roll(sums[1][MW:], 96, 1)
    return jnp.where(lane < 80, result, 0.0)


def to_rows(value, merid, level, send, spares):
    lane = lax.broadcasted_iota(jnp.int32, (MW, 128), 1)
    moved = pltpu.roll(value, 80, 1)
    second = jnp.where(lane >= 80, moved, 0.0)
    third = jnp.where(lane < 32, moved, 0.0)
    fourth = pltpu.roll(value, 32, 1)
    for tile, pair in enumerate(((value, second), (third, fourth))):
        high, low = split(jnp.concatenate(pair, axis=0))
        rows = dot(merid[tile, 0], high) + dot(merid[tile, 0], low) + dot(merid[tile, 1], high)
        if tile == 1 and spares:
            row = lax.broadcasted_iota(jnp.int32, (BANDS * 8, 128), 0)
            column = lax.broadcasted_iota(jnp.int32, (BANDS * 8, 128), 1)
            top = (row % 8) == 0
            for position, spare in enumerate(spares):
                rows = rows + jnp.where(top & (column == 112 + 8 * position), spare, 0.0)
        send[:, pl.ds(level * 16 + tile * 8, 8), :] = rows.reshape(BANDS, 8, 128)


def spare_sum(received):
    data = received[:, pl.ds(8, 8), :].reshape(BANDS * 8, 128)
    row = lax.broadcasted_iota(jnp.int32, (BANDS * 8, 128), 0)
    column = lax.broadcasted_iota(jnp.int32, (BANDS * 8, 128), 1)
    return total_of(jnp.where(((row % 8) == 0) & (column == 112), data, 0.0))


def scale_of(localization):
    return jnp.concatenate([localization[...]] * 16, axis=0).T


def gradient_kernel(received, localization, merid_t, merid, send, gradient):
    scale = scale_of(localization)
    acc = jnp.zeros((MW, 128), jnp.float32)
    for level in range(LEV):
        value = to_modes(received, level, merid_t) * scale
        gradient[level] = value
        acc = acc + value * value
    norm = total_of(acc)
    for level in range(LEV):
        to_rows(gradient[level] * scale, merid, level, send, (norm,) if level == 0 else ())


def residual_kernel(received, localization, merid_t, merid, gradient, scal, send, residual, step_out):
    scale = scale_of(localization)
    norm = scal[0:1, 0:1]
    step = norm / (norm + spare_sum(received))
    step_out[...] = jnp.broadcast_to(step, (8, 128))
    squares = jnp.zeros((MW, 128), jnp.float32)
    cross = jnp.zeros((MW, 128), jnp.float32)
    for level in range(LEV):
        old = gradient[level]
        image = old + to_modes(received, level, merid_t) * scale
        value = old - step * image
        residual[level] = value
        squares = squares + value * value
        cross = cross + value * old
    spares = (total_of(squares), total_of(cross))
    for level in range(LEV):
        to_rows(residual[level] * scale, merid, level, send, spares if level == 0 else ())


def last_kernel(
    received, localization, merid_t, gradient, residual, scal, step_in, first_own, second_own,
    control_out, residual_out, increment_out,
):
    scale = scale_of(localization)
    norm_next, square, beta = scal[0:1, 0:1], scal[1:2, 0:1], scal[2:3, 0:1]
    first_step = step_in[0:1, 0:1]
    step = norm_next / (square + spare_sum(received))
    for level in range(LEV):
        old, res = gradient[level], residual[level]
        direction = res + beta * old
        image = direction + to_modes(received, level, merid_t) * scale
        for out, value in (
            (control_out, first_step * old + step * direction),
            (residual_out, res - step * image),
        ):
            turned = value.T
            for k in range(KLOC):
                out[k, level] = turned[k * 8 : k * 8 + 8]
    increment_out[...] = first_step[None, None] * first_own[...] + step[None, None] * second_own[...]


def chunk_of(me, ahead, amp, pert, extra, out):
    c = lax.rem(me + ahead, RING)
    variable, level = c // LEV, lax.rem(c, LEV)
    for lt in range(LTILES):
        lanes = pl.ds(lt * 128, 128)
        acc = jnp.zeros((ROWS, 128), jnp.float32)
        for k in range(KLOC):
            field = jnp.concatenate(
                [
                    amp[pl.ds(pl.multiple_of(level * 240 + (rt * KLOC + k) * 8, 8), 8), lanes]
                    for rt in range(TILES)
                ],
                axis=0,
            )
            acc = acc + pert[k, variable, level, :, lanes].astype(jnp.float32) * field
        for rt in range(TILES):
            out[pl.ds((rt * LTILES + lt) * 8, 8), :] = acc[rt * 8 : rt * 8 + 8]
    out[pl.ds(CHUNK, 8), :] = extra


def synth_kernel(me_ref, received, zonal, pert, out3, out4, out5, amp, extra, coef):
    me = me_ref[0]
    for level in range(LEV):
        for tile in range(2):
            for half in range(2):
                got = swap_groups(
                    received[half * 16 + g, pl.ds(level * 16 + tile * 8, 8), :] for g in range(16)
                )
                for i in range(16):
                    at = level * 256 + (tile * 16 + i) * 8
                    coef[pl.ds(at, 8), pl.ds(half * 128, 128)] = got[i]
    scalars = [total_of(coef[pl.ds(240 + 8 * i, 8), :]) for i in range(2)]
    high, low = split(jnp.concatenate([coef[pl.ds(0, 240), :], coef[pl.ds(256, 240), :]], axis=0))
    for part in range(LTILES // 2):
        wide = pl.ds(part * 256, 256)
        amp[:, wide] = (
            dot(high, zonal[0, :, wide]) + dot(low, zonal[0, :, wide]) + dot(high, zonal[1, :, wide])
        )
    row = lax.broadcasted_iota(jnp.int32, (8, 128), 0)
    extra[...] = jnp.where(row == 0, scalars[0], jnp.where(row == 1, scalars[1], 0.0))
    for ahead, out in ((4, out4), (3, out3), (5, out5)):
        chunk_of(me, ahead, amp, pert, extra[...], out)


def rest_kernel(me_ref, amp, pert, extra, out1, out7, out2, out6, out0):
    for ahead, out in ((1, out1), (7, out7), (2, out2), (6, out6), (0, out0)):
        chunk_of(me_ref[0], ahead, amp, pert, extra[...], out)


def f32(*shape):
    return jax.ShapeDtypeStruct(shape, jnp.float32)


def call(kernel, outs, scratch, *args, scalars=0, flops=0, far=0, limit=16):
    in_specs = [pl.BlockSpec(memory_space=pltpu.SMEM)] * scalars
    in_specs += [pl.BlockSpec(memory_space=pltpu.VMEM)] * (len(args) - scalars - far)
    in_specs += [pl.BlockSpec(memory_space=pl.ANY)] * far
    moved = sum(math.prod(a.shape) * a.dtype.itemsize for a in args)
    return pl.pallas_call(
        kernel,
        out_shape=outs,
        in_specs=in_specs,
        out_specs=jax.tree.map(lambda _: pl.BlockSpec(memory_space=pltpu.VMEM), outs),
        scratch_shapes=scratch,
        compiler_params=pltpu.CompilerParams(vmem_limit_bytes=limit * 1024 * 1024),
        cost_estimate=pl.CostEstimate(flops=flops, bytes_accessed=moved, transcendentals=0),
    )(*args)


def ring_permute(value, distance):
    return lax.ppermute(value, "member", [(i, (i + distance) % RING) for i in range(RING)])


def sum_members(outs):
    across = ring_permute(outs[4], 4)
    right3, left3 = ring_permute(outs[3], 1), ring_permute(outs[5], -1)
    right1, left1 = ring_permute(outs[1], 1), ring_permute(outs[7], -1)
    right, left = lax.optimization_barrier((outs[2] + right3, outs[6] + left3))
    own = outs[0] + across + right1 + left1 + ring_permute(right, 2) + ring_permute(left, -2)
    mine = own[:CHUNK]
    across = ring_permute(mine, 4)
    right2, left2 = ring_permute(mine, 2), ring_permute(mine, -2)
    right1, left1 = ring_permute(mine, 1), ring_permute(mine, -1)
    right2, left2 = lax.optimization_barrier((right2, left2))
    right3, left3 = ring_permute(right2, 1), ring_permute(left2, -1)
    return [own, across, right2, left2, right1, left1, right3, left3]


def local(perturbations, innovations, error_weight, localization):
    const = {name: jnp.asarray(value) for name, value in bases().items()}
    me = lax.axis_index("member").astype(jnp.int32)[None]
    payload = f32(BANDS, 32, 128)
    vmem = lambda *shape: pltpu.VMEM(shape, jnp.float32)
    project_scratch = [vmem(480, NLON), vmem(512, ZW)]
    own = f32(VARS, LEV, ROWS, SHARE)
    modes = f32(LEV, MW, 128)
    field = f32(RING, CHUNK, 128)

    def exchange(value):
        return lax.all_to_all(value, "band", 0, 0)

    def synthesize(rows):
        piece = f32(CHUNK + 8, 128)
        out3, out4, out5, amp, extra = call(
            synth_kernel, [piece] * 3 + [f32(480, NLON), f32(8, 128)], [vmem(512, ZW)],
            me, rows, const["zonal"], pert, scalars=1, flops=1200000000,
        )
        out1, out7, out2, out6, out0 = call(
            rest_kernel, [piece] * 5, [], me, amp, pert, extra, scalars=1, flops=400000000,
        )
        outs = [out0, out1, out2, out3, out4, out5, out6, out7]
        return sum_members(outs)

    sent, pert = call(
        first_kernel, [payload, jax.ShapeDtypeStruct(perturbations.shape, jnp.bfloat16)],
        project_scratch + [
            vmem(*innovations.shape),
            vmem(*error_weight.shape), pltpu.VMEM(const["zonal_t"].shape, jnp.bfloat16),
            pltpu.SemaphoreType.DMA((5,)),
        ],
        me, perturbations, innovations, error_weight, const["zonal_t"],
        scalars=1, flops=1200000000, far=4, limit=44,
    )
    sent, gradient = call(
        gradient_kernel, [payload, modes], [],
        exchange(sent), localization, const["merid_t"], const["merid"], flops=200000000,
    )
    parts = synthesize(exchange(sent))
    sent, first_field, first_own, scal = call(
        second_kernel, [payload, field, own, f32(8, 128)], project_scratch,
        me, pert, error_weight, const["zonal_t"], *parts, scalars=1, flops=1200000000,
    )
    sent, residual, step = call(
        residual_kernel, [payload, modes, f32(8, 128)], [],
        exchange(sent), localization, const["merid_t"], const["merid"], gradient, scal,
        flops=200000000,
    )
    parts = synthesize(exchange(sent))
    sent, second_own, scal = call(
        third_kernel, [payload, own, f32(8, 128)], project_scratch + [vmem(RING, CHUNK, 128)],
        me, pert, error_weight, const["zonal_t"], scal, first_field, *parts,
        scalars=1, flops=1200000000,
    )
    return tuple(call(
        last_kernel,
        [f32(KLOC, LEV, ZW // BANDS, MW), f32(KLOC, LEV, ZW // BANDS, MW), own], [],
        exchange(sent), localization, const["merid_t"], gradient, residual, scal, step,
        first_own, second_own, flops=100000000,
    ))


def solution(mesh):
    return jax.shard_map(
        local,
        mesh=mesh,
        in_specs=(
            P("member", None, None, "band", None),
            P(None, None, "band", None),
            P(None, None, "band", None),
            P("band", None),
        ),
        out_specs=(
            P("member", None, "band", None),
            P("member", None, "band", None),
            P(None, None, "band", "member"),
        ),
        check_vma=False,
    )
```

```python
import functools
import math

import jax
import jax.numpy as jnp
import ml_dtypes
import numpy as np
from jax import lax
from jax.experimental import pallas as pl
from jax.experimental.pallas import tpu as pltpu
from jax.sharding import PartitionSpec as P

NLON = 1536
NLAT = 768
ZW = 256
MW = 128
VARS = 4
LEV = 2
KLOC = 10
BANDS = 32
RING = 8
ROWS = 24
TILES = 3
LTILES = NLON // 128
SHARE = NLON // RING
CHUNK = TILES * LTILES * 8
SLOTS = TILES * KLOC


def halves(array):
    high = array.astype(np.float32).astype(ml_dtypes.bfloat16)
    low = (array - high.astype(np.float64)).astype(np.float32).astype(ml_dtypes.bfloat16)
    return high, low


@functools.lru_cache(None)
def bases():
    wave = np.arange(ZW)
    number = (wave + 1) // 2
    angle = 2.0 * math.pi / NLON * ((number[:, None] * np.arange(NLON)[None, :]) % NLON)
    zonal = np.where((wave % 2 == 0)[:, None], np.cos(angle), np.sin(angle))
    zonal = zonal * (np.where(wave == 0, math.sqrt(0.5), 1.0) * math.sqrt(2.0 / NLON))[:, None]
    mode, row = np.arange(MW), np.arange(NLAT)
    angle = math.pi / (2.0 * NLAT) * ((mode[None, :] * (2 * row[:, None] + 1)) % (4 * NLAT))
    merid = np.cos(angle) * (np.where(mode == 0, math.sqrt(0.5), 1.0) * math.sqrt(2.0 / NLAT))
    parts = merid.reshape(BANDS, TILES, 8, MW).transpose(1, 0, 2, 3).reshape(TILES, BANDS * 8, MW)
    first = np.concatenate([parts[0], parts[1]], axis=1)
    second = np.concatenate([parts[1], parts[2]], axis=1)
    return {
        "zonal": np.stack(halves(zonal)),
        "zonal_t": np.stack(halves(zonal.T.copy())),
        "merid": np.stack([np.stack(halves(first)), np.stack(halves(second))]),
        "merid_t": np.stack([np.stack(halves(first.T.copy())), np.stack(halves(second.T.copy()))]),
    }


def split(value):
    high = value.astype(jnp.bfloat16)
    low = (value - high.astype(jnp.float32)).astype(jnp.bfloat16)
    return high, low


def dot(left, right):
    return jnp.dot(left, right, preferred_element_type=jnp.float32)


def swap_groups(vectors):
    group = lax.broadcasted_iota(jnp.int32, (8, 128), 1) // 8
    vectors = [pltpu.roll(v, 8 * i, 1) if i else v for i, v in enumerate(vectors)]
    for bit in (1, 2, 4, 8):
        move = (group & bit) != 0
        vectors = [jnp.where(move, vectors[(j + bit) % 16], vectors[j]) for j in range(16)]
    return [pltpu.roll(vectors[16 - g], 128 - 8 * g, 1) if g else vectors[0] for g in range(16)]


def total_of(value):
    return jnp.sum(jnp.sum(value, axis=1, keepdims=True), axis=0, keepdims=True)


def project_and_send(weights, pert, zonal_t, proj, coef, send, spare=None, ready=None):
    def zonal(first, rows):
        high, low = split(proj[pl.ds(first, rows), :])
        return dot(high, zonal_t[0]) + dot(low, zonal_t[0]) + dot(high, zonal_t[1])

    def keep(level, result):
        coef[pl.ds(level * 256, 240), :] = result
        coef[pl.ds(level * 256 + 240, 16), :] = jnp.zeros((16, ZW), jnp.float32)

    def project(level, members):
        for lt in range(LTILES):
            lanes = pl.ds(lt * 128, 128)
            fields = [
                jnp.concatenate([weights(v, level, rt, lt) for rt in range(TILES)], axis=0)
                for v in range(VARS)
            ]
            for k in members:
                acc = pert[k, 0, level, :, lanes].astype(jnp.float32) * fields[0]
                for v in range(1, VARS):
                    acc = acc + pert[k, v, level, :, lanes].astype(jnp.float32) * fields[v]
                for rt in range(TILES):
                    proj[pl.ds(level * 240 + (rt * KLOC + k) * 8, 8), lanes] = acc[
                        rt * 8 : rt * 8 + 8
                    ]

    def regroup(level):
        for tile in range(2):
            for half in range(2):
                got = swap_groups(
                    coef[pl.ds(level * 256 + (tile * 16 + i) * 8, 8), pl.ds(half * 128, 128)]
                    for i in range(16)
                )
                for g in range(16):
                    send[half * 16 + g, pl.ds(level * 16 + tile * 8, 8), :] = got[g]

    if ready:
        for level in range(LEV):
            ready("fields", level)
            for piece in range(2):
                ready("members", level, piece)
                project(level, range(piece * KLOC // 2, (piece + 1) * KLOC // 2))
            if level == 0:
                ready("basis")
            keep(level, zonal(level * 240, 240))
            regroup(level)
        return
    for level in range(LEV):
        project(level, range(KLOC))
    result = zonal(0, 480)
    for level in range(LEV):
        keep(level, result[level * 240 : level * 240 + 240])
    coef[pl.ds(240, 8), :] = jnp.broadcast_to(spare(), (8, ZW))
    for level in range(LEV):
        regroup(level)


def first_kernel(
    unused_me, pert_in, innovations_in, weight_in, zonal_in, send,
    proj, coef, pert, innovations, weight, zonal_t, sems,
):
    copies = {}

    def begin(name, source, target):
        copies[name] = pltpu.make_async_copy(source, target, sems.at[len(copies)])
        copies[name].start()

    for level in range(LEV):
        begin(("innovations", level), innovations_in.at[:, level], innovations.at[:, level])
        begin(("weight", level), weight_in.at[:, level], weight.at[:, level])
        for piece in range(2):
            ks = pl.ds(piece * KLOC // 2, KLOC // 2)
            begin(("members", level, piece), pert_in.at[ks, :, level], pert.at[ks, :, level])
        if level == 0:
            begin(("basis",), zonal_in, zonal_t)

    def weights(v, level, rt, lt):
        at = (v, level, pl.ds(rt * 8, 8), pl.ds(lt * 128, 128))
        return weight[at] * innovations[at]

    def ready(*name):
        if name[0] == "fields":
            copies["innovations", name[1]].wait()
            copies["weight", name[1]].wait()
        else:
            copies[name].wait()

    project_and_send(weights, pert, zonal_t, proj, coef, send, ready=ready)


def arrived(me, parts):
    for j, part in zip((0, 4, 2, 6, 1, 7, 3, 5), parts):
        yield lax.rem(me + (RING - j), RING), part[pl.ds(0, CHUNK), :]


def assemble(me, parts, field):
    for c, value in arrived(me, parts):
        field[c] = value


def own_columns(me, field, out):
    start = (3 * me) // 2
    odd = lax.rem(me, 2) == 1
    for c in range(RING):
        for rt in range(TILES):
            at = pl.multiple_of((rt * LTILES + start) * 8, 8)
            window = jnp.concatenate(
                [field[c, pl.ds(at, 8), :], field[c, pl.ds(at + 8, 8), :]], axis=1
            )
            window = jnp.where(odd, pltpu.roll(window, 192, 1), window)
            out[c // LEV, c % LEV, pl.ds(rt * 8, 8), :] = window[:, :SHARE]


def weigh(weight, field):
    energy = [jnp.zeros((8, 128), jnp.float32)]

    def weights(v, level, rt, lt):
        value = field[v * LEV + level, pl.ds((rt * LTILES + lt) * 8, 8), :]
        weighted = weight[v, level, pl.ds(rt * 8, 8), pl.ds(lt * 128, 128)] * value
        energy[0] = energy[0] + weighted * value
        return weighted

    return weights, lambda: total_of(energy[0])


def second_kernel(me_ref, pert, weight, zonal_t, *refs):
    parts, (send, field, own, scal, proj, coef) = refs[:RING], refs[RING:]
    me = me_ref[0]
    assemble(me, parts, field)
    own_columns(me, field, own)
    scal[...] = parts[0][pl.ds(CHUNK, 8), :]
    weights, energy = weigh(weight, field)
    project_and_send(weights, pert, zonal_t, proj, coef, send, spare=energy)


def third_kernel(me_ref, pert, weight, zonal_t, old_scal, old_field, *refs):
    parts, (send, own, scal, proj, coef, field) = refs[:RING], refs[RING:]
    me = me_ref[0]
    norm = old_scal[0:1, 0:1]
    norm_next = parts[0][CHUNK : CHUNK + 1, 0:1]
    cross = parts[0][CHUNK + 1 : CHUNK + 2, 0:1]
    beta = norm_next / norm
    for c, value in arrived(me, parts):
        field[c] = value + beta * old_field[c]
    own_columns(me, field, own)
    square = norm_next + 2.0 * beta * cross + beta * beta * norm
    row = lax.broadcasted_iota(jnp.int32, (8, 128), 0)
    scal[...] = jnp.where(row == 0, norm_next, jnp.where(row == 1, square, beta))
    weights, energy = weigh(weight, field)
    project_and_send(weights, pert, zonal_t, proj, coef, send, spare=energy)


def to_modes(received, level, merid_t):
    lane = lax.broadcasted_iota(jnp.int32, (MW, 128), 1)
    sums = []
    for tile in range(2):
        data = received[:, pl.ds(level * 16 + tile * 8, 8), :].reshape(BANDS * 8, 128)
        high, low = split(data)
        sums.append(
            dot(merid_t[tile, 0], high) + dot(merid_t[tile, 0], low) + dot(merid_t[tile, 1], high)
        )
    result = sums[0][:MW] + jnp.where(lane < 48, pltpu.roll(sums[0][MW:], 48, 1), 0.0)
    result = result + jnp.where(lane >= 48, pltpu.roll(sums[1][:MW], 48, 1), 0.0)
    result = result + pltpu.roll(sums[1][MW:], 96, 1)
    return jnp.where(lane < 80, result, 0.0)


def to_rows(value, merid, level, send, spares):
    lane = lax.broadcasted_iota(jnp.int32, (MW, 128), 1)
    moved = pltpu.roll(value, 80, 1)
    second = jnp.where(lane >= 80, moved, 0.0)
    third = jnp.where(lane < 32, moved, 0.0)
    fourth = pltpu.roll(value, 32, 1)
    for tile, pair in enumerate(((value, second), (third, fourth))):
        high, low = split(jnp.concatenate(pair, axis=0))
        rows = dot(merid[tile, 0], high) + dot(merid[tile, 0], low) + dot(merid[tile, 1], high)
        if tile == 1 and spares:
            row = lax.broadcasted_iota(jnp.int32, (BANDS * 8, 128), 0)
            column = lax.broadcasted_iota(jnp.int32, (BANDS * 8, 128), 1)
            top = (row % 8) == 0
            for position, spare in enumerate(spares):
                rows = rows + jnp.where(top & (column == 112 + 8 * position), spare, 0.0)
        send[:, pl.ds(level * 16 + tile * 8, 8), :] = rows.reshape(BANDS, 8, 128)


def spare_sum(received):
    data = received[:, pl.ds(8, 8), :].reshape(BANDS * 8, 128)
    row = lax.broadcasted_iota(jnp.int32, (BANDS * 8, 128), 0)
    column = lax.broadcasted_iota(jnp.int32, (BANDS * 8, 128), 1)
    return total_of(jnp.where(((row % 8) == 0) & (column == 112), data, 0.0))


def scale_of(localization):
    return jnp.concatenate([localization[...]] * 16, axis=0).T


def gradient_kernel(received, localization, merid_t, merid, send, gradient):
    scale = scale_of(localization)
    acc = jnp.zeros((MW, 128), jnp.float32)
    for level in range(LEV):
        value = to_modes(received, level, merid_t) * scale
        gradient[level] = value
        acc = acc + value * value
    norm = total_of(acc)
    for level in range(LEV):
        to_rows(gradient[level] * scale, merid, level, send, (norm,) if level == 0 else ())


def residual_kernel(received, localization, merid_t, merid, gradient, scal, send, residual, step_out):
    scale = scale_of(localization)
    norm = scal[0:1, 0:1]
    step = norm / (norm + spare_sum(received))
    step_out[...] = jnp.broadcast_to(step, (8, 128))
    squares = jnp.zeros((MW, 128), jnp.float32)
    cross = jnp.zeros((MW, 128), jnp.float32)
    for level in range(LEV):
        old = gradient[level]
        image = old + to_modes(received, level, merid_t) * scale
        value = old - step * image
        residual[level] = value
        squares = squares + value * value
        cross = cross + value * old
    spares = (total_of(squares), total_of(cross))
    for level in range(LEV):
        to_rows(residual[level] * scale, merid, level, send, spares if level == 0 else ())


def last_kernel(
    received, localization, merid_t, gradient, residual, scal, step_in, first_own, second_own,
    control_out, residual_out, increment_out,
):
    scale = scale_of(localization)
    norm_next, square, beta = scal[0:1, 0:1], scal[1:2, 0:1], scal[2:3, 0:1]
    first_step = step_in[0:1, 0:1]
    step = norm_next / (square + spare_sum(received))
    for level in range(LEV):
        old, res = gradient[level], residual[level]
        direction = res + beta * old
        image = direction + to_modes(received, level, merid_t) * scale
        for out, value in (
            (control_out, first_step * old + step * direction),
            (residual_out, res - step * image),
        ):
            turned = value.T
            for k in range(KLOC):
                out[k, level] = turned[k * 8 : k * 8 + 8]
    increment_out[...] = first_step[None, None] * first_own[...] + step[None, None] * second_own[...]


def chunk_of(me, ahead, amp, pert, extra, out):
    c = lax.rem(me + ahead, RING)
    variable, level = c // LEV, lax.rem(c, LEV)
    for lt in range(LTILES):
        lanes = pl.ds(lt * 128, 128)
        acc = jnp.zeros((ROWS, 128), jnp.float32)
        for k in range(KLOC):
            field = jnp.concatenate(
                [
                    amp[pl.ds(pl.multiple_of(level * 240 + (rt * KLOC + k) * 8, 8), 8), lanes]
                    for rt in range(TILES)
                ],
                axis=0,
            )
            acc = acc + pert[k, variable, level, :, lanes].astype(jnp.float32) * field
        for rt in range(TILES):
            out[pl.ds((rt * LTILES + lt) * 8, 8), :] = acc[rt * 8 : rt * 8 + 8]
    out[pl.ds(CHUNK, 8), :] = extra


def synth_kernel(me_ref, received, zonal, pert, out3, out4, out5, amp, extra, coef):
    synthesize_first(me_ref[0], received, zonal, pert, out3, out4, out5, amp, extra, coef)


def fetch_kernel(
    me_ref, received, zonal, pert_in, out3, out4, out5, amp, extra, pert, coef, sem
):
    copy = pltpu.make_async_copy(pert_in, pert, sem)
    copy.start()
    synthesize_first(
        me_ref[0], received, zonal, pert, out3, out4, out5, amp, extra, coef, copy.wait
    )


def synthesize_first(
    me, received, zonal, pert, out3, out4, out5, amp, extra, coef, ready=lambda: None
):
    for level in range(LEV):
        for tile in range(2):
            for half in range(2):
                got = swap_groups(
                    received[half * 16 + g, pl.ds(level * 16 + tile * 8, 8), :] for g in range(16)
                )
                for i in range(16):
                    at = level * 256 + (tile * 16 + i) * 8
                    coef[pl.ds(at, 8), pl.ds(half * 128, 128)] = got[i]
    scalars = [total_of(coef[pl.ds(240 + 8 * i, 8), :]) for i in range(2)]
    high, low = split(jnp.concatenate([coef[pl.ds(0, 240), :], coef[pl.ds(256, 240), :]], axis=0))
    for part in range(LTILES // 2):
        wide = pl.ds(part * 256, 256)
        amp[:, wide] = (
            dot(high, zonal[0, :, wide]) + dot(low, zonal[0, :, wide]) + dot(high, zonal[1, :, wide])
        )
    row = lax.broadcasted_iota(jnp.int32, (8, 128), 0)
    extra[...] = jnp.where(row == 0, scalars[0], jnp.where(row == 1, scalars[1], 0.0))
    ready()
    for ahead, out in ((4, out4), (3, out3), (5, out5)):
        chunk_of(me, ahead, amp, pert, extra[...], out)


def rest_kernel(me_ref, amp, pert, extra, out1, out7, out2, out6, out0):
    for ahead, out in ((1, out1), (7, out7), (2, out2), (6, out6), (0, out0)):
        chunk_of(me_ref[0], ahead, amp, pert, extra[...], out)


def f32(*shape):
    return jax.ShapeDtypeStruct(shape, jnp.float32)


def call(kernel, outs, scratch, *args, scalars=0, flops=0, far=0, limit=16):
    in_specs = [pl.BlockSpec(memory_space=pltpu.SMEM)] * scalars
    in_specs += [pl.BlockSpec(memory_space=pltpu.VMEM)] * (len(args) - scalars - far)
    in_specs += [pl.BlockSpec(memory_space=pl.ANY)] * far
    moved = sum(math.prod(a.shape) * a.dtype.itemsize for a in args)
    return pl.pallas_call(
        kernel,
        out_shape=outs,
        in_specs=in_specs,
        out_specs=jax.tree.map(lambda _: pl.BlockSpec(memory_space=pltpu.VMEM), outs),
        scratch_shapes=scratch,
        compiler_params=pltpu.CompilerParams(vmem_limit_bytes=limit * 1024 * 1024),
        cost_estimate=pl.CostEstimate(flops=flops, bytes_accessed=moved, transcendentals=0),
    )(*args)


def ring_permute(value, distance):
    return lax.ppermute(value, "member", [(i, (i + distance) % RING) for i in range(RING)])


def sum_members(outs):
    across = ring_permute(outs[4], 4)
    right3, left3 = ring_permute(outs[3], 1), ring_permute(outs[5], -1)
    right1, left1 = ring_permute(outs[1], 1), ring_permute(outs[7], -1)
    right, left = lax.optimization_barrier((outs[2] + right3, outs[6] + left3))
    own = outs[0] + across + right1 + left1 + ring_permute(right, 2) + ring_permute(left, -2)
    mine = own[:CHUNK]
    across = ring_permute(mine, 4)
    right2, left2 = ring_permute(mine, 2), ring_permute(mine, -2)
    right1, left1 = ring_permute(mine, 1), ring_permute(mine, -1)
    right2, left2 = lax.optimization_barrier((right2, left2))
    right3, left3 = ring_permute(right2, 1), ring_permute(left2, -1)
    return [own, across, right2, left2, right1, left1, right3, left3]


def local(perturbations, innovations, error_weight, localization):
    const = {name: jnp.asarray(value) for name, value in bases().items()}
    me = lax.axis_index("member").astype(jnp.int32)[None]
    payload = f32(BANDS, 32, 128)
    vmem = lambda *shape: pltpu.VMEM(shape, jnp.float32)
    project_scratch = [vmem(480, NLON), vmem(512, ZW)]
    own = f32(VARS, LEV, ROWS, SHARE)
    modes = f32(LEV, MW, 128)
    field = f32(RING, CHUNK, 128)

    def exchange(value):
        return lax.all_to_all(value, "band", 0, 0)

    piece = f32(CHUNK + 8, 128)
    firsts = [piece] * 3 + [f32(480, NLON), f32(8, 128)]

    def add_up(out3, out4, out5, amp, extra):
        out1, out7, out2, out6, out0 = call(
            rest_kernel, [piece] * 5, [], me, amp, pert, extra, scalars=1, flops=400000000,
        )
        return sum_members([out0, out1, out2, out3, out4, out5, out6, out7])

    sent = call(
        first_kernel, payload,
        project_scratch + [
            pltpu.VMEM(perturbations.shape, jnp.bfloat16), vmem(*innovations.shape),
            vmem(*error_weight.shape), pltpu.VMEM(const["zonal_t"].shape, jnp.bfloat16),
            pltpu.SemaphoreType.DMA((9,)),
        ],
        me, perturbations, innovations, error_weight, const["zonal_t"],
        scalars=1, flops=1200000000, far=4, limit=59,
    )
    sent, gradient = call(
        gradient_kernel, [payload, modes], [],
        exchange(sent), localization, const["merid_t"], const["merid"], flops=200000000,
    )
    *outs, pert = call(
        fetch_kernel, firsts + [jax.ShapeDtypeStruct(perturbations.shape, jnp.bfloat16)],
        [vmem(512, ZW), pltpu.SemaphoreType.DMA(())],
        me, exchange(sent), const["zonal"], perturbations,
        scalars=1, flops=1200000000, far=1, limit=41,
    )
    parts = add_up(*outs)
    sent, first_field, first_own, scal = call(
        second_kernel, [payload, field, own, f32(8, 128)], project_scratch,
        me, pert, error_weight, const["zonal_t"], *parts, scalars=1, flops=1200000000,
    )
    sent, residual, step = call(
        residual_kernel, [payload, modes, f32(8, 128)], [],
        exchange(sent), localization, const["merid_t"], const["merid"], gradient, scal,
        flops=200000000,
    )
    parts = add_up(*call(
        synth_kernel, firsts, [vmem(512, ZW)],
        me, exchange(sent), const["zonal"], pert, scalars=1, flops=1200000000,
    ))
    sent, second_own, scal = call(
        third_kernel, [payload, own, f32(8, 128)], project_scratch + [vmem(RING, CHUNK, 128)],
        me, pert, error_weight, const["zonal_t"], scal, first_field, *parts,
        scalars=1, flops=1200000000,
    )
    return tuple(call(
        last_kernel,
        [f32(KLOC, LEV, ZW // BANDS, MW), f32(KLOC, LEV, ZW // BANDS, MW), own], [],
        exchange(sent), localization, const["merid_t"], gradient, residual, scal, step,
        first_own, second_own, flops=100000000,
    ))


def solution(mesh):
    return jax.shard_map(
        local,
        mesh=mesh,
        in_specs=(
            P("member", None, None, "band", None),
            P(None, None, "band", None),
            P(None, None, "band", None),
            P("band", None),
        ),
        out_specs=(
            P("member", None, "band", None),
            P("member", None, "band", None),
            P(None, None, "band", "member"),
        ),
        check_vma=False,
    )
```

```python
import functools
import math

import jax
import jax.numpy as jnp
import ml_dtypes
import numpy as np
from jax import lax
from jax.experimental import pallas as pl
from jax.experimental.pallas import tpu as pltpu
from jax.sharding import PartitionSpec as P

NLON = 1536
NLAT = 768
ZW = 256
MW = 128
VARS = 4
LEV = 2
KLOC = 10
BANDS = 32
RING = 8
ROWS = 24
TILES = 3
LTILES = NLON // 128
SHARE = NLON // RING
CHUNK = TILES * LTILES * 8
SLOTS = TILES * KLOC


def halves(array):
    high = array.astype(np.float32).astype(ml_dtypes.bfloat16)
    low = (array - high.astype(np.float64)).astype(np.float32).astype(ml_dtypes.bfloat16)
    return high, low


@functools.lru_cache(None)
def bases():
    wave = np.arange(ZW)
    number = (wave + 1) // 2
    angle = 2.0 * math.pi / NLON * ((number[:, None] * np.arange(NLON)[None, :]) % NLON)
    zonal = np.where((wave % 2 == 0)[:, None], np.cos(angle), np.sin(angle))
    zonal = zonal * (np.where(wave == 0, math.sqrt(0.5), 1.0) * math.sqrt(2.0 / NLON))[:, None]
    mode, row = np.arange(MW), np.arange(NLAT)
    angle = math.pi / (2.0 * NLAT) * ((mode[None, :] * (2 * row[:, None] + 1)) % (4 * NLAT))
    merid = np.cos(angle) * (np.where(mode == 0, math.sqrt(0.5), 1.0) * math.sqrt(2.0 / NLAT))
    parts = merid.reshape(BANDS, TILES, 8, MW).transpose(1, 0, 2, 3).reshape(TILES, BANDS * 8, MW)
    first = np.concatenate([parts[0], parts[1]], axis=1)
    second = np.concatenate([parts[1], parts[2]], axis=1)
    return {
        "zonal": np.stack(halves(zonal)),
        "zonal_t": np.stack(halves(zonal.T.copy())),
        "merid": np.stack([np.stack(halves(first)), np.stack(halves(second))]),
        "merid_t": np.stack([np.stack(halves(first.T.copy())), np.stack(halves(second.T.copy()))]),
    }


def split(value):
    high = value.astype(jnp.bfloat16)
    low = (value - high.astype(jnp.float32)).astype(jnp.bfloat16)
    return high, low


def dot(left, right):
    return jnp.dot(left, right, preferred_element_type=jnp.float32)


def swap_groups(vectors):
    group = lax.broadcasted_iota(jnp.int32, (8, 128), 1) // 8
    vectors = [pltpu.roll(v, 8 * i, 1) if i else v for i, v in enumerate(vectors)]
    for bit in (1, 2, 4, 8):
        move = (group & bit) != 0
        vectors = [jnp.where(move, vectors[(j + bit) % 16], vectors[j]) for j in range(16)]
    return [pltpu.roll(vectors[16 - g], 128 - 8 * g, 1) if g else vectors[0] for g in range(16)]


def total_of(value):
    return jnp.sum(jnp.sum(value, axis=1, keepdims=True), axis=0, keepdims=True)


def project_and_send(weights, pert, zonal_t, proj, coef, send, spare=None, ready=None):
    def zonal(first, rows):
        high, low = split(proj[pl.ds(first, rows), :])
        return dot(high, zonal_t[0]) + dot(low, zonal_t[0]) + dot(high, zonal_t[1])

    def keep(level, result):
        coef[pl.ds(level * 256, 240), :] = result
        coef[pl.ds(level * 256 + 240, 16), :] = jnp.zeros((16, ZW), jnp.float32)

    def project(level, members):
        for lt in range(LTILES):
            lanes = pl.ds(lt * 128, 128)
            fields = [
                jnp.concatenate([weights(v, level, rt, lt) for rt in range(TILES)], axis=0)
                for v in range(VARS)
            ]
            for k in members:
                acc = pert[k, 0, level, :, lanes].astype(jnp.float32) * fields[0]
                for v in range(1, VARS):
                    acc = acc + pert[k, v, level, :, lanes].astype(jnp.float32) * fields[v]
                for rt in range(TILES):
                    proj[pl.ds(level * 240 + (rt * KLOC + k) * 8, 8), lanes] = acc[
                        rt * 8 : rt * 8 + 8
                    ]

    def regroup(level):
        for tile in range(2):
            for half in range(2):
                got = swap_groups(
                    coef[pl.ds(level * 256 + (tile * 16 + i) * 8, 8), pl.ds(half * 128, 128)]
                    for i in range(16)
                )
                for g in range(16):
                    send[half * 16 + g, pl.ds(level * 16 + tile * 8, 8), :] = got[g]

    if ready:
        for level in range(LEV):
            ready("fields", level)
            for piece in range(2):
                ready("members", level, piece)
                project(level, range(piece * KLOC // 2, (piece + 1) * KLOC // 2))
            if level == 0:
                ready("basis")
            keep(level, zonal(level * 240, 240))
            regroup(level)
        return
    for level in range(LEV):
        project(level, range(KLOC))
    result = zonal(0, 480)
    for level in range(LEV):
        keep(level, result[level * 240 : level * 240 + 240])
    coef[pl.ds(240, 8), :] = jnp.broadcast_to(spare(), (8, ZW))
    for level in range(LEV):
        regroup(level)


def first_kernel(
    unused_me, unused_core, pert_in, innovations_in, weight_in, zonal_in, send,
    proj, coef, pert, innovations, weight, zonal_t, sems,
):
    copies = {}

    def begin(name, source, target):
        copies[name] = pltpu.make_async_copy(source, target, sems.at[len(copies)])
        copies[name].start()

    for level in range(LEV):
        begin(("innovations", level), innovations_in.at[:, level], innovations.at[:, level])
        begin(("weight", level), weight_in.at[:, level], weight.at[:, level])
        for piece in range(2):
            ks = pl.ds(piece * KLOC // 2, KLOC // 2)
            begin(("members", level, piece), pert_in.at[ks, :, level], pert.at[ks, :, level])
        if level == 0:
            begin(("basis",), zonal_in, zonal_t)

    def weights(v, level, rt, lt):
        at = (v, level, pl.ds(rt * 8, 8), pl.ds(lt * 128, 128))
        return weight[at] * innovations[at]

    def ready(*name):
        if name[0] == "fields":
            copies["innovations", name[1]].wait()
            copies["weight", name[1]].wait()
        else:
            copies[name].wait()

    project_and_send(weights, pert, zonal_t, proj, coef, send, ready=ready)


def arrived(me, parts):
    for j, part in zip((0, 4, 2, 6, 1, 7, 3, 5), parts):
        yield lax.rem(me + (RING - j), RING), part[pl.ds(0, CHUNK), :]


def assemble(me, parts, field):
    for c, value in arrived(me, parts):
        field[c] = value


def own_columns(me, field, out):
    start = (3 * me) // 2
    odd = lax.rem(me, 2) == 1
    for c in range(RING):
        for rt in range(TILES):
            at = pl.multiple_of((rt * LTILES + start) * 8, 8)
            window = jnp.concatenate(
                [field[c, pl.ds(at, 8), :], field[c, pl.ds(at + 8, 8), :]], axis=1
            )
            window = jnp.where(odd, pltpu.roll(window, 192, 1), window)
            out[c // LEV, c % LEV, pl.ds(rt * 8, 8), :] = window[:, :SHARE]


def weigh(weight, field):
    energy = [jnp.zeros((8, 128), jnp.float32)]

    def weights(v, level, rt, lt):
        value = field[v * LEV + level, pl.ds((rt * LTILES + lt) * 8, 8), :]
        weighted = weight[v, level, pl.ds(rt * 8, 8), pl.ds(lt * 128, 128)] * value
        energy[0] = energy[0] + weighted * value
        return weighted

    return weights, lambda: total_of(energy[0])


def second_kernel(me_ref, pert, weight, zonal_t, *refs):
    parts, (send, field, own, scal, proj, coef) = refs[:RING], refs[RING:]
    me = me_ref[0]
    assemble(me, parts, field)
    own_columns(me, field, own)
    scal[...] = parts[0][pl.ds(CHUNK, 8), :]
    weights, energy = weigh(weight, field)
    project_and_send(weights, pert, zonal_t, proj, coef, send, spare=energy)


def third_kernel(me_ref, pert, weight, zonal_t, old_scal, old_field, *refs):
    parts, (send, own, scal, proj, coef, field) = refs[:RING], refs[RING:]
    me = me_ref[0]
    norm = old_scal[0:1, 0:1]
    norm_next = parts[0][CHUNK : CHUNK + 1, 0:1]
    cross = parts[0][CHUNK + 1 : CHUNK + 2, 0:1]
    beta = norm_next / norm
    for c, value in arrived(me, parts):
        field[c] = value + beta * old_field[c]
    own_columns(me, field, own)
    square = norm_next + 2.0 * beta * cross + beta * beta * norm
    row = lax.broadcasted_iota(jnp.int32, (8, 128), 0)
    scal[...] = jnp.where(row == 0, norm_next, jnp.where(row == 1, square, beta))
    weights, energy = weigh(weight, field)
    project_and_send(weights, pert, zonal_t, proj, coef, send, spare=energy)


def to_modes(received, level, merid_t):
    lane = lax.broadcasted_iota(jnp.int32, (MW, 128), 1)
    sums = []
    for tile in range(2):
        data = received[:, pl.ds(level * 16 + tile * 8, 8), :].reshape(BANDS * 8, 128)
        high, low = split(data)
        sums.append(
            dot(merid_t[tile, 0], high) + dot(merid_t[tile, 0], low) + dot(merid_t[tile, 1], high)
        )
    result = sums[0][:MW] + jnp.where(lane < 48, pltpu.roll(sums[0][MW:], 48, 1), 0.0)
    result = result + jnp.where(lane >= 48, pltpu.roll(sums[1][:MW], 48, 1), 0.0)
    result = result + pltpu.roll(sums[1][MW:], 96, 1)
    return jnp.where(lane < 80, result, 0.0)


def to_rows(value, merid, level, send, spares):
    lane = lax.broadcasted_iota(jnp.int32, (MW, 128), 1)
    moved = pltpu.roll(value, 80, 1)
    second = jnp.where(lane >= 80, moved, 0.0)
    third = jnp.where(lane < 32, moved, 0.0)
    fourth = pltpu.roll(value, 32, 1)
    for tile, pair in enumerate(((value, second), (third, fourth))):
        high, low = split(jnp.concatenate(pair, axis=0))
        rows = dot(merid[tile, 0], high) + dot(merid[tile, 0], low) + dot(merid[tile, 1], high)
        if tile == 1 and spares:
            row = lax.broadcasted_iota(jnp.int32, (BANDS * 8, 128), 0)
            column = lax.broadcasted_iota(jnp.int32, (BANDS * 8, 128), 1)
            top = (row % 8) == 0
            for position, spare in enumerate(spares):
                rows = rows + jnp.where(top & (column == 112 + 8 * position), spare, 0.0)
        send[:, pl.ds(level * 16 + tile * 8, 8), :] = rows.reshape(BANDS, 8, 128)


def spare_sum(received):
    data = received[:, pl.ds(8, 8), :].reshape(BANDS * 8, 128)
    row = lax.broadcasted_iota(jnp.int32, (BANDS * 8, 128), 0)
    column = lax.broadcasted_iota(jnp.int32, (BANDS * 8, 128), 1)
    return total_of(jnp.where(((row % 8) == 0) & (column == 112), data, 0.0))


def scale_of(localization):
    return jnp.concatenate([localization[...]] * 16, axis=0).T


def gradient_kernel(received, localization, merid_t, merid, send, gradient):
    scale = scale_of(localization)
    acc = jnp.zeros((MW, 128), jnp.float32)
    for level in range(LEV):
        value = to_modes(received, level, merid_t) * scale
        gradient[level] = value
        acc = acc + value * value
    norm = total_of(acc)
    for level in range(LEV):
        to_rows(gradient[level] * scale, merid, level, send, (norm,) if level == 0 else ())


def residual_kernel(received, localization, merid_t, merid, gradient, scal, send, residual, step_out):
    scale = scale_of(localization)
    norm = scal[0:1, 0:1]
    step = norm / (norm + spare_sum(received))
    step_out[...] = jnp.broadcast_to(step, (8, 128))
    squares = jnp.zeros((MW, 128), jnp.float32)
    cross = jnp.zeros((MW, 128), jnp.float32)
    for level in range(LEV):
        old = gradient[level]
        image = old + to_modes(received, level, merid_t) * scale
        value = old - step * image
        residual[level] = value
        squares = squares + value * value
        cross = cross + value * old
    spares = (total_of(squares), total_of(cross))
    for level in range(LEV):
        to_rows(residual[level] * scale, merid, level, send, spares if level == 0 else ())


def last_kernel(
    received, localization, merid_t, gradient, residual, scal, step_in, first_own, second_own,
    control_out, residual_out, increment_out,
):
    scale = scale_of(localization)
    norm_next, square, beta = scal[0:1, 0:1], scal[1:2, 0:1], scal[2:3, 0:1]
    first_step = step_in[0:1, 0:1]
    step = norm_next / (square + spare_sum(received))
    for level in range(LEV):
        old, res = gradient[level], residual[level]
        direction = res + beta * old
        image = direction + to_modes(received, level, merid_t) * scale
        for out, value in (
            (control_out, first_step * old + step * direction),
            (residual_out, res - step * image),
        ):
            turned = value.T
            for k in range(KLOC):
                out[k, level] = turned[k * 8 : k * 8 + 8]
    increment_out[...] = first_step[None, None] * first_own[...] + step[None, None] * second_own[...]


def chunk_of(me, ahead, amp, pert, extra, out):
    c = lax.rem(me + ahead, RING)
    variable, level = c // LEV, lax.rem(c, LEV)
    for lt in range(LTILES):
        lanes = pl.ds(lt * 128, 128)
        acc = jnp.zeros((ROWS, 128), jnp.float32)
        for k in range(KLOC):
            field = jnp.concatenate(
                [
                    amp[pl.ds(pl.multiple_of(level * 240 + (rt * KLOC + k) * 8, 8), 8), lanes]
                    for rt in range(TILES)
                ],
                axis=0,
            )
            acc = acc + pert[k, variable, level, :, lanes].astype(jnp.float32) * field
        for rt in range(TILES):
            out[pl.ds((rt * LTILES + lt) * 8, 8), :] = acc[rt * 8 : rt * 8 + 8]
    out[pl.ds(CHUNK, 8), :] = extra


def tell_side(core_ref, side):
    even = core_ref[0] == 0
    side[...] = jnp.broadcast_to(jnp.where(even, 1.0, 0.0).astype(jnp.float32), (8, 128))


def synth_kernel(
    me_ref, core_ref, received, zonal, pert, out3, out4, out5, amp, extra, side, coef
):
    tell_side(core_ref, side)
    synthesize_first(me_ref[0], received, zonal, pert, out3, out4, out5, amp, extra, coef)


def fetch_kernel(
    me_ref, core_ref, received, zonal, pert_in,
    out3, out4, out5, amp, extra, side, pert, coef, sem,
):
    tell_side(core_ref, side)
    copy = pltpu.make_async_copy(pert_in, pert, sem)
    copy.start()
    synthesize_first(
        me_ref[0], received, zonal, pert, out3, out4, out5, amp, extra, coef, copy.wait
    )


def synthesize_first(
    me, received, zonal, pert, out3, out4, out5, amp, extra, coef, ready=lambda: None
):
    for level in range(LEV):
        for tile in range(2):
            for half in range(2):
                got = swap_groups(
                    received[half * 16 + g, pl.ds(level * 16 + tile * 8, 8), :] for g in range(16)
                )
                for i in range(16):
                    at = level * 256 + (tile * 16 + i) * 8
                    coef[pl.ds(at, 8), pl.ds(half * 128, 128)] = got[i]
    scalars = [total_of(coef[pl.ds(240 + 8 * i, 8), :]) for i in range(2)]
    high, low = split(jnp.concatenate([coef[pl.ds(0, 240), :], coef[pl.ds(256, 240), :]], axis=0))
    for part in range(LTILES // 2):
        wide = pl.ds(part * 256, 256)
        amp[:, wide] = (
            dot(high, zonal[0, :, wide]) + dot(low, zonal[0, :, wide]) + dot(high, zonal[1, :, wide])
        )
    row = lax.broadcasted_iota(jnp.int32, (8, 128), 0)
    extra[...] = jnp.where(row == 0, scalars[0], jnp.where(row == 1, scalars[1], 0.0))
    ready()
    for ahead, out in ((4, out4), (3, out3), (5, out5)):
        chunk_of(me, ahead, amp, pert, extra[...], out)


def rest_kernel(me_ref, amp, pert, extra, out1, out7, out2, out6, out0):
    for ahead, out in ((1, out1), (7, out7), (2, out2), (6, out6), (0, out0)):
        chunk_of(me_ref[0], ahead, amp, pert, extra[...], out)


def f32(*shape):
    return jax.ShapeDtypeStruct(shape, jnp.float32)


def call(kernel, outs, scratch, *args, scalars=0, flops=0, far=0, limit=16):
    in_specs = [pl.BlockSpec(memory_space=pltpu.SMEM)] * scalars
    in_specs += [pl.BlockSpec(memory_space=pltpu.VMEM)] * (len(args) - scalars - far)
    in_specs += [pl.BlockSpec(memory_space=pl.ANY)] * far
    moved = sum(math.prod(a.shape) * a.dtype.itemsize for a in args)
    return pl.pallas_call(
        kernel,
        out_shape=outs,
        in_specs=in_specs,
        out_specs=jax.tree.map(lambda _: pl.BlockSpec(memory_space=pltpu.VMEM), outs),
        scratch_shapes=scratch,
        compiler_params=pltpu.CompilerParams(vmem_limit_bytes=limit * 1024 * 1024),
        cost_estimate=pl.CostEstimate(flops=flops, bytes_accessed=moved, transcendentals=0),
    )(*args)


def ring_permute(value, distance):
    return lax.ppermute(value, "member", [(i, (i + distance) % RING) for i in range(RING)])


def cross_permute(value, distance):
    pairs = [
        (m * BANDS + b, (m + (distance if b % 2 == 0 else RING - distance)) % RING * BANDS + b)
        for m in range(RING)
        for b in range(BANDS)
    ]
    return lax.ppermute(value, ("member", "band"), pairs)


def sum_members(outs, side):
    rightwards = side[:1] > 0.0
    right3, left3 = ring_permute(outs[3], 1), ring_permute(outs[5], -1)
    leg = cross_permute(outs[4], 2)
    right, left, near, behind = lax.optimization_barrier((
        outs[2] + right3 + jnp.where(rightwards, leg, 0.0),
        outs[6] + left3 + jnp.where(rightwards, 0.0, leg),
        outs[1], outs[7],
    ))
    own = outs[0] + ring_permute(right, 2) + ring_permute(left, -2)
    own = own + ring_permute(near, 1) + ring_permute(behind, -1)
    mine = own[:CHUNK]
    right2, left2 = ring_permute(mine, 2), ring_permute(mine, -2)
    right1, left1 = ring_permute(mine, 1), ring_permute(mine, -1)
    right2, left2 = lax.optimization_barrier((right2, left2))
    across = cross_permute(jnp.where(rightwards, right2, left2), 2)
    right3, left3 = ring_permute(right2, 1), ring_permute(left2, -1)
    return [own, across, right2, left2, right1, left1, right3, left3]


def local(perturbations, innovations, error_weight, localization):
    const = {name: jnp.asarray(value) for name, value in bases().items()}
    me = lax.axis_index("member").astype(jnp.int32)[None]
    core = (lax.axis_index("band") % 2).astype(jnp.int32)[None]
    payload = f32(BANDS, 32, 128)
    vmem = lambda *shape: pltpu.VMEM(shape, jnp.float32)
    project_scratch = [vmem(480, NLON), vmem(512, ZW)]
    own = f32(VARS, LEV, ROWS, SHARE)
    modes = f32(LEV, MW, 128)
    field = f32(RING, CHUNK, 128)

    def exchange(value):
        return lax.all_to_all(value, "band", 0, 0)

    piece = f32(CHUNK + 8, 128)
    firsts = [piece] * 3 + [f32(480, NLON), f32(8, 128), f32(8, 128)]

    def add_up(out3, out4, out5, amp, extra, side):
        out1, out7, out2, out6, out0 = call(
            rest_kernel, [piece] * 5, [], me, amp, pert, extra, scalars=1, flops=400000000,
        )
        return sum_members([out0, out1, out2, out3, out4, out5, out6, out7], side)

    sent = call(
        first_kernel, payload,
        project_scratch + [
            pltpu.VMEM(perturbations.shape, jnp.bfloat16), vmem(*innovations.shape),
            vmem(*error_weight.shape), pltpu.VMEM(const["zonal_t"].shape, jnp.bfloat16),
            pltpu.SemaphoreType.DMA((9,)),
        ],
        me, core, perturbations, innovations, error_weight, const["zonal_t"],
        scalars=2, flops=1200000000, far=4, limit=59,
    )
    sent, gradient = call(
        gradient_kernel, [payload, modes], [],
        exchange(sent), localization, const["merid_t"], const["merid"], flops=200000000,
    )
    *outs, pert = call(
        fetch_kernel, firsts + [jax.ShapeDtypeStruct(perturbations.shape, jnp.bfloat16)],
        [vmem(512, ZW), pltpu.SemaphoreType.DMA(())],
        me, core, exchange(sent), const["zonal"], perturbations,
        scalars=2, flops=1200000000, far=1, limit=41,
    )
    parts = add_up(*outs)
    sent, first_field, first_own, scal = call(
        second_kernel, [payload, field, own, f32(8, 128)], project_scratch,
        me, pert, error_weight, const["zonal_t"], *parts, scalars=1, flops=1200000000,
    )
    sent, residual, step = call(
        residual_kernel, [payload, modes, f32(8, 128)], [],
        exchange(sent), localization, const["merid_t"], const["merid"], gradient, scal,
        flops=200000000,
    )
    parts = add_up(*call(
        synth_kernel, firsts, [vmem(512, ZW)],
        me, core, exchange(sent), const["zonal"], pert, scalars=2, flops=1200000000,
    ))
    sent, second_own, scal = call(
        third_kernel, [payload, own, f32(8, 128)], project_scratch + [vmem(RING, CHUNK, 128)],
        me, pert, error_weight, const["zonal_t"], scal, first_field, *parts,
        scalars=1, flops=1200000000,
    )
    return tuple(call(
        last_kernel,
        [f32(KLOC, LEV, ZW // BANDS, MW), f32(KLOC, LEV, ZW // BANDS, MW), own], [],
        exchange(sent), localization, const["merid_t"], gradient, residual, scal, step,
        first_own, second_own, flops=100000000,
    ))


def solution(mesh):
    return jax.shard_map(
        local,
        mesh=mesh,
        in_specs=(
            P("member", None, None, "band", None),
            P(None, None, "band", None),
            P(None, None, "band", None),
            P("band", None),
        ),
        out_specs=(
            P("member", None, "band", None),
            P("member", None, "band", None),
            P(None, None, "band", "member"),
        ),
        check_vma=False,
    )
```

```python
import functools
import math

import jax
import jax.numpy as jnp
import ml_dtypes
import numpy as np
from jax import lax
from jax.experimental import pallas as pl
from jax.experimental.pallas import tpu as pltpu
from jax.sharding import PartitionSpec as P

NLON = 1536
NLAT = 768
ZW = 256
MW = 128
VARS = 4
LEV = 2
KLOC = 10
BANDS = 32
RING = 8
ROWS = 24
TILES = 3
LTILES = NLON // 128
SHARE = NLON // RING
CHUNK = TILES * LTILES * 8
SLOTS = TILES * KLOC


def halves(array):
    high = array.astype(np.float32).astype(ml_dtypes.bfloat16)
    low = (array - high.astype(np.float64)).astype(np.float32).astype(ml_dtypes.bfloat16)
    return high, low


@functools.lru_cache(None)
def bases():
    wave = np.arange(ZW)
    number = (wave + 1) // 2
    angle = 2.0 * math.pi / NLON * ((number[:, None] * np.arange(NLON)[None, :]) % NLON)
    zonal = np.where((wave % 2 == 0)[:, None], np.cos(angle), np.sin(angle))
    zonal = zonal * (np.where(wave == 0, math.sqrt(0.5), 1.0) * math.sqrt(2.0 / NLON))[:, None]
    mode, row = np.arange(MW), np.arange(NLAT)
    angle = math.pi / (2.0 * NLAT) * ((mode[None, :] * (2 * row[:, None] + 1)) % (4 * NLAT))
    merid = np.cos(angle) * (np.where(mode == 0, math.sqrt(0.5), 1.0) * math.sqrt(2.0 / NLAT))
    parts = merid.reshape(BANDS, TILES, 8, MW).transpose(1, 0, 2, 3).reshape(TILES, BANDS * 8, MW)
    first = np.concatenate([parts[0], parts[1]], axis=1)
    second = np.concatenate([parts[1], parts[2]], axis=1)
    return {
        "zonal": np.stack(halves(zonal)),
        "zonal_t": np.stack(halves(zonal.T.copy())),
        "merid": np.stack([np.stack(halves(first)), np.stack(halves(second))]),
        "merid_t": np.stack([np.stack(halves(first.T.copy())), np.stack(halves(second.T.copy()))]),
    }


def split(value):
    high = value.astype(jnp.bfloat16)
    low = (value - high.astype(jnp.float32)).astype(jnp.bfloat16)
    return high, low


def dot(left, right):
    return jnp.dot(left, right, preferred_element_type=jnp.float32)


def swap_groups(vectors):
    group = lax.broadcasted_iota(jnp.int32, (8, 128), 1) // 8
    vectors = [pltpu.roll(v, 8 * i, 1) if i else v for i, v in enumerate(vectors)]
    for bit in (1, 2, 4, 8):
        move = (group & bit) != 0
        vectors = [jnp.where(move, vectors[(j + bit) % 16], vectors[j]) for j in range(16)]
    return [pltpu.roll(vectors[16 - g], 128 - 8 * g, 1) if g else vectors[0] for g in range(16)]


def total_of(value):
    return jnp.sum(jnp.sum(value, axis=1, keepdims=True), axis=0, keepdims=True)


def project_and_send(weights, pert, zonal_t, proj, coef, send, spare=None, ready=None):
    def zonal(first, rows):
        high, low = split(proj[pl.ds(first, rows), :])
        return dot(high, zonal_t[0]) + dot(low, zonal_t[0]) + dot(high, zonal_t[1])

    def keep(level, result):
        coef[pl.ds(level * 256, 240), :] = result
        coef[pl.ds(level * 256 + 240, 16), :] = jnp.zeros((16, ZW), jnp.float32)

    def project(level, members):
        for lt in range(LTILES):
            lanes = pl.ds(lt * 128, 128)
            fields = [
                jnp.concatenate([weights(v, level, rt, lt) for rt in range(TILES)], axis=0)
                for v in range(VARS)
            ]
            for k in members:
                acc = pert[k, 0, level, :, lanes].astype(jnp.float32) * fields[0]
                for v in range(1, VARS):
                    acc = acc + pert[k, v, level, :, lanes].astype(jnp.float32) * fields[v]
                for rt in range(TILES):
                    proj[pl.ds(level * 240 + (rt * KLOC + k) * 8, 8), lanes] = acc[
                        rt * 8 : rt * 8 + 8
                    ]

    def regroup(level):
        for tile in range(2):
            for half in range(2):
                got = swap_groups(
                    coef[pl.ds(level * 256 + (tile * 16 + i) * 8, 8), pl.ds(half * 128, 128)]
                    for i in range(16)
                )
                for g in range(16):
                    send[half * 16 + g, pl.ds(level * 16 + tile * 8, 8), :] = got[g]

    if ready:
        for level in range(LEV):
            ready("fields", level)
            for piece in range(2):
                ready("members", level, piece)
                project(level, range(piece * KLOC // 2, (piece + 1) * KLOC // 2))
            if level == 0:
                ready("basis")
            keep(level, zonal(level * 240, 240))
            regroup(level)
        return
    for level in range(LEV):
        project(level, range(KLOC))
    result = zonal(0, 480)
    for level in range(LEV):
        keep(level, result[level * 240 : level * 240 + 240])
    coef[pl.ds(240, 8), :] = jnp.broadcast_to(spare(), (8, ZW))
    for level in range(LEV):
        regroup(level)


def first_kernel(
    unused_me, unused_core, pert_in, innovations_in, weight_in, zonal_in, send,
    proj, coef, pert, innovations, weight, zonal_t, sems,
):
    copies = {}

    def begin(name, source, target):
        copies[name] = pltpu.make_async_copy(source, target, sems.at[len(copies)])
        copies[name].start()

    for level in range(LEV):
        begin(("innovations", level), innovations_in.at[:, level], innovations.at[:, level])
        begin(("weight", level), weight_in.at[:, level], weight.at[:, level])
        for piece in range(2):
            ks = pl.ds(piece * KLOC // 2, KLOC // 2)
            begin(("members", level, piece), pert_in.at[ks, :, level], pert.at[ks, :, level])
        if level == 0:
            begin(("basis",), zonal_in, zonal_t)

    def weights(v, level, rt, lt):
        at = (v, level, pl.ds(rt * 8, 8), pl.ds(lt * 128, 128))
        return weight[at] * innovations[at]

    def ready(*name):
        if name[0] == "fields":
            copies["innovations", name[1]].wait()
            copies["weight", name[1]].wait()
        else:
            copies[name].wait()

    project_and_send(weights, pert, zonal_t, proj, coef, send, ready=ready)


def arrived(me, parts):
    for j, part in zip((0, 4, 2, 6, 1, 7, 3, 5), parts):
        yield lax.rem(me + (RING - j), RING), part[pl.ds(0, CHUNK), :]


def assemble(me, parts, field):
    for c, value in arrived(me, parts):
        field[c] = value


def own_columns(me, field, out):
    start = (3 * me) // 2
    odd = lax.rem(me, 2) == 1
    for c in range(RING):
        for rt in range(TILES):
            at = pl.multiple_of((rt * LTILES + start) * 8, 8)
            window = jnp.concatenate(
                [field[c, pl.ds(at, 8), :], field[c, pl.ds(at + 8, 8), :]], axis=1
            )
            window = jnp.where(odd, pltpu.roll(window, 192, 1), window)
            out[c // LEV, c % LEV, pl.ds(rt * 8, 8), :] = window[:, :SHARE]


def weigh(weight, field):
    energy = [jnp.zeros((8, 128), jnp.float32)]

    def weights(v, level, rt, lt):
        value = field[v * LEV + level, pl.ds((rt * LTILES + lt) * 8, 8), :]
        weighted = weight[v, level, pl.ds(rt * 8, 8), pl.ds(lt * 128, 128)] * value
        energy[0] = energy[0] + weighted * value
        return weighted

    return weights, lambda: total_of(energy[0])


def second_kernel(me_ref, pert, weight, zonal_t, *refs):
    parts, (send, field, own, scal, proj, coef) = refs[:RING], refs[RING:]
    me = me_ref[0]
    assemble(me, parts, field)
    own_columns(me, field, own)
    scal[...] = parts[0][pl.ds(CHUNK, 8), :]
    weights, energy = weigh(weight, field)
    project_and_send(weights, pert, zonal_t, proj, coef, send, spare=energy)


def third_kernel(me_ref, pert, weight, zonal_t, old_scal, old_field, *refs):
    parts, (send, own, scal, proj, coef, field) = refs[:RING], refs[RING:]
    me = me_ref[0]
    norm = old_scal[0:1, 0:1]
    norm_next = parts[0][CHUNK : CHUNK + 1, 0:1]
    cross = parts[0][CHUNK + 1 : CHUNK + 2, 0:1]
    beta = norm_next / norm
    for c, value in arrived(me, parts):
        field[c] = value + beta * old_field[c]
    own_columns(me, field, own)
    square = norm_next + 2.0 * beta * cross + beta * beta * norm
    row = lax.broadcasted_iota(jnp.int32, (8, 128), 0)
    scal[...] = jnp.where(row == 0, norm_next, jnp.where(row == 1, square, beta))
    weights, energy = weigh(weight, field)
    project_and_send(weights, pert, zonal_t, proj, coef, send, spare=energy)


def to_modes(received, level, merid_t):
    lane = lax.broadcasted_iota(jnp.int32, (MW, 128), 1)
    sums = []
    for tile in range(2):
        data = received[:, pl.ds(level * 16 + tile * 8, 8), :].reshape(BANDS * 8, 128)
        high, low = split(data)
        sums.append(
            dot(merid_t[tile, 0], high) + dot(merid_t[tile, 0], low) + dot(merid_t[tile, 1], high)
        )
    result = sums[0][:MW] + jnp.where(lane < 48, pltpu.roll(sums[0][MW:], 48, 1), 0.0)
    result = result + jnp.where(lane >= 48, pltpu.roll(sums[1][:MW], 48, 1), 0.0)
    result = result + pltpu.roll(sums[1][MW:], 96, 1)
    return jnp.where(lane < 80, result, 0.0)


def to_rows(value, merid, level, send, spares):
    lane = lax.broadcasted_iota(jnp.int32, (MW, 128), 1)
    moved = pltpu.roll(value, 80, 1)
    second = jnp.where(lane >= 80, moved, 0.0)
    third = jnp.where(lane < 32, moved, 0.0)
    fourth = pltpu.roll(value, 32, 1)
    for tile, pair in enumerate(((value, second), (third, fourth))):
        high, low = split(jnp.concatenate(pair, axis=0))
        rows = dot(merid[tile, 0], high) + dot(merid[tile, 0], low) + dot(merid[tile, 1], high)
        if tile == 1 and spares:
            row = lax.broadcasted_iota(jnp.int32, (BANDS * 8, 128), 0)
            column = lax.broadcasted_iota(jnp.int32, (BANDS * 8, 128), 1)
            top = (row % 8) == 0
            for position, spare in enumerate(spares):
                rows = rows + jnp.where(top & (column == 112 + 8 * position), spare, 0.0)
        send[:, pl.ds(level * 16 + tile * 8, 8), :] = rows.reshape(BANDS, 8, 128)


def spare_sum(received):
    data = received[:, pl.ds(8, 8), :].reshape(BANDS * 8, 128)
    row = lax.broadcasted_iota(jnp.int32, (BANDS * 8, 128), 0)
    column = lax.broadcasted_iota(jnp.int32, (BANDS * 8, 128), 1)
    return total_of(jnp.where(((row % 8) == 0) & (column == 112), data, 0.0))


def scale_of(localization):
    return jnp.concatenate([localization[...]] * 16, axis=0).T


def gradient_kernel(received, localization, merid_t, merid, send, gradient):
    scale = scale_of(localization)
    acc = jnp.zeros((MW, 128), jnp.float32)
    for level in range(LEV):
        value = to_modes(received, level, merid_t) * scale
        gradient[level] = value
        acc = acc + value * value
    norm = total_of(acc)
    for level in range(LEV):
        to_rows(gradient[level] * scale, merid, level, send, (norm,) if level == 0 else ())


def residual_kernel(received, localization, merid_t, merid, gradient, scal, send, residual, step_out):
    scale = scale_of(localization)
    norm = scal[0:1, 0:1]
    step = norm / (norm + spare_sum(received))
    step_out[...] = jnp.broadcast_to(step, (8, 128))
    squares = jnp.zeros((MW, 128), jnp.float32)
    cross = jnp.zeros((MW, 128), jnp.float32)
    for level in range(LEV):
        old = gradient[level]
        image = old + to_modes(received, level, merid_t) * scale
        value = old - step * image
        residual[level] = value
        squares = squares + value * value
        cross = cross + value * old
    spares = (total_of(squares), total_of(cross))
    for level in range(LEV):
        to_rows(residual[level] * scale, merid, level, send, spares if level == 0 else ())


def last_kernel(
    received, localization, merid_t, gradient, residual, scal, step_in, first_own, second_own,
    control_out, residual_out, increment_out,
):
    scale = scale_of(localization)
    norm_next, square, beta = scal[0:1, 0:1], scal[1:2, 0:1], scal[2:3, 0:1]
    first_step = step_in[0:1, 0:1]
    step = norm_next / (square + spare_sum(received))
    for level in range(LEV):
        old, res = gradient[level], residual[level]
        direction = res + beta * old
        image = direction + to_modes(received, level, merid_t) * scale
        for out, value in (
            (control_out, first_step * old + step * direction),
            (residual_out, res - step * image),
        ):
            turned = value.T
            for k in range(KLOC):
                out[k, level] = turned[k * 8 : k * 8 + 8]
    increment_out[...] = first_step[None, None] * first_own[...] + step[None, None] * second_own[...]


def chunk_of(me, ahead, amp, pert, extra, out):
    c = lax.rem(me + ahead, RING)
    variable, level = c // LEV, lax.rem(c, LEV)
    for lt in range(LTILES):
        lanes = pl.ds(lt * 128, 128)
        acc = jnp.zeros((ROWS, 128), jnp.float32)
        for k in range(KLOC):
            field = jnp.concatenate(
                [
                    amp[pl.ds(pl.multiple_of(level * 240 + (rt * KLOC + k) * 8, 8), 8), lanes]
                    for rt in range(TILES)
                ],
                axis=0,
            )
            acc = acc + pert[k, variable, level, :, lanes].astype(jnp.float32) * field
        for rt in range(TILES):
            out[pl.ds((rt * LTILES + lt) * 8, 8), :] = acc[rt * 8 : rt * 8 + 8]
    out[pl.ds(CHUNK, 8), :] = extra


def tell_side(core_ref, side):
    even = core_ref[0] == 0
    side[...] = jnp.broadcast_to(jnp.where(even, 1.0, 0.0).astype(jnp.float32), (8, 128))


def synth_kernel(
    me_ref, core_ref, received, zonal, pert, out3, out4, out5, amp, extra, side, coef
):
    tell_side(core_ref, side)
    synthesize_first(me_ref[0], received, zonal, pert, out3, out4, out5, amp, extra, coef)


def fetch_kernel(
    me_ref, core_ref, received, zonal, pert_in,
    out3, out4, out5, amp, extra, side, pert, coef, sems,
):
    tell_side(core_ref, side)
    copies = {}
    for at, ahead in enumerate((4, 3, 5, 1, 7, 2, 6, 0)):
        c = lax.rem(me_ref[0] + ahead, RING)
        part = (slice(None), c // LEV, lax.rem(c, LEV))
        copies[ahead] = pltpu.make_async_copy(pert_in.at[part], pert.at[part], sems.at[at])
        copies[ahead].start()
    synthesize_first(
        me_ref[0], received, zonal, pert, out3, out4, out5, amp, extra, coef,
        lambda ahead: copies[ahead].wait(),
    )
    for ahead in (1, 7, 2, 6, 0):
        copies[ahead].wait()


def synthesize_first(
    me, received, zonal, pert, out3, out4, out5, amp, extra, coef, ready=lambda ahead: None
):
    for level in range(LEV):
        for tile in range(2):
            for half in range(2):
                got = swap_groups(
                    received[half * 16 + g, pl.ds(level * 16 + tile * 8, 8), :] for g in range(16)
                )
                for i in range(16):
                    at = level * 256 + (tile * 16 + i) * 8
                    coef[pl.ds(at, 8), pl.ds(half * 128, 128)] = got[i]
    scalars = [total_of(coef[pl.ds(240 + 8 * i, 8), :]) for i in range(2)]
    high, low = split(jnp.concatenate([coef[pl.ds(0, 240), :], coef[pl.ds(256, 240), :]], axis=0))
    for part in range(LTILES // 2):
        wide = pl.ds(part * 256, 256)
        amp[:, wide] = (
            dot(high, zonal[0, :, wide]) + dot(low, zonal[0, :, wide]) + dot(high, zonal[1, :, wide])
        )
    row = lax.broadcasted_iota(jnp.int32, (8, 128), 0)
    extra[...] = jnp.where(row == 0, scalars[0], jnp.where(row == 1, scalars[1], 0.0))
    for ahead, out in ((4, out4), (3, out3), (5, out5)):
        ready(ahead)
        chunk_of(me, ahead, amp, pert, extra[...], out)


def rest_kernel(me_ref, amp, pert, extra, out1, out7, out2, out6, out0):
    for ahead, out in ((1, out1), (7, out7), (2, out2), (6, out6), (0, out0)):
        chunk_of(me_ref[0], ahead, amp, pert, extra[...], out)


def f32(*shape):
    return jax.ShapeDtypeStruct(shape, jnp.float32)


def call(kernel, outs, scratch, *args, scalars=0, flops=0, far=0, limit=16):
    in_specs = [pl.BlockSpec(memory_space=pltpu.SMEM)] * scalars
    in_specs += [pl.BlockSpec(memory_space=pltpu.VMEM)] * (len(args) - scalars - far)
    in_specs += [pl.BlockSpec(memory_space=pl.ANY)] * far
    moved = sum(math.prod(a.shape) * a.dtype.itemsize for a in args)
    return pl.pallas_call(
        kernel,
        out_shape=outs,
        in_specs=in_specs,
        out_specs=jax.tree.map(lambda _: pl.BlockSpec(memory_space=pltpu.VMEM), outs),
        scratch_shapes=scratch,
        compiler_params=pltpu.CompilerParams(vmem_limit_bytes=limit * 1024 * 1024),
        cost_estimate=pl.CostEstimate(flops=flops, bytes_accessed=moved, transcendentals=0),
    )(*args)


def ring_permute(value, distance):
    return lax.ppermute(value, "member", [(i, (i + distance) % RING) for i in range(RING)])


def cross_permute(value, distance):
    pairs = [
        (m * BANDS + b, (m + (distance if b % 2 == 0 else RING - distance)) % RING * BANDS + b)
        for m in range(RING)
        for b in range(BANDS)
    ]
    return lax.ppermute(value, ("member", "band"), pairs)


def sum_members(outs, side):
    rightwards = side[:1] > 0.0
    right3, left3 = ring_permute(outs[3], 1), ring_permute(outs[5], -1)
    leg = cross_permute(outs[4], 2)
    right3, near, behind = lax.optimization_barrier((right3, outs[1], outs[7]))
    right1, left1 = ring_permute(near, 1), ring_permute(behind, -1)
    right, left = lax.optimization_barrier((
        outs[2] + right3 + jnp.where(rightwards, leg, 0.0),
        outs[6] + left3 + jnp.where(rightwards, 0.0, leg),
    ))
    own = outs[0] + right1 + left1 + ring_permute(right, 2) + ring_permute(left, -2)
    mine = own[:CHUNK]
    right2, left2 = ring_permute(mine, 2), ring_permute(mine, -2)
    right1, left1 = ring_permute(mine, 1), ring_permute(mine, -1)
    right2, left2 = lax.optimization_barrier((right2, left2))
    across = cross_permute(jnp.where(rightwards, right2, left2), 2)
    right3, left3 = ring_permute(right2, 1), ring_permute(left2, -1)
    return [own, across, right2, left2, right1, left1, right3, left3]


def local(perturbations, innovations, error_weight, localization):
    const = {name: jnp.asarray(value) for name, value in bases().items()}
    me = lax.axis_index("member").astype(jnp.int32)[None]
    core = (lax.axis_index("band") % 2).astype(jnp.int32)[None]
    payload = f32(BANDS, 32, 128)
    vmem = lambda *shape: pltpu.VMEM(shape, jnp.float32)
    project_scratch = [vmem(480, NLON), vmem(512, ZW)]
    own = f32(VARS, LEV, ROWS, SHARE)
    modes = f32(LEV, MW, 128)
    field = f32(RING, CHUNK, 128)

    def exchange(value):
        return lax.all_to_all(value, "band", 0, 0)

    piece = f32(CHUNK + 8, 128)
    firsts = [piece] * 3 + [f32(480, NLON), f32(8, 128), f32(8, 128)]

    def add_up(out3, out4, out5, amp, extra, side):
        out1, out7, out2, out6, out0 = call(
            rest_kernel, [piece] * 5, [], me, amp, pert, extra, scalars=1, flops=400000000,
        )
        return sum_members([out0, out1, out2, out3, out4, out5, out6, out7], side)

    sent = call(
        first_kernel, payload,
        project_scratch + [
            pltpu.VMEM(perturbations.shape, jnp.bfloat16), vmem(*innovations.shape),
            vmem(*error_weight.shape), pltpu.VMEM(const["zonal_t"].shape, jnp.bfloat16),
            pltpu.SemaphoreType.DMA((9,)),
        ],
        me, core, perturbations, innovations, error_weight, const["zonal_t"],
        scalars=2, flops=1200000000, far=4, limit=59,
    )
    sent, gradient = call(
        gradient_kernel, [payload, modes], [],
        exchange(sent), localization, const["merid_t"], const["merid"], flops=200000000,
    )
    *outs, pert = call(
        fetch_kernel, firsts + [jax.ShapeDtypeStruct(perturbations.shape, jnp.bfloat16)],
        [vmem(512, ZW), pltpu.SemaphoreType.DMA((RING,))],
        me, core, exchange(sent), const["zonal"], perturbations,
        scalars=2, flops=1200000000, far=1, limit=41,
    )
    parts = add_up(*outs)
    sent, first_field, first_own, scal = call(
        second_kernel, [payload, field, own, f32(8, 128)], project_scratch,
        me, pert, error_weight, const["zonal_t"], *parts, scalars=1, flops=1200000000,
    )
    sent, residual, step = call(
        residual_kernel, [payload, modes, f32(8, 128)], [],
        exchange(sent), localization, const["merid_t"], const["merid"], gradient, scal,
        flops=200000000,
    )
    parts = add_up(*call(
        synth_kernel, firsts, [vmem(512, ZW)],
        me, core, exchange(sent), const["zonal"], pert, scalars=2, flops=1200000000,
    ))
    sent, second_own, scal = call(
        third_kernel, [payload, own, f32(8, 128)], project_scratch + [vmem(RING, CHUNK, 128)],
        me, pert, error_weight, const["zonal_t"], scal, first_field, *parts,
        scalars=1, flops=1200000000,
    )
    return tuple(call(
        last_kernel,
        [f32(KLOC, LEV, ZW // BANDS, MW), f32(KLOC, LEV, ZW // BANDS, MW), own], [],
        exchange(sent), localization, const["merid_t"], gradient, residual, scal, step,
        first_own, second_own, flops=100000000,
    ))


def solution(mesh):
    return jax.shard_map(
        local,
        mesh=mesh,
        in_specs=(
            P("member", None, None, "band", None),
            P(None, None, "band", None),
            P(None, None, "band", None),
            P("band", None),
        ),
        out_specs=(
            P("member", None, "band", None),
            P("member", None, "band", None),
            P(None, None, "band", "member"),
        ),
        check_vma=False,
    )
```

```python
import functools
import math

import jax
import jax.numpy as jnp
import ml_dtypes
import numpy as np
from jax import lax
from jax.experimental import pallas as pl
from jax.experimental.pallas import tpu as pltpu
from jax.sharding import PartitionSpec as P

NLON = 1536
NLAT = 768
ZW = 256
MW = 128
VARS = 4
LEV = 2
KLOC = 10
BANDS = 32
RING = 8
ROWS = 24
TILES = 3
LTILES = NLON // 128
SHARE = NLON // RING
CHUNK = TILES * LTILES * 8
SLOTS = TILES * KLOC


def halves(array):
    high = array.astype(np.float32).astype(ml_dtypes.bfloat16)
    low = (array - high.astype(np.float64)).astype(np.float32).astype(ml_dtypes.bfloat16)
    return high, low


@functools.lru_cache(None)
def bases():
    wave = np.arange(ZW)
    number = (wave + 1) // 2
    angle = 2.0 * math.pi / NLON * ((number[:, None] * np.arange(NLON)[None, :]) % NLON)
    zonal = np.where((wave % 2 == 0)[:, None], np.cos(angle), np.sin(angle))
    zonal = zonal * (np.where(wave == 0, math.sqrt(0.5), 1.0) * math.sqrt(2.0 / NLON))[:, None]
    mode, row = np.arange(MW), np.arange(NLAT)
    angle = math.pi / (2.0 * NLAT) * ((mode[None, :] * (2 * row[:, None] + 1)) % (4 * NLAT))
    merid = np.cos(angle) * (np.where(mode == 0, math.sqrt(0.5), 1.0) * math.sqrt(2.0 / NLAT))
    parts = merid.reshape(BANDS, TILES, 8, MW).transpose(1, 0, 2, 3).reshape(TILES, BANDS * 8, MW)
    first = np.concatenate([parts[0], parts[1]], axis=1)
    second = np.concatenate([parts[1], parts[2]], axis=1)
    return {
        "zonal": np.stack(halves(zonal)),
        "zonal_t": np.stack(halves(zonal.T.copy())),
        "merid": np.stack([np.stack(halves(first)), np.stack(halves(second))]),
        "merid_t": np.stack([np.stack(halves(first.T.copy())), np.stack(halves(second.T.copy()))]),
    }


def split(value):
    high = value.astype(jnp.bfloat16)
    low = (value - high.astype(jnp.float32)).astype(jnp.bfloat16)
    return high, low


def dot(left, right):
    return jnp.dot(left, right, preferred_element_type=jnp.float32)


def swap_groups(vectors):
    group = lax.broadcasted_iota(jnp.int32, (8, 128), 1) // 8
    vectors = [pltpu.roll(v, 8 * i, 1) if i else v for i, v in enumerate(vectors)]
    for bit in (1, 2, 4, 8):
        move = (group & bit) != 0
        vectors = [jnp.where(move, vectors[(j + bit) % 16], vectors[j]) for j in range(16)]
    return [pltpu.roll(vectors[16 - g], 128 - 8 * g, 1) if g else vectors[0] for g in range(16)]


def total_of(value):
    return jnp.sum(jnp.sum(value, axis=1, keepdims=True), axis=0, keepdims=True)


def project_and_send(weights, pert, zonal_t, proj, coef, send, spare=None, ready=None):
    def zonal(first, rows):
        high, low = split(proj[pl.ds(first, rows), :])
        return dot(high, zonal_t[0]) + dot(low, zonal_t[0]) + dot(high, zonal_t[1])

    def keep(level, result):
        coef[pl.ds(level * 256, 240), :] = result
        coef[pl.ds(level * 256 + 240, 16), :] = jnp.zeros((16, ZW), jnp.float32)

    def project(level, members):
        for lt in range(LTILES):
            lanes = pl.ds(lt * 128, 128)
            fields = [
                jnp.concatenate([weights(v, level, rt, lt) for rt in range(TILES)], axis=0)
                for v in range(VARS)
            ]
            for k in members:
                acc = pert[k, 0, level, :, lanes].astype(jnp.float32) * fields[0]
                for v in range(1, VARS):
                    acc = acc + pert[k, v, level, :, lanes].astype(jnp.float32) * fields[v]
                for rt in range(TILES):
                    proj[pl.ds(level * 240 + (rt * KLOC + k) * 8, 8), lanes] = acc[
                        rt * 8 : rt * 8 + 8
                    ]

    def regroup(level):
        for tile in range(2):
            for half in range(2):
                got = swap_groups(
                    coef[pl.ds(level * 256 + (tile * 16 + i) * 8, 8), pl.ds(half * 128, 128)]
                    for i in range(16)
                )
                for g in range(16):
                    send[half * 16 + g, pl.ds(level * 16 + tile * 8, 8), :] = got[g]

    if ready:
        for level in range(LEV):
            ready("level", level)
            project(level, range(KLOC))
            if level == 0:
                ready("basis")
            keep(level, zonal(level * 240, 240))
            regroup(level)
        return
    for level in range(LEV):
        project(level, range(KLOC))
    result = zonal(0, 480)
    for level in range(LEV):
        keep(level, result[level * 240 : level * 240 + 240])
    coef[pl.ds(240, 8), :] = jnp.broadcast_to(spare(), (8, ZW))
    for level in range(LEV):
        regroup(level)


def first_kernel(
    unused_me, unused_core, pert_in, innovations_in, weight_in, zonal_in, send,
    proj, coef, pert, innovations, weight, zonal_t, sems,
):
    copies = {}

    def begin(name, source, target):
        copies[name] = pltpu.make_async_copy(source, target, sems.at[len(copies)])
        copies[name].start()

    def begin_level(level):
        begin(("innovations", level), innovations_in.at[:, level], innovations.at[:, level])
        begin(("weight", level), weight_in.at[:, level], weight.at[:, level])
        begin(("members", level), pert_in.at[:, :, level], pert.at[:, :, level])

    begin_level(0)
    begin(("basis",), zonal_in, zonal_t)

    def weights(v, level, rt, lt):
        at = (v, level, pl.ds(rt * 8, 8), pl.ds(lt * 128, 128))
        return weight[at] * innovations[at]

    def ready(name, *level):
        if name == "basis":
            copies["basis",].wait()
            return
        for kind in ("innovations", "weight", "members"):
            copies[(kind, *level)].wait()
        if level[0] + 1 < LEV:
            begin_level(level[0] + 1)

    project_and_send(weights, pert, zonal_t, proj, coef, send, ready=ready)


def arrived(me, parts):
    for j, part in zip((0, 4, 2, 6, 1, 7, 3, 5), parts):
        yield lax.rem(me + (RING - j), RING), part[pl.ds(0, CHUNK), :]


def assemble(me, parts, field):
    for c, value in arrived(me, parts):
        field[c] = value


def own_columns(me, field, out):
    start = (3 * me) // 2
    odd = lax.rem(me, 2) == 1
    for c in range(RING):
        for rt in range(TILES):
            at = pl.multiple_of((rt * LTILES + start) * 8, 8)
            window = jnp.concatenate(
                [field[c, pl.ds(at, 8), :], field[c, pl.ds(at + 8, 8), :]], axis=1
            )
            window = jnp.where(odd, pltpu.roll(window, 192, 1), window)
            out[c // LEV, c % LEV, pl.ds(rt * 8, 8), :] = window[:, :SHARE]


def weigh(weight, field):
    energy = [jnp.zeros((8, 128), jnp.float32)]

    def weights(v, level, rt, lt):
        value = field[v * LEV + level, pl.ds((rt * LTILES + lt) * 8, 8), :]
        weighted = weight[v, level, pl.ds(rt * 8, 8), pl.ds(lt * 128, 128)] * value
        energy[0] = energy[0] + weighted * value
        return weighted

    return weights, lambda: total_of(energy[0])


def second_kernel(me_ref, pert, weight, zonal_t, *refs):
    parts, (send, field, own, scal, proj, coef) = refs[:RING], refs[RING:]
    me = me_ref[0]
    assemble(me, parts, field)
    own_columns(me, field, own)
    scal[...] = parts[0][pl.ds(CHUNK, 8), :]
    weights, energy = weigh(weight, field)
    project_and_send(weights, pert, zonal_t, proj, coef, send, spare=energy)


def third_kernel(me_ref, pert, weight, zonal_t, old_scal, old_field, *refs):
    parts, (send, own, scal, proj, coef, field) = refs[:RING], refs[RING:]
    me = me_ref[0]
    norm = old_scal[0:1, 0:1]
    norm_next = parts[0][CHUNK : CHUNK + 1, 0:1]
    cross = parts[0][CHUNK + 1 : CHUNK + 2, 0:1]
    beta = norm_next / norm
    for c, value in arrived(me, parts):
        field[c] = value + beta * old_field[c]
    own_columns(me, field, own)
    square = norm_next + 2.0 * beta * cross + beta * beta * norm
    row = lax.broadcasted_iota(jnp.int32, (8, 128), 0)
    scal[...] = jnp.where(row == 0, norm_next, jnp.where(row == 1, square, beta))
    weights, energy = weigh(weight, field)
    project_and_send(weights, pert, zonal_t, proj, coef, send, spare=energy)


def to_modes(received, level, merid_t):
    lane = lax.broadcasted_iota(jnp.int32, (MW, 128), 1)
    sums = []
    for tile in range(2):
        data = received[:, pl.ds(level * 16 + tile * 8, 8), :].reshape(BANDS * 8, 128)
        high, low = split(data)
        sums.append(
            dot(merid_t[tile, 0], high) + dot(merid_t[tile, 0], low) + dot(merid_t[tile, 1], high)
        )
    result = sums[0][:MW] + jnp.where(lane < 48, pltpu.roll(sums[0][MW:], 48, 1), 0.0)
    result = result + jnp.where(lane >= 48, pltpu.roll(sums[1][:MW], 48, 1), 0.0)
    result = result + pltpu.roll(sums[1][MW:], 96, 1)
    return jnp.where(lane < 80, result, 0.0)


def to_rows(value, merid, level, send, spares):
    lane = lax.broadcasted_iota(jnp.int32, (MW, 128), 1)
    moved = pltpu.roll(value, 80, 1)
    second = jnp.where(lane >= 80, moved, 0.0)
    third = jnp.where(lane < 32, moved, 0.0)
    fourth = pltpu.roll(value, 32, 1)
    for tile, pair in enumerate(((value, second), (third, fourth))):
        high, low = split(jnp.concatenate(pair, axis=0))
        rows = dot(merid[tile, 0], high) + dot(merid[tile, 0], low) + dot(merid[tile, 1], high)
        if tile == 1 and spares:
            row = lax.broadcasted_iota(jnp.int32, (BANDS * 8, 128), 0)
            column = lax.broadcasted_iota(jnp.int32, (BANDS * 8, 128), 1)
            top = (row % 8) == 0
            for position, spare in enumerate(spares):
                rows = rows + jnp.where(top & (column == 112 + 8 * position), spare, 0.0)
        send[:, pl.ds(level * 16 + tile * 8, 8), :] = rows.reshape(BANDS, 8, 128)


def spare_sum(received):
    data = received[:, pl.ds(8, 8), :].reshape(BANDS * 8, 128)
    row = lax.broadcasted_iota(jnp.int32, (BANDS * 8, 128), 0)
    column = lax.broadcasted_iota(jnp.int32, (BANDS * 8, 128), 1)
    return total_of(jnp.where(((row % 8) == 0) & (column == 112), data, 0.0))


def scale_of(localization):
    return jnp.concatenate([localization[...]] * 16, axis=0).T


def gradient_kernel(received, localization, merid_t, merid, send, gradient):
    scale = scale_of(localization)
    acc = jnp.zeros((MW, 128), jnp.float32)
    for level in range(LEV):
        value = to_modes(received, level, merid_t) * scale
        gradient[level] = value
        acc = acc + value * value
    norm = total_of(acc)
    for level in range(LEV):
        to_rows(gradient[level] * scale, merid, level, send, (norm,) if level == 0 else ())


def residual_kernel(received, localization, merid_t, merid, gradient, scal, send, residual, step_out):
    scale = scale_of(localization)
    norm = scal[0:1, 0:1]
    step = norm / (norm + spare_sum(received))
    step_out[...] = jnp.broadcast_to(step, (8, 128))
    squares = jnp.zeros((MW, 128), jnp.float32)
    cross = jnp.zeros((MW, 128), jnp.float32)
    for level in range(LEV):
        old = gradient[level]
        image = old + to_modes(received, level, merid_t) * scale
        value = old - step * image
        residual[level] = value
        squares = squares + value * value
        cross = cross + value * old
    spares = (total_of(squares), total_of(cross))
    for level in range(LEV):
        to_rows(residual[level] * scale, merid, level, send, spares if level == 0 else ())


def last_kernel(
    received, localization, merid_t, gradient, residual, scal, step_in, first_own, second_own,
    control_out, residual_out, increment_out,
):
    scale = scale_of(localization)
    norm_next, square, beta = scal[0:1, 0:1], scal[1:2, 0:1], scal[2:3, 0:1]
    first_step = step_in[0:1, 0:1]
    step = norm_next / (square + spare_sum(received))
    for level in range(LEV):
        old, res = gradient[level], residual[level]
        direction = res + beta * old
        image = direction + to_modes(received, level, merid_t) * scale
        for out, value in (
            (control_out, first_step * old + step * direction),
            (residual_out, res - step * image),
        ):
            turned = value.T
            for k in range(KLOC):
                out[k, level] = turned[k * 8 : k * 8 + 8]
    increment_out[...] = first_step[None, None] * first_own[...] + step[None, None] * second_own[...]


def chunk_of(me, ahead, amp, pert, extra, out):
    c = lax.rem(me + ahead, RING)
    variable, level = c // LEV, lax.rem(c, LEV)
    for lt in range(LTILES):
        lanes = pl.ds(lt * 128, 128)
        acc = jnp.zeros((ROWS, 128), jnp.float32)
        for k in range(KLOC):
            field = jnp.concatenate(
                [
                    amp[pl.ds(pl.multiple_of(level * 240 + (rt * KLOC + k) * 8, 8), 8), lanes]
                    for rt in range(TILES)
                ],
                axis=0,
            )
            acc = acc + pert[k, variable, level, :, lanes].astype(jnp.float32) * field
        for rt in range(TILES):
            out[pl.ds((rt * LTILES + lt) * 8, 8), :] = acc[rt * 8 : rt * 8 + 8]
    out[pl.ds(CHUNK, 8), :] = extra


def tell_side(core_ref, side):
    even = core_ref[0] == 0
    side[...] = jnp.broadcast_to(jnp.where(even, 1.0, 0.0).astype(jnp.float32), (8, 128))


def synth_kernel(
    me_ref, core_ref, received, zonal, pert, out3, out4, out5, amp, extra, side, coef
):
    tell_side(core_ref, side)
    synthesize_first(me_ref[0], received, zonal, pert, out3, out4, out5, amp, extra, coef)


def fetch_kernel(
    me_ref, core_ref, received, zonal, pert_in,
    out3, out4, out5, amp, extra, side, pert, coef, sem,
):
    tell_side(core_ref, side)
    copy = pltpu.make_async_copy(pert_in, pert, sem)
    copy.start()
    synthesize_first(
        me_ref[0], received, zonal, pert, out3, out4, out5, amp, extra, coef, copy.wait
    )


def synthesize_first(
    me, received, zonal, pert, out3, out4, out5, amp, extra, coef, ready=lambda: None
):
    for level in range(LEV):
        for tile in range(2):
            for half in range(2):
                got = swap_groups(
                    received[half * 16 + g, pl.ds(level * 16 + tile * 8, 8), :] for g in range(16)
                )
                for i in range(16):
                    at = level * 256 + (tile * 16 + i) * 8
                    coef[pl.ds(at, 8), pl.ds(half * 128, 128)] = got[i]
    scalars = [total_of(coef[pl.ds(240 + 8 * i, 8), :]) for i in range(2)]
    high, low = split(jnp.concatenate([coef[pl.ds(0, 240), :], coef[pl.ds(256, 240), :]], axis=0))
    for part in range(LTILES // 2):
        wide = pl.ds(part * 256, 256)
        amp[:, wide] = (
            dot(high, zonal[0, :, wide]) + dot(low, zonal[0, :, wide]) + dot(high, zonal[1, :, wide])
        )
    row = lax.broadcasted_iota(jnp.int32, (8, 128), 0)
    extra[...] = jnp.where(row == 0, scalars[0], jnp.where(row == 1, scalars[1], 0.0))
    ready()
    for ahead, out in ((4, out4), (3, out3), (5, out5)):
        chunk_of(me, ahead, amp, pert, extra[...], out)


def rest_kernel(me_ref, amp, pert, extra, out1, out7, out2, out6, out0):
    for ahead, out in ((1, out1), (7, out7), (2, out2), (6, out6), (0, out0)):
        chunk_of(me_ref[0], ahead, amp, pert, extra[...], out)


def f32(*shape):
    return jax.ShapeDtypeStruct(shape, jnp.float32)


def call(kernel, outs, scratch, *args, scalars=0, flops=0, far=0, limit=16):
    in_specs = [pl.BlockSpec(memory_space=pltpu.SMEM)] * scalars
    in_specs += [pl.BlockSpec(memory_space=pltpu.VMEM)] * (len(args) - scalars - far)
    in_specs += [pl.BlockSpec(memory_space=pl.ANY)] * far
    moved = sum(math.prod(a.shape) * a.dtype.itemsize for a in args)
    return pl.pallas_call(
        kernel,
        out_shape=outs,
        in_specs=in_specs,
        out_specs=jax.tree.map(lambda _: pl.BlockSpec(memory_space=pltpu.VMEM), outs),
        scratch_shapes=scratch,
        compiler_params=pltpu.CompilerParams(vmem_limit_bytes=limit * 1024 * 1024),
        cost_estimate=pl.CostEstimate(flops=flops, bytes_accessed=moved, transcendentals=0),
    )(*args)


def ring_permute(value, distance):
    return lax.ppermute(value, "member", [(i, (i + distance) % RING) for i in range(RING)])


def cross_permute(value, distance):
    pairs = [
        (m * BANDS + b, (m + (distance if b % 2 == 0 else RING - distance)) % RING * BANDS + b)
        for m in range(RING)
        for b in range(BANDS)
    ]
    return lax.ppermute(value, ("member", "band"), pairs)


def sum_members(outs, side):
    rightwards = side[:1] > 0.0
    right3, left3 = ring_permute(outs[3], 1), ring_permute(outs[5], -1)
    leg = cross_permute(outs[4], 2)
    right3, near, behind = lax.optimization_barrier((right3, outs[1], outs[7]))
    right1, left1 = ring_permute(near, 1), ring_permute(behind, -1)
    right, left = lax.optimization_barrier((
        outs[2] + right3 + jnp.where(rightwards, leg, 0.0),
        outs[6] + left3 + jnp.where(rightwards, 0.0, leg),
    ))
    own = outs[0] + right1 + left1 + ring_permute(right, 2) + ring_permute(left, -2)
    mine = own[:CHUNK]
    right2, left2 = ring_permute(mine, 2), ring_permute(mine, -2)
    right1, left1 = ring_permute(mine, 1), ring_permute(mine, -1)
    right2, left2 = lax.optimization_barrier((right2, left2))
    across = cross_permute(jnp.where(rightwards, right2, left2), 2)
    right3, left3 = ring_permute(right2, 1), ring_permute(left2, -1)
    return [own, across, right2, left2, right1, left1, right3, left3]


def local(perturbations, innovations, error_weight, localization):
    const = {name: jnp.asarray(value) for name, value in bases().items()}
    me = lax.axis_index("member").astype(jnp.int32)[None]
    core = (lax.axis_index("band") % 2).astype(jnp.int32)[None]
    payload = f32(BANDS, 32, 128)
    vmem = lambda *shape: pltpu.VMEM(shape, jnp.float32)
    project_scratch = [vmem(480, NLON), vmem(512, ZW)]
    own = f32(VARS, LEV, ROWS, SHARE)
    modes = f32(LEV, MW, 128)
    field = f32(RING, CHUNK, 128)

    def exchange(value):
        return lax.all_to_all(value, "band", 0, 0)

    piece = f32(CHUNK + 8, 128)
    firsts = [piece] * 3 + [f32(480, NLON), f32(8, 128), f32(8, 128)]

    def add_up(out3, out4, out5, amp, extra, side):
        out1, out7, out2, out6, out0 = call(
            rest_kernel, [piece] * 5, [], me, amp, pert, extra, scalars=1, flops=400000000,
        )
        return sum_members([out0, out1, out2, out3, out4, out5, out6, out7], side)

    sent = call(
        first_kernel, payload,
        project_scratch + [
            pltpu.VMEM(perturbations.shape, jnp.bfloat16), vmem(*innovations.shape),
            vmem(*error_weight.shape), pltpu.VMEM(const["zonal_t"].shape, jnp.bfloat16),
            pltpu.SemaphoreType.DMA((7,)),
        ],
        me, core, perturbations, innovations, error_weight, const["zonal_t"],
        scalars=2, flops=1200000000, far=4, limit=59,
    )
    sent, gradient = call(
        gradient_kernel, [payload, modes], [],
        exchange(sent), localization, const["merid_t"], const["merid"], flops=200000000,
    )
    *outs, pert = call(
        fetch_kernel, firsts + [jax.ShapeDtypeStruct(perturbations.shape, jnp.bfloat16)],
        [vmem(512, ZW), pltpu.SemaphoreType.DMA(())],
        me, core, exchange(sent), const["zonal"], perturbations,
        scalars=2, flops=1200000000, far=1, limit=41,
    )
    parts = add_up(*outs)
    sent, first_field, first_own, scal = call(
        second_kernel, [payload, field, own, f32(8, 128)], project_scratch,
        me, pert, error_weight, const["zonal_t"], *parts, scalars=1, flops=1200000000,
    )
    sent, residual, step = call(
        residual_kernel, [payload, modes, f32(8, 128)], [],
        exchange(sent), localization, const["merid_t"], const["merid"], gradient, scal,
        flops=200000000,
    )
    parts = add_up(*call(
        synth_kernel, firsts, [vmem(512, ZW)],
        me, core, exchange(sent), const["zonal"], pert, scalars=2, flops=1200000000,
    ))
    sent, second_own, scal = call(
        third_kernel, [payload, own, f32(8, 128)], project_scratch + [vmem(RING, CHUNK, 128)],
        me, pert, error_weight, const["zonal_t"], scal, first_field, *parts,
        scalars=1, flops=1200000000,
    )
    return tuple(call(
        last_kernel,
        [f32(KLOC, LEV, ZW // BANDS, MW), f32(KLOC, LEV, ZW // BANDS, MW), own], [],
        exchange(sent), localization, const["merid_t"], gradient, residual, scal, step,
        first_own, second_own, flops=100000000,
    ))


def solution(mesh):
    return jax.shard_map(
        local,
        mesh=mesh,
        in_specs=(
            P("member", None, None, "band", None),
            P(None, None, "band", None),
            P(None, None, "band", None),
            P("band", None),
        ),
        out_specs=(
            P("member", None, "band", None),
            P("member", None, "band", None),
            P(None, None, "band", "member"),
        ),
        check_vma=False,
    )
```

```python
import functools
import math

import jax
import jax.numpy as jnp
import ml_dtypes
import numpy as np
from jax import lax
from jax.experimental import pallas as pl
from jax.experimental.pallas import tpu as pltpu
from jax.sharding import PartitionSpec as P

NLON = 1536
NLAT = 768
ZW = 256
MW = 128
VARS = 4
LEV = 2
KLOC = 10
BANDS = 32
RING = 8
ROWS = 24
TILES = 3
LTILES = NLON // 128
SHARE = NLON // RING
CHUNK = TILES * LTILES * 8
SLOTS = TILES * KLOC


def halves(array):
    high = array.astype(np.float32).astype(ml_dtypes.bfloat16)
    low = (array - high.astype(np.float64)).astype(np.float32).astype(ml_dtypes.bfloat16)
    return high, low


@functools.lru_cache(None)
def bases():
    wave = np.arange(ZW)
    number = (wave + 1) // 2
    angle = 2.0 * math.pi / NLON * ((number[:, None] * np.arange(NLON)[None, :]) % NLON)
    zonal = np.where((wave % 2 == 0)[:, None], np.cos(angle), np.sin(angle))
    zonal = zonal * (np.where(wave == 0, math.sqrt(0.5), 1.0) * math.sqrt(2.0 / NLON))[:, None]
    mode, row = np.arange(MW), np.arange(NLAT)
    angle = math.pi / (2.0 * NLAT) * ((mode[None, :] * (2 * row[:, None] + 1)) % (4 * NLAT))
    merid = np.cos(angle) * (np.where(mode == 0, math.sqrt(0.5), 1.0) * math.sqrt(2.0 / NLAT))
    parts = merid.reshape(BANDS, TILES, 8, MW).transpose(1, 0, 2, 3).reshape(TILES, BANDS * 8, MW)
    first = np.concatenate([parts[0], parts[1]], axis=1)
    second = np.concatenate([parts[1], parts[2]], axis=1)
    return {
        "zonal": np.stack(halves(zonal)),
        "zonal_t": np.stack(halves(zonal.T.copy())),
        "merid": np.stack([np.stack(halves(first)), np.stack(halves(second))]),
        "merid_t": np.stack([np.stack(halves(first.T.copy())), np.stack(halves(second.T.copy()))]),
    }


def split(value):
    high = value.astype(jnp.bfloat16)
    low = (value - high.astype(jnp.float32)).astype(jnp.bfloat16)
    return high, low


def dot(left, right):
    return jnp.dot(left, right, preferred_element_type=jnp.float32)


def swap_groups(vectors):
    group = lax.broadcasted_iota(jnp.int32, (8, 128), 1) // 8
    vectors = [pltpu.roll(v, 8 * i, 1) if i else v for i, v in enumerate(vectors)]
    for bit in (1, 2, 4, 8):
        move = (group & bit) != 0
        vectors = [jnp.where(move, vectors[(j + bit) % 16], vectors[j]) for j in range(16)]
    return [pltpu.roll(vectors[16 - g], 128 - 8 * g, 1) if g else vectors[0] for g in range(16)]


def total_of(value):
    return jnp.sum(jnp.sum(value, axis=1, keepdims=True), axis=0, keepdims=True)


def project_and_send(weights, pert, zonal_t, proj, coef, send, spare=None, ready=None):
    def zonal(first, rows):
        high, low = split(proj[pl.ds(first, rows), :])
        return dot(high, zonal_t[0]) + dot(low, zonal_t[0]) + dot(high, zonal_t[1])

    def keep(level, result):
        coef[pl.ds(level * 256, 240), :] = result
        coef[pl.ds(level * 256 + 240, 16), :] = jnp.zeros((16, ZW), jnp.float32)

    def project(level, members):
        for lt in range(LTILES):
            lanes = pl.ds(lt * 128, 128)
            fields = [
                jnp.concatenate([weights(v, level, rt, lt) for rt in range(TILES)], axis=0)
                for v in range(VARS)
            ]
            for k in members:
                acc = pert[k, 0, level, :, lanes].astype(jnp.float32) * fields[0]
                for v in range(1, VARS):
                    acc = acc + pert[k, v, level, :, lanes].astype(jnp.float32) * fields[v]
                for rt in range(TILES):
                    proj[pl.ds(level * 240 + (rt * KLOC + k) * 8, 8), lanes] = acc[
                        rt * 8 : rt * 8 + 8
                    ]

    def regroup(level):
        for tile in range(2):
            for half in range(2):
                got = swap_groups(
                    coef[pl.ds(level * 256 + (tile * 16 + i) * 8, 8), pl.ds(half * 128, 128)]
                    for i in range(16)
                )
                for g in range(16):
                    send[half * 16 + g, pl.ds(level * 16 + tile * 8, 8), :] = got[g]

    if ready:
        for level in range(LEV):
            ready("level", level)
            project(level, range(KLOC))
            if level == 0:
                ready("basis")
            keep(level, zonal(level * 240, 240))
            regroup(level)
        return
    for level in range(LEV):
        project(level, range(KLOC))
    result = zonal(0, 480)
    for level in range(LEV):
        keep(level, result[level * 240 : level * 240 + 240])
    coef[pl.ds(240, 8), :] = jnp.broadcast_to(spare(), (8, ZW))
    for level in range(LEV):
        regroup(level)


def first_kernel(
    unused_me, unused_core, pert_in, innovations_in, weight_in, zonal_in, send,
    proj, coef, pert, innovations, weight, zonal_t, sems,
):
    copies = {}

    def begin(name, source, target):
        copies[name] = pltpu.make_async_copy(source, target, sems.at[len(copies)])
        copies[name].start()

    def begin_level(level):
        begin(("innovations", level), innovations_in.at[:, level], innovations.at[:, level])
        begin(("weight", level), weight_in.at[:, level], weight.at[:, level])
        begin(("members", level), pert_in.at[:, :, level], pert.at[:, :, level])

    begin_level(0)
    begin(("basis",), zonal_in, zonal_t)
    begin_level(1)

    def weights(v, level, rt, lt):
        at = (v, level, pl.ds(rt * 8, 8), pl.ds(lt * 128, 128))
        return weight[at] * innovations[at]

    def ready(name, *level):
        if name == "basis":
            copies["basis",].wait()
            return
        for kind in ("innovations", "weight", "members"):
            copies[(kind, *level)].wait()

    project_and_send(weights, pert, zonal_t, proj, coef, send, ready=ready)


def arrived(me, parts):
    for j, part in zip((0, 4, 2, 6, 1, 7, 3, 5), parts):
        yield lax.rem(me + (RING - j), RING), part[pl.ds(0, CHUNK), :]


def assemble(me, parts, field):
    for c, value in arrived(me, parts):
        field[c] = value


def own_columns(me, field, out):
    start = (3 * me) // 2
    odd = lax.rem(me, 2) == 1
    for c in range(RING):
        for rt in range(TILES):
            at = pl.multiple_of((rt * LTILES + start) * 8, 8)
            window = jnp.concatenate(
                [field[c, pl.ds(at, 8), :], field[c, pl.ds(at + 8, 8), :]], axis=1
            )
            window = jnp.where(odd, pltpu.roll(window, 192, 1), window)
            out[c // LEV, c % LEV, pl.ds(rt * 8, 8), :] = window[:, :SHARE]


def weigh(weight, field):
    energy = [jnp.zeros((8, 128), jnp.float32)]

    def weights(v, level, rt, lt):
        value = field[v * LEV + level, pl.ds((rt * LTILES + lt) * 8, 8), :]
        weighted = weight[v, level, pl.ds(rt * 8, 8), pl.ds(lt * 128, 128)] * value
        energy[0] = energy[0] + weighted * value
        return weighted

    return weights, lambda: total_of(energy[0])


def second_kernel(me_ref, pert, weight, zonal_t, *refs):
    parts, (send, field, own, scal, proj, coef) = refs[:RING], refs[RING:]
    me = me_ref[0]
    assemble(me, parts, field)
    own_columns(me, field, own)
    scal[...] = parts[0][pl.ds(CHUNK, 8), :]
    weights, energy = weigh(weight, field)
    project_and_send(weights, pert, zonal_t, proj, coef, send, spare=energy)


def third_kernel(me_ref, pert, weight, zonal_t, old_scal, old_field, *refs):
    parts, (send, own, scal, proj, coef, field) = refs[:RING], refs[RING:]
    me = me_ref[0]
    norm = old_scal[0:1, 0:1]
    norm_next = parts[0][CHUNK : CHUNK + 1, 0:1]
    cross = parts[0][CHUNK + 1 : CHUNK + 2, 0:1]
    beta = norm_next / norm
    for c, value in arrived(me, parts):
        field[c] = value + beta * old_field[c]
    own_columns(me, field, own)
    square = norm_next + 2.0 * beta * cross + beta * beta * norm
    row = lax.broadcasted_iota(jnp.int32, (8, 128), 0)
    scal[...] = jnp.where(row == 0, norm_next, jnp.where(row == 1, square, beta))
    weights, energy = weigh(weight, field)
    project_and_send(weights, pert, zonal_t, proj, coef, send, spare=energy)


def to_modes(received, level, merid_t):
    lane = lax.broadcasted_iota(jnp.int32, (MW, 128), 1)
    sums = []
    for tile in range(2):
        data = received[:, pl.ds(level * 16 + tile * 8, 8), :].reshape(BANDS * 8, 128)
        high, low = split(data)
        sums.append(
            dot(merid_t[tile, 0], high) + dot(merid_t[tile, 0], low) + dot(merid_t[tile, 1], high)
        )
    result = sums[0][:MW] + jnp.where(lane < 48, pltpu.roll(sums[0][MW:], 48, 1), 0.0)
    result = result + jnp.where(lane >= 48, pltpu.roll(sums[1][:MW], 48, 1), 0.0)
    result = result + pltpu.roll(sums[1][MW:], 96, 1)
    return jnp.where(lane < 80, result, 0.0)


def to_rows(value, merid, level, send, spares):
    lane = lax.broadcasted_iota(jnp.int32, (MW, 128), 1)
    moved = pltpu.roll(value, 80, 1)
    second = jnp.where(lane >= 80, moved, 0.0)
    third = jnp.where(lane < 32, moved, 0.0)
    fourth = pltpu.roll(value, 32, 1)
    for tile, pair in enumerate(((value, second), (third, fourth))):
        high, low = split(jnp.concatenate(pair, axis=0))
        rows = dot(merid[tile, 0], high) + dot(merid[tile, 0], low) + dot(merid[tile, 1], high)
        if tile == 1 and spares:
            row = lax.broadcasted_iota(jnp.int32, (BANDS * 8, 128), 0)
            column = lax.broadcasted_iota(jnp.int32, (BANDS * 8, 128), 1)
            top = (row % 8) == 0
            for position, spare in enumerate(spares):
                rows = rows + jnp.where(top & (column == 112 + 8 * position), spare, 0.0)
        send[:, pl.ds(level * 16 + tile * 8, 8), :] = rows.reshape(BANDS, 8, 128)


def spare_sum(received):
    data = received[:, pl.ds(8, 8), :].reshape(BANDS * 8, 128)
    row = lax.broadcasted_iota(jnp.int32, (BANDS * 8, 128), 0)
    column = lax.broadcasted_iota(jnp.int32, (BANDS * 8, 128), 1)
    return total_of(jnp.where(((row % 8) == 0) & (column == 112), data, 0.0))


def scale_of(localization):
    return jnp.concatenate([localization[...]] * 16, axis=0).T


def gradient_kernel(received, localization, merid_t, merid, send, gradient):
    scale = scale_of(localization)
    acc = jnp.zeros((MW, 128), jnp.float32)
    for level in range(LEV):
        value = to_modes(received, level, merid_t) * scale
        gradient[level] = value
        acc = acc + value * value
    norm = total_of(acc)
    for level in range(LEV):
        to_rows(gradient[level] * scale, merid, level, send, (norm,) if level == 0 else ())


def residual_kernel(received, localization, merid_t, merid, gradient, scal, send, residual, step_out):
    scale = scale_of(localization)
    norm = scal[0:1, 0:1]
    step = norm / (norm + spare_sum(received))
    step_out[...] = jnp.broadcast_to(step, (8, 128))
    squares = jnp.zeros((MW, 128), jnp.float32)
    cross = jnp.zeros((MW, 128), jnp.float32)
    for level in range(LEV):
        old = gradient[level]
        image = old + to_modes(received, level, merid_t) * scale
        value = old - step * image
        residual[level] = value
        squares = squares + value * value
        cross = cross + value * old
    spares = (total_of(squares), total_of(cross))
    for level in range(LEV):
        to_rows(residual[level] * scale, merid, level, send, spares if level == 0 else ())


def last_kernel(
    received, localization, merid_t, gradient, residual, scal, step_in, first_own, second_own,
    control_out, residual_out, increment_out,
):
    scale = scale_of(localization)
    norm_next, square, beta = scal[0:1, 0:1], scal[1:2, 0:1], scal[2:3, 0:1]
    first_step = step_in[0:1, 0:1]
    step = norm_next / (square + spare_sum(received))
    for level in range(LEV):
        old, res = gradient[level], residual[level]
        direction = res + beta * old
        image = direction + to_modes(received, level, merid_t) * scale
        for out, value in (
            (control_out, first_step * old + step * direction),
            (residual_out, res - step * image),
        ):
            turned = value.T
            for k in range(KLOC):
                out[k, level] = turned[k * 8 : k * 8 + 8]
    increment_out[...] = first_step[None, None] * first_own[...] + step[None, None] * second_own[...]


def chunk_of(me, ahead, amp, pert, extra, out):
    c = lax.rem(me + ahead, RING)
    variable, level = c // LEV, lax.rem(c, LEV)
    for lt in range(LTILES):
        lanes = pl.ds(lt * 128, 128)
        acc = jnp.zeros((ROWS, 128), jnp.float32)
        for k in range(KLOC):
            field = jnp.concatenate(
                [
                    amp[pl.ds(pl.multiple_of(level * 240 + (rt * KLOC + k) * 8, 8), 8), lanes]
                    for rt in range(TILES)
                ],
                axis=0,
            )
            acc = acc + pert[k, variable, level, :, lanes].astype(jnp.float32) * field
        for rt in range(TILES):
            out[pl.ds((rt * LTILES + lt) * 8, 8), :] = acc[rt * 8 : rt * 8 + 8]
    out[pl.ds(CHUNK, 8), :] = extra


def tell_side(core_ref, side):
    even = core_ref[0] == 0
    side[...] = jnp.broadcast_to(jnp.where(even, 1.0, 0.0).astype(jnp.float32), (8, 128))


def synth_kernel(
    me_ref, core_ref, received, zonal, pert, out3, out4, out5, amp, extra, side, coef
):
    tell_side(core_ref, side)
    synthesize_first(me_ref[0], received, zonal, pert, out3, out4, out5, amp, extra, coef)


def fetch_kernel(
    me_ref, core_ref, received, zonal, pert_in,
    out3, out4, out5, amp, extra, side, pert, coef, sem,
):
    tell_side(core_ref, side)
    copy = pltpu.make_async_copy(pert_in, pert, sem)
    copy.start()
    synthesize_first(
        me_ref[0], received, zonal, pert, out3, out4, out5, amp, extra, coef, copy.wait
    )


def synthesize_first(
    me, received, zonal, pert, out3, out4, out5, amp, extra, coef, ready=lambda: None
):
    for level in range(LEV):
        for tile in range(2):
            for half in range(2):
                got = swap_groups(
                    received[half * 16 + g, pl.ds(level * 16 + tile * 8, 8), :] for g in range(16)
                )
                for i in range(16):
                    at = level * 256 + (tile * 16 + i) * 8
                    coef[pl.ds(at, 8), pl.ds(half * 128, 128)] = got[i]
    scalars = [total_of(coef[pl.ds(240 + 8 * i, 8), :]) for i in range(2)]
    high, low = split(jnp.concatenate([coef[pl.ds(0, 240), :], coef[pl.ds(256, 240), :]], axis=0))
    for part in range(LTILES // 2):
        wide = pl.ds(part * 256, 256)
        amp[:, wide] = (
            dot(high, zonal[0, :, wide]) + dot(low, zonal[0, :, wide]) + dot(high, zonal[1, :, wide])
        )
    row = lax.broadcasted_iota(jnp.int32, (8, 128), 0)
    extra[...] = jnp.where(row == 0, scalars[0], jnp.where(row == 1, scalars[1], 0.0))
    ready()
    for ahead, out in ((4, out4), (3, out3), (5, out5)):
        chunk_of(me, ahead, amp, pert, extra[...], out)


def rest_kernel(me_ref, amp, pert, extra, out1, out7, out2, out6, out0):
    for ahead, out in ((1, out1), (7, out7), (2, out2), (6, out6), (0, out0)):
        chunk_of(me_ref[0], ahead, amp, pert, extra[...], out)


def f32(*shape):
    return jax.ShapeDtypeStruct(shape, jnp.float32)


def call(kernel, outs, scratch, *args, scalars=0, flops=0, far=0, limit=16):
    in_specs = [pl.BlockSpec(memory_space=pltpu.SMEM)] * scalars
    in_specs += [pl.BlockSpec(memory_space=pltpu.VMEM)] * (len(args) - scalars - far)
    in_specs += [pl.BlockSpec(memory_space=pl.ANY)] * far
    moved = sum(math.prod(a.shape) * a.dtype.itemsize for a in args)
    return pl.pallas_call(
        kernel,
        out_shape=outs,
        in_specs=in_specs,
        out_specs=jax.tree.map(lambda _: pl.BlockSpec(memory_space=pltpu.VMEM), outs),
        scratch_shapes=scratch,
        compiler_params=pltpu.CompilerParams(vmem_limit_bytes=limit * 1024 * 1024),
        cost_estimate=pl.CostEstimate(flops=flops, bytes_accessed=moved, transcendentals=0),
    )(*args)


def ring_permute(value, distance):
    return lax.ppermute(value, "member", [(i, (i + distance) % RING) for i in range(RING)])


def cross_permute(value, distance):
    pairs = [
        (m * BANDS + b, (m + (distance if b % 2 == 0 else RING - distance)) % RING * BANDS + b)
        for m in range(RING)
        for b in range(BANDS)
    ]
    return lax.ppermute(value, ("member", "band"), pairs)


def sum_members(outs, side):
    rightwards = side[:1] > 0.0
    right3, left3 = ring_permute(outs[3], 1), ring_permute(outs[5], -1)
    leg = cross_permute(outs[4], 2)
    right3, near, behind = lax.optimization_barrier((right3, outs[1], outs[7]))
    right1, left1 = ring_permute(near, 1), ring_permute(behind, -1)
    right, left = lax.optimization_barrier((
        outs[2] + right3 + jnp.where(rightwards, leg, 0.0),
        outs[6] + left3 + jnp.where(rightwards, 0.0, leg),
    ))
    own = outs[0] + right1 + left1 + ring_permute(right, 2) + ring_permute(left, -2)
    mine = own[:CHUNK]
    right2, left2 = ring_permute(mine, 2), ring_permute(mine, -2)
    right1, left1 = ring_permute(mine, 1), ring_permute(mine, -1)
    right2, left2 = lax.optimization_barrier((right2, left2))
    across = cross_permute(jnp.where(rightwards, right2, left2), 2)
    right3, left3 = ring_permute(right2, 1), ring_permute(left2, -1)
    return [own, across, right2, left2, right1, left1, right3, left3]


def local(perturbations, innovations, error_weight, localization):
    const = {name: jnp.asarray(value) for name, value in bases().items()}
    me = lax.axis_index("member").astype(jnp.int32)[None]
    core = (lax.axis_index("band") % 2).astype(jnp.int32)[None]
    payload = f32(BANDS, 32, 128)
    vmem = lambda *shape: pltpu.VMEM(shape, jnp.float32)
    project_scratch = [vmem(480, NLON), vmem(512, ZW)]
    own = f32(VARS, LEV, ROWS, SHARE)
    modes = f32(LEV, MW, 128)
    field = f32(RING, CHUNK, 128)

    def exchange(value):
        return lax.all_to_all(value, "band", 0, 0)

    piece = f32(CHUNK + 8, 128)
    firsts = [piece] * 3 + [f32(480, NLON), f32(8, 128), f32(8, 128)]

    def add_up(out3, out4, out5, amp, extra, side):
        out1, out7, out2, out6, out0 = call(
            rest_kernel, [piece] * 5, [], me, amp, pert, extra, scalars=1, flops=400000000,
        )
        return sum_members([out0, out1, out2, out3, out4, out5, out6, out7], side)

    sent = call(
        first_kernel, payload,
        project_scratch + [
            pltpu.VMEM(perturbations.shape, jnp.bfloat16), vmem(*innovations.shape),
            vmem(*error_weight.shape), pltpu.VMEM(const["zonal_t"].shape, jnp.bfloat16),
            pltpu.SemaphoreType.DMA((7,)),
        ],
        me, core, perturbations, innovations, error_weight, const["zonal_t"],
        scalars=2, flops=1200000000, far=4, limit=59,
    )
    sent, gradient = call(
        gradient_kernel, [payload, modes], [],
        exchange(sent), localization, const["merid_t"], const["merid"], flops=200000000,
    )
    *outs, pert = call(
        fetch_kernel, firsts + [jax.ShapeDtypeStruct(perturbations.shape, jnp.bfloat16)],
        [vmem(512, ZW), pltpu.SemaphoreType.DMA(())],
        me, core, exchange(sent), const["zonal"], perturbations,
        scalars=2, flops=1200000000, far=1, limit=41,
    )
    parts = add_up(*outs)
    sent, first_field, first_own, scal = call(
        second_kernel, [payload, field, own, f32(8, 128)], project_scratch,
        me, pert, error_weight, const["zonal_t"], *parts, scalars=1, flops=1200000000,
    )
    sent, residual, step = call(
        residual_kernel, [payload, modes, f32(8, 128)], [],
        exchange(sent), localization, const["merid_t"], const["merid"], gradient, scal,
        flops=200000000,
    )
    parts = add_up(*call(
        synth_kernel, firsts, [vmem(512, ZW)],
        me, core, exchange(sent), const["zonal"], pert, scalars=2, flops=1200000000,
    ))
    sent, second_own, scal = call(
        third_kernel, [payload, own, f32(8, 128)], project_scratch + [vmem(RING, CHUNK, 128)],
        me, pert, error_weight, const["zonal_t"], scal, first_field, *parts,
        scalars=1, flops=1200000000,
    )
    return tuple(call(
        last_kernel,
        [f32(KLOC, LEV, ZW // BANDS, MW), f32(KLOC, LEV, ZW // BANDS, MW), own], [],
        exchange(sent), localization, const["merid_t"], gradient, residual, scal, step,
        first_own, second_own, flops=100000000,
    ))


def solution(mesh):
    return jax.shard_map(
        local,
        mesh=mesh,
        in_specs=(
            P("member", None, None, "band", None),
            P(None, None, "band", None),
            P(None, None, "band", None),
            P("band", None),
        ),
        out_specs=(
            P("member", None, "band", None),
            P("member", None, "band", None),
            P(None, None, "band", "member"),
        ),
        check_vma=False,
    )
```
